512 devices in a mesh: tm: 16 (over z_hi, y), height: 32 (over z_lo, x, core).
Axes of the slice: x: 4, y: 8, z: 8 (z_hi: 2, z_lo: 4; z = z_hi * 4 + z_lo), core: 2. Of those that a mesh axis runs over, the one named last changes fastest.
Arguments:
- features: bfloat16 [32, 64, 16, 192], P('tm', 'height'), may hold values from -6 to 6
- cotangent: bfloat16 [32, 128, 32, 96], P('tm', 'height'), may hold values from -6 to 6
- weight_one: bfloat16 [3, 3, 3, 192, 96], replicated, may hold values from -0.078125 to 0.078125
- weight_two: bfloat16 [3, 3, 3, 96, 96], replicated, may hold values from -0.125 to 0.125
- norm_gain: float32 [96], replicated, may hold values from 0.5 to 1.5
- norm_shift: float32 [96], replicated, may hold values from -3 to 3
Outputs:
- decoded: bfloat16 [32, 128, 32, 96], P('tm', 'height')
- grad_features: float32 [32, 64, 16, 192], P('tm', 'height')
- grad_one: float32 [3, 3, 3, 192, 96], replicated
- grad_two: float32 [3, 3, 3, 96, 96], replicated
The draws below stay inside these ranges and needn't reach their ends.
All inputs are finite; a program needn't handle non-finite values.
Results may differ from the reference program's by a relative error of at most 0.0055.
Values may be sent and summed in bfloat16 or wider, within the bound.
No kernel may reach another device: no remote copies, remote signals or barrier semaphores. Data moves between devices by JAX's collectives and lax.ppermute only.
A program may use at most 64 MiB of HBM per device.

```python
import jax
import jax.numpy as jnp
from jax import lax

C_IN = 192
C_MID = 96
GROUPS = 32
COLS_IN = 16
FRAMES = 32
ROWS_IN = 64
ROWS_OUT = 128
COLS_OUT = 32


def shard_levels(own_key, extent, shards, low, largest):
    loudness, own = 1.0, jax.random.fold_in(own_key, 6)
    for dim, parts in shards:
        draws = jnp.exp(jax.random.uniform(jax.random.fold_in(own, dim), (parts,), jnp.float32, low / len(shards), largest / len(shards)))
        loudness = loudness * jnp.repeat(draws, extent[dim] // parts).reshape([-1 if axis == dim else 1 for axis in range(len(extent))])
    return loudness


def centred(rng, shape, spread, most, shards=(), held_as=jnp.bfloat16):
    drawn = spread * jax.random.normal(rng, shape, jnp.float32)
    if shards:
        drawn = drawn * shard_levels(rng, shape, shards, -0.22, 0.18)
    return jnp.clip(drawn, -most, most).astype(held_as)


def setup_inputs(seed: int = 0) -> dict:
    key_of = jax.random.split(jax.random.key(seed), 7)
    features = centred(key_of[0], (FRAMES, ROWS_IN, COLS_IN, C_IN), 1.0, 6.0, ((0, 16), (1, 32)))
    cotangent = centred(key_of[1], (FRAMES, ROWS_OUT, COLS_OUT, C_MID), 1.0, 6.0, ((0, 16), (1, 32)))
    weight_one = centred(key_of[2], (3, 3, 3, C_IN, C_MID), (27 * C_IN) ** -0.5, 0.078125)
    weight_two = centred(key_of[3], (3, 3, 3, C_MID, C_MID), (27 * C_MID) ** -0.5, 0.125)
    norm_gain = jnp.clip(1.0 + 0.1 * jax.random.normal(key_of[4], (C_MID,), jnp.float32), 0.5, 1.5)
    norm_shift = centred(key_of[5], (C_MID,), 0.5, 3.0, (), jnp.float32)
    return {"features": features, "cotangent": cotangent, "weight_one": weight_one, "weight_two": weight_two, "norm_gain": norm_gain, "norm_shift": norm_shift}


EPSILON = 1e-05

def convolve(padded, weight):
    result = lax.conv_general_dilated(padded[None], weight, (1, 1, 1), 'VALID', dimension_numbers=('NDHWC', 'DHWIO', 'NDHWC'), preferred_element_type=jnp.float32)
    return result[0]

def flipped(weight):
    return jnp.transpose(jnp.flip(weight, (0, 1, 2)), (0, 1, 2, 4, 3))

def taps(padded, grad):
    frames, rows, cols, outs = grad.shape
    flat_grad = grad.reshape(-1, outs)
    pieces = []
    for time_tap in range(3):
        for row_tap in range(3):
            for col_tap in range(3):
                patch = padded[time_tap:time_tap + frames, row_tap:row_tap + rows, col_tap:col_tap + cols]
                patch = patch.reshape(-1, padded.shape[-1])
                pieces.append(lax.dot_general(patch, flat_grad, (((0,), (0,)), ((), ())), preferred_element_type=jnp.float32))
    return jnp.stack(pieces).reshape(3, 3, 3, padded.shape[-1], outs)

def upsample(field):
    return jnp.repeat(jnp.repeat(field, 2, 1), 2, 2)

def reference(features, cotangent, weight_one, weight_two, norm_gain, norm_shift):
    upsampled = upsample(features)
    padded_in = jnp.pad(upsampled, ((2, 0), (1, 1), (1, 1), (0, 0)))
    pre_norm = convolve(padded_in, weight_one)
    shape = pre_norm.shape
    grouped = pre_norm.reshape(shape[0], shape[1], shape[2], GROUPS, -1)
    count = FRAMES * ROWS_OUT * COLS_OUT * (C_MID // GROUPS)
    total_one = lax.optimization_barrier(jnp.sum(grouped, (0, 1, 2, 4)))
    total_two = lax.optimization_barrier(jnp.sum(grouped * grouped, (0, 1, 2, 4)))
    mean = total_one / count
    rstd = lax.rsqrt(total_two / count - mean * mean + EPSILON)
    normed = ((grouped - mean[:, None]) * rstd[:, None]).reshape(shape)
    shifted = normed * norm_gain + norm_shift
    hidden = jax.nn.silu(shifted).astype(jnp.bfloat16)
    padded_mid = jnp.pad(hidden, ((2, 0), (1, 1), (1, 1), (0, 0)))
    decoded = convolve(padded_mid, weight_two).astype(jnp.bfloat16)
    scale = 1.0 / (FRAMES * ROWS_OUT * COLS_OUT) ** 0.5
    grad_two = taps(padded_mid, cotangent) * scale
    cot_pad = jnp.pad(cotangent, ((0, 2), (1, 1), (1, 1), (0, 0)))
    grad_hidden = convolve(cot_pad, flipped(weight_two))
    sigma = jax.nn.sigmoid(shifted)
    grad_normed = grad_hidden * sigma * (1.0 + shifted * (1.0 - sigma)) * norm_gain
    grad_grouped = grad_normed.reshape(grouped.shape)
    normed_grouped = normed.reshape(grouped.shape)
    first = lax.optimization_barrier(jnp.sum(grad_grouped, (0, 1, 2, 4))) / count
    second = lax.optimization_barrier(jnp.sum(grad_grouped * normed_grouped, (0, 1, 2, 4))) / count
    grad_pre = ((grad_grouped - first[:, None] - normed_grouped * second[:, None]) * rstd[:, None]).reshape(shape).astype(jnp.bfloat16)
    grad_one = taps(padded_in, grad_pre) * scale
    grad_pad = jnp.pad(grad_pre, ((0, 2), (1, 1), (1, 1), (0, 0)))
    grad_upsampled = convolve(grad_pad, flipped(weight_one))
    frames, rows, cols, chans = features.shape
    grad_features = grad_upsampled.reshape(frames, rows, 2, cols, 2, chans).sum((2, 4))
    return (decoded, grad_features, grad_one, grad_two)
```

```python
import functools

import jax
import jax.numpy as jnp
from jax import lax
from jax.sharding import Mesh
from jax.sharding import PartitionSpec as P

GROUPS = 32
EPSILON = 1e-05

TM = ("zh", "y")
HEIGHT = ("zl", "x", "c")
REST = ("zh", "y", "zl")


def fine_mesh(mesh):
    tm, height = mesh.shape["tm"], mesh.shape["height"]
    zh = 2 if tm % 2 == 0 else 1
    core = 2
    x = 4 if height % 8 == 0 else height // 2
    return Mesh(mesh.devices.reshape(zh, tm // zh, height // (core * x), x, core), TM + HEIGHT)


def neighbour(value, axis, steps):
    count = lax.axis_size(axis)
    first, last = max(0, -steps), min(count, count - steps)
    return lax.ppermute(value, axis, [(i, i + steps) for i in range(first, last)])


def row_halo(cells):
    return jnp.concatenate(
        [neighbour(cells[:, -1:], HEIGHT, 1), cells, neighbour(cells[:, :1], HEIGHT, -1)], axis=1
    )


def sum_everywhere(value, stages):
    for axes in stages:
        count = lax.axis_size(axes)
        value = lax.all_to_all(jnp.broadcast_to(value[None], (count,) + value.shape), axes, 0, 0).sum(0)
    return value


def conv(padded, weight):
    return lax.conv_general_dilated(
        padded[None],
        weight,
        (1, 1, 1),
        "VALID",
        dimension_numbers=("NDHWC", "DHWIO", "NDHWC"),
        preferred_element_type=jnp.float32,
    )[0]


def flipped(weight):
    return jnp.transpose(jnp.flip(weight, (0, 1, 2)), (0, 1, 2, 4, 3))


def pad_cols(field):
    return jnp.pad(field, ((0, 0), (0, 0), (1, 1), (0, 0)))


def upsample(field):
    return jnp.repeat(jnp.repeat(field, 2, 1), 2, 2)


def pooled(grad):
    frames, rows, cols, outs = grad.shape
    row_sets = []
    for b in range(3):
        part = grad[:, 2 - b : 2 - b + rows - 2]
        row_sets.append(part.reshape(frames, (rows - 2) // 2, 2, cols, outs).sum(2))
    pieces = []
    for part in row_sets:
        wide = jnp.pad(part, ((0, 0), (0, 0), (1, 1), (0, 0)))
        for e in range(3):
            cell = wide[:, :, 2 - e : 2 - e + cols].reshape(frames, (rows - 2) // 2, cols // 2, 2, outs)
            pieces.append(cell.sum(3))
    return jnp.concatenate(pieces, -1)


def pack(local_one, local_two):
    both = jnp.concatenate([local_one.reshape(-1, 864), local_two.reshape(-1, 864)], 0)
    both = jnp.pad(both, ((0, 0), (0, 32)))
    rows = both.shape[0]
    return jnp.transpose(both.reshape(rows, 7, 128), (1, 0, 2)).reshape(7 * rows, 128)


def unpack(packed, ins, mids):
    rows = 3 * (ins + mids)
    both = jnp.transpose(packed[: 7 * rows].reshape(7, rows, 128), (1, 0, 2)).reshape(rows, 896)
    both = both[:, : 9 * mids]
    one, two = both[: 3 * ins], both[3 * ins :]
    one = jnp.transpose(one.reshape(3, ins, 3, 3, mids), (0, 2, 3, 1, 4))
    two = jnp.transpose(two.reshape(3, mids, 3, 3, mids), (0, 2, 3, 1, 4))
    return one, two


def sum_large(packed):
    core, xs, rest = lax.axis_size("c"), lax.axis_size("x"), lax.axis_size(REST)
    rows = packed.shape[0]
    unit = core * xs * rest
    piece = -(-rows // unit)
    packed = jnp.pad(packed, ((0, piece * unit - rows), (0, 0)))
    swap = [(0, 1), (1, 0)]
    mine = lax.axis_index("c")
    halves = packed.reshape(2, -1, 128)
    away = lax.dynamic_index_in_dim(halves, 1 - mine, 0, False).astype(jnp.bfloat16)
    kept = lax.dynamic_index_in_dim(halves, mine, 0, False)
    part = kept + lax.ppermute(away, "c", swap).astype(jnp.float32)
    part = part.astype(jnp.bfloat16).reshape(xs, -1, 128)
    part = lax.all_to_all(part, "x", 0, 0).astype(jnp.float32).sum(0)
    part = lax.all_to_all(part.reshape(rest, piece, 128), REST, 0, 0).sum(0)
    part = part.astype(jnp.bfloat16)
    part = lax.all_to_all(jnp.broadcast_to(part[None], (rest, piece, 128)), REST, 0, 0)
    part = part.reshape(rest * piece, 128)
    part = lax.all_to_all(jnp.broadcast_to(part[None], (xs,) + part.shape), "x", 0, 0)
    part = part.reshape(-1, 128)
    other = lax.ppermute(part, "c", swap)
    low = jnp.where(mine == 0, part, other)
    high = jnp.where(mine == 0, other, part)
    return jnp.concatenate([low, high], 0)


def body(features, cotangent, weight_one, weight_two, norm_gain, norm_shift):
    frames, ins = features.shape[0], features.shape[-1]
    mids = cotangent.shape[-1]
    devices_all = lax.axis_size(TM) * lax.axis_size(HEIGHT)
    per_group = mids // GROUPS
    member = jnp.arange(mids) // per_group
    same_group = (member[:, None] == member[None]).astype(jnp.float32)

    def group_sums(first, second, stages):
        both = jnp.stack([first, second])
        both = jnp.dot(both, same_group, precision=lax.Precision.HIGHEST)
        return sum_everywhere(both, stages)

    timed = jnp.concatenate([neighbour(features, TM, 1), features], 0)
    rowed = row_halo(timed)
    padded_in = pad_cols(upsample(rowed)[:, 1:-1])
    pre_norm = conv(padded_in, weight_one)
    shape = pre_norm.shape
    count = shape[0] * shape[1] * shape[2] * per_group * devices_all
    total_one, total_two = group_sums(
        jnp.sum(pre_norm, (0, 1, 2)), jnp.sum(pre_norm * pre_norm, (0, 1, 2)), (HEIGHT, TM)
    )
    cot_rowed = row_halo(jnp.concatenate([cotangent, neighbour(cotangent, TM, -1)], 0))
    grad_hidden = conv(pad_cols(cot_rowed), flipped(weight_two))

    mean = total_one / count
    rstd = lax.rsqrt(total_two / count - mean * mean + EPSILON)
    normed = (pre_norm - mean) * rstd
    shifted = normed * norm_gain + norm_shift
    sigma = jax.nn.sigmoid(shifted)
    hidden = (shifted * sigma).astype(jnp.bfloat16)
    grad_normed = grad_hidden * sigma * (1.0 + shifted * (1.0 - sigma)) * norm_gain
    sum_first, sum_second = group_sums(
        jnp.sum(grad_normed, (0, 1, 2)),
        jnp.sum(grad_normed * normed, (0, 1, 2)),
        (("y", "c"), ("zh", "zl", "x")),
    )
    mid_rowed = row_halo(jnp.concatenate([neighbour(hidden[frames - 2 :], TM, 1), hidden], 0))
    decoded = conv(pad_cols(mid_rowed), weight_two).astype(jnp.bfloat16)

    scale = 1.0 / (shape[0] * shape[1] * shape[2] * devices_all) ** 0.5
    wide_cot = pad_cols(cot_rowed)
    shifted_cot = jnp.concatenate(
        [
            wide_cot[:, 2 - b : 2 - b + shape[1], 2 - e : 2 - e + shape[2]]
            for b in range(3)
            for e in range(3)
        ],
        -1,
    )
    flat_hidden = hidden.reshape(-1, mids)
    local_two = jnp.stack(
        [
            lax.dot_general(
                flat_hidden,
                shifted_cot[2 - a : 2 - a + frames].reshape(-1, 9 * mids),
                (((0,), (0,)), ((), ())),
                preferred_element_type=jnp.float32,
            )
            for a in range(3)
        ]
    )

    first = sum_first / count
    second = sum_second / count
    grad_pre = ((grad_normed - first - normed * second) * rstd).astype(jnp.bfloat16)
    local = pooled(jnp.pad(grad_pre, ((0, 0), (3, 3), (0, 0), (0, 0))).astype(jnp.float32))
    local = local.astype(jnp.bfloat16).reshape(-1, 9 * mids)
    local_one = jnp.stack(
        [
            lax.dot_general(
                rowed[a : a + frames].reshape(-1, ins),
                local,
                (((0,), (0,)), ((), ())),
                preferred_element_type=jnp.float32,
            )
            for a in range(3)
        ]
    )
    summed_one, summed_two = unpack(sum_large(pack(local_one, local_two)), ins, mids)
    grad_one = summed_one.astype(jnp.float32) * scale
    grad_two = summed_two.astype(jnp.float32) * scale

    grad_rowed = row_halo(jnp.concatenate([grad_pre, neighbour(grad_pre, TM, -1)], 0))
    cells = pooled(grad_rowed.astype(jnp.float32)).astype(jnp.bfloat16)
    back = jnp.transpose(weight_one, (0, 1, 2, 4, 3)).reshape(3, 9 * mids, ins)
    grad_features = sum(
        lax.dot_general(
            cells[2 - a : 2 - a + frames],
            back[a],
            (((3,), (0,)), ((), ())),
            preferred_element_type=jnp.float32,
        )
        for a in range(3)
    )
    return decoded, grad_features, grad_one, grad_two


def solution(mesh):
    split = P(TM, HEIGHT, None, None)
    return jax.shard_map(
        body,
        mesh=fine_mesh(mesh),
        in_specs=(split, split, P(), P(), P(), P()),
        out_specs=(split, split, P(), P()),
        check_vma=False,
    )
```

```python
import functools

import jax
import jax.numpy as jnp
from jax import lax
from jax.experimental import pallas as pl
from jax.experimental.pallas import tpu as pltpu
from jax.sharding import Mesh
from jax.sharding import PartitionSpec as P

GROUPS = 32
EPSILON = 1e-05

TM = ("zh", "y")
HEIGHT = ("zl", "x", "c")
REST = ("zh", "y", "zl")

VMEM_LIMIT = 32 * 2**20


def fine_mesh(mesh):
    tm, height = mesh.shape["tm"], mesh.shape["height"]
    zh = 2 if tm % 2 == 0 else 1
    core = 2
    x = 4 if height % 8 == 0 else height // 2
    return Mesh(mesh.devices.reshape(zh, tm // zh, height // (core * x), x, core), TM + HEIGHT)


def neighbour(value, axis, steps):
    count = lax.axis_size(axis)
    first, last = max(0, -steps), min(count, count - steps)
    return lax.ppermute(value, axis, [(i, i + steps) for i in range(first, last)])


def row_halo(cells):
    return jnp.concatenate(
        [neighbour(cells[:, -1:], HEIGHT, 1), cells, neighbour(cells[:, :1], HEIGHT, -1)], axis=1
    )


def stage_sum(value, axes):
    count = lax.axis_size(axes)
    return lax.all_to_all(jnp.broadcast_to(value[None], (count,) + value.shape), axes, 0, 0).sum(0)


def conv(padded, weight):
    return lax.conv_general_dilated(
        padded[None],
        weight,
        (1, 1, 1),
        "VALID",
        dimension_numbers=("NDHWC", "DHWIO", "NDHWC"),
        preferred_element_type=jnp.float32,
    )[0]


def flipped(weight):
    return jnp.transpose(jnp.flip(weight, (0, 1, 2)), (0, 1, 2, 4, 3))


def pad_cols(field):
    return jnp.pad(field, ((0, 0), (0, 0), (1, 1), (0, 0)))


def upsample(field):
    return jnp.repeat(jnp.repeat(field, 2, 1), 2, 2)


def col_sums(wide, cells):
    half = cells.shape[1] // 2
    wide[...] = jnp.zeros_like(wide)
    wide[:, 8 : 8 + cells.shape[1], : cells.shape[2]] = cells

    def every_second(start):
        return wide[:, pl.ds(start, half, stride=2), : cells.shape[2]]

    before, even, odd, after = (every_second(7 + k) for k in range(4))
    return odd + after, even + odd, before + even


def weight_grads_kernel(core, rows_in, grad_normed, normed, vectors, two, grad_pre, away, kept, wide):
    frames, rows, cols, outs = grad_normed.shape
    ins, mids = rows_in.shape[-1], two.shape[1]
    first, second, rstd = (vectors[k : k + 1] for k in range(3))
    merged = (frames * rows * cols, outs)
    grad = grad_normed[...].reshape(merged) - first - normed[...].reshape(merged) * second
    grad = (grad * rstd).astype(jnp.bfloat16)
    grad_pre[...] = grad.reshape(grad_pre.shape)
    by_tap = col_sums(wide, grad.astype(jnp.float32).reshape(frames * rows, cols, outs))
    pieces = []
    for b in range(3):
        for e in range(3):
            part = by_tap[e].reshape(frames, rows, cols // 2, outs)
            none = jnp.zeros_like(part[:, 0])
            r = [part[:, k] for k in range(rows)]
            stacked = (
                [r[0], r[1] + r[2], r[3], none],
                [none, r[0] + r[1], r[2] + r[3], none],
                [none, r[0], r[1] + r[2], r[3]],
            )[b]
            cells = jnp.stack(stacked, 1).astype(jnp.bfloat16)
            pieces.append(cells.reshape(-1, outs))
    pieces.append(jnp.zeros((pieces[0].shape[0], 32), jnp.bfloat16))
    cells = jnp.concatenate(pieces, 1)
    lower = core[0] == 0

    def write(at, low, high):
        away[at : at + low.shape[0]] = jnp.where(lower, high, low).astype(jnp.bfloat16)
        kept[at : at + low.shape[0]] = jnp.where(lower, low, high)

    at = 0
    for a in range(3):
        product = lax.dot_general(
            rows_in[a : a + frames].reshape(-1, ins),
            cells,
            (((0,), (0,)), ((), ())),
            preferred_element_type=jnp.float32,
        )
        for j in range(7):
            block = product[:, 128 * j : 128 * j + 128]
            write(at, block[: ins // 2], block[ins // 2 :])
            at += ins // 2
    for a in range(3):
        product = two[a]
        for j in range(7):
            block = product[:, 128 * j : 128 * j + 128]
            write(at, block[: mids // 2], block[mids // 2 :])
            at += mids // 2
    if at < kept.shape[0]:
        tail = jnp.zeros((kept.shape[0] - at, 128), jnp.float32)
        away[at:] = tail.astype(jnp.bfloat16)
        kept[at:] = tail


def weight_grads(core, rows_in, grad_normed, normed, vectors, two, half_rows):
    frames, rows, cols, outs = grad_normed.shape
    whole = pl.BlockSpec(memory_space=pltpu.VMEM)
    return pl.pallas_call(
        weight_grads_kernel,
        out_shape=(
            jax.ShapeDtypeStruct(grad_normed.shape, jnp.bfloat16),
            jax.ShapeDtypeStruct((half_rows, 128), jnp.bfloat16),
            jax.ShapeDtypeStruct((half_rows, 128), jnp.float32),
        ),
        in_specs=[pl.BlockSpec(memory_space=pltpu.SMEM)] + [whole] * 5,
        out_specs=[whole] * 3,
        scratch_shapes=[pltpu.VMEM((frames * rows, cols + 16, 128), jnp.float32)],
        compiler_params=pltpu.CompilerParams(vmem_limit_bytes=VMEM_LIMIT),
        name="weight_grads",
    )(core, rows_in, grad_normed, normed, vectors, two)


def unpack_kernel(scale, core, mine_one, other_one, mine_two, other_two, one, two):
    lower = core[0] == 0
    for mine, other, out in ((mine_one, other_one, one), (mine_two, other_two, two)):
        taps, rows, outs = out.shape
        half = rows // 2
        own = jnp.concatenate([mine[half * j : half * j + half] for j in range(7)], 1)
        far = jnp.concatenate([other[half * j : half * j + half] for j in range(7)], 1)
        own, far = own.astype(jnp.float32) * scale, far.astype(jnp.float32) * scale
        low, high = jnp.where(lower, own, far), jnp.where(lower, far, own)
        for k in range(taps):
            out[k, :half] = low[:, outs * k : outs * k + outs]
            out[k, half:] = high[:, outs * k : outs * k + outs]


def unpack(core, mine, other, ins, mids, scale):
    half_one, half_two = 7 * ins // 2, 7 * mids // 2
    skip = 3 * half_one // half_two
    block_one = pl.BlockSpec((half_one, 128), lambda a: (a, 0))
    block_two = pl.BlockSpec((half_two, 128), lambda a: (a + skip, 0))
    return pl.pallas_call(
        functools.partial(unpack_kernel, scale),
        grid=(3,),
        out_shape=(
            jax.ShapeDtypeStruct((27, ins, mids), jnp.float32),
            jax.ShapeDtypeStruct((27, mids, mids), jnp.float32),
        ),
        in_specs=[pl.BlockSpec(memory_space=pltpu.SMEM), block_one, block_one, block_two, block_two],
        out_specs=[
            pl.BlockSpec((9, ins, mids), lambda a: (a, 0, 0)),
            pl.BlockSpec((9, mids, mids), lambda a: (a, 0, 0)),
        ],
        compiler_params=pltpu.CompilerParams(vmem_limit_bytes=VMEM_LIMIT),
        name="unpack",
    )(core, mine, other, mine, other)


def feature_grads_kernel(grad_pre, weight, out, wide):
    frames, rows, cols, outs = grad_pre.shape
    own, cells_in, cols_in, ins = out.shape
    by_tap = col_sums(wide, grad_pre[...].astype(jnp.float32).reshape(frames * rows, cols, outs))
    total = jnp.zeros((own * cells_in * cols_in, ins), jnp.float32)
    for b in range(3):
        for e in range(3):
            part = by_tap[e].reshape(frames, rows, cols // 2, outs)
            cells = jnp.stack(
                [part[:, 2 * k + 2 - b] + part[:, 2 * k + 3 - b] for k in range(cells_in)], 1
            ).astype(jnp.bfloat16)
            for a in range(3):
                total += lax.dot_general(
                    cells[2 - a : 2 - a + own].reshape(-1, outs),
                    weight[a, b, e],
                    (((1,), (1,)), ((), ())),
                    preferred_element_type=jnp.float32,
                )
    out[...] = total.reshape(out.shape)


def feature_grads(grad_rowed, weight, shape):
    frames, rows, cols, _ = grad_rowed.shape
    whole = pl.BlockSpec(memory_space=pltpu.VMEM)
    return pl.pallas_call(
        feature_grads_kernel,
        out_shape=jax.ShapeDtypeStruct(shape, jnp.float32),
        in_specs=[whole] * 2,
        out_specs=whole,
        scratch_shapes=[pltpu.VMEM((frames * rows, cols + 16, 128), jnp.float32)],
        compiler_params=pltpu.CompilerParams(vmem_limit_bytes=VMEM_LIMIT),
        cost_estimate=pl.CostEstimate(flops=2**28, bytes_accessed=2**21, transcendentals=0),
        name="feature_grads",
    )(grad_rowed, weight)


def half_rows(ins, mids):
    unit = lax.axis_size("x") * lax.axis_size(REST)
    return -(-(21 * (ins + mids) // 2) // unit) * unit


SWAP = [(0, 1), (1, 0)]


def body(features, cotangent, weight_one, weight_two, norm_gain, norm_shift):
    frames, ins = features.shape[0], features.shape[-1]
    mids = cotangent.shape[-1]
    xs, rest = lax.axis_size("x"), lax.axis_size(REST)
    devices_all = 2 * xs * rest
    per_group = mids // GROUPS
    member = jnp.arange(mids) // per_group
    same_group = (member[:, None] == member[None]).astype(jnp.float32)
    core = lax.axis_index("c").astype(jnp.int32).reshape(1)
    barrier = lax.optimization_barrier

    def group_sums(first, second):
        both = jnp.stack([first, second])
        return jnp.dot(both, same_group, precision=lax.Precision.HIGHEST)

    timed = jnp.concatenate([neighbour(features, TM, 1), features], 0)
    rowed = row_halo(timed)
    padded_in = pad_cols(upsample(rowed)[:, 1:-1])
    pre_norm = conv(padded_in, weight_one)
    shape = pre_norm.shape
    count = shape[0] * shape[1] * shape[2] * per_group * devices_all
    sums = group_sums(jnp.sum(pre_norm, (0, 1, 2)), jnp.sum(pre_norm * pre_norm, (0, 1, 2)))
    sums, cotangent = barrier((sums, cotangent))
    sums = stage_sum(sums, HEIGHT)
    cot_timed = jnp.concatenate([cotangent, neighbour(cotangent, TM, -1)], 0)
    sums, cot_timed = barrier((sums, cot_timed))
    sums = stage_sum(sums, TM)
    wide_cot = pad_cols(row_halo(cot_timed))
    grad_hidden = conv(wide_cot, flipped(weight_two))
    shifted_cot = jnp.concatenate(
        [
            wide_cot[:, 2 - b : 2 - b + shape[1], 2 - e : 2 - e + shape[2]]
            for b in range(3)
            for e in range(3)
        ],
        -1,
    )
    (total_one, total_two), grad_hidden, shifted_cot = barrier((sums, grad_hidden, shifted_cot))

    mean = total_one / count
    rstd = lax.rsqrt(total_two / count - mean * mean + EPSILON)
    normed = (pre_norm - mean) * rstd
    shifted = normed * norm_gain + norm_shift
    sigma = jax.nn.sigmoid(shifted)
    hidden = (shifted * sigma).astype(jnp.bfloat16)
    grad_normed = grad_hidden * sigma * (1.0 + shifted * (1.0 - sigma)) * norm_gain
    sums = group_sums(jnp.sum(grad_normed, (0, 1, 2)), jnp.sum(grad_normed * normed, (0, 1, 2)))
    sums, hidden = barrier((sums, hidden))
    sums = stage_sum(sums, ("y", "c"))
    mid_timed = jnp.concatenate([neighbour(hidden[frames - 2 :], TM, 1), hidden], 0)
    flat_hidden = hidden.reshape(-1, mids)
    local_two = jnp.stack(
        [
            lax.dot_general(
                flat_hidden,
                shifted_cot[2 - a : 2 - a + frames].reshape(-1, 9 * mids),
                (((0,), (0,)), ((), ())),
                preferred_element_type=jnp.float32,
            )
            for a in range(3)
        ]
    )
    sums, mid_timed, local_two = barrier((sums, mid_timed, local_two))
    sums = stage_sum(sums, ("zh", "zl", "x"))
    mid_rowed = row_halo(mid_timed)
    sums, mid_rowed = barrier((sums, mid_rowed))

    scale = 1.0 / (shape[0] * shape[1] * shape[2] * devices_all) ** 0.5
    vectors = jnp.concatenate([sums / count, rstd[None]], 0)
    local_two = jnp.pad(local_two, ((0, 0), (0, 0), (0, 32)))
    grad_pre, away, kept = weight_grads(
        core, rowed, grad_normed, normed, vectors, local_two, half_rows(ins, mids)
    )

    part = kept + lax.ppermute(away, "c", SWAP).astype(jnp.float32)
    part = part.astype(jnp.bfloat16).reshape(xs, -1, 128)
    part, grad_pre, mid_rowed = barrier((part, grad_pre, mid_rowed))
    part = lax.all_to_all(part, "x", 0, 0).astype(jnp.float32).sum(0)
    grad_timed = jnp.concatenate([grad_pre, neighbour(grad_pre, TM, -1)], 0)
    part, grad_timed = barrier((part, grad_timed))
    part = lax.all_to_all(part.reshape(rest, -1, 128), REST, 0, 0).sum(0).astype(jnp.bfloat16)
    grad_rowed = row_halo(grad_timed)
    part, grad_rowed = barrier((part, grad_rowed))
    part = lax.all_to_all(jnp.broadcast_to(part[None], (rest,) + part.shape), REST, 0, 0)
    decoded = conv(pad_cols(mid_rowed), weight_two).astype(jnp.bfloat16)
    part, decoded, grad_rowed = barrier((part.reshape(-1, 128), decoded, grad_rowed))
    part = lax.all_to_all(jnp.broadcast_to(part[None], (xs,) + part.shape), "x", 0, 0)
    grad_features = feature_grads(grad_rowed, weight_one, features.shape)
    part, grad_features = barrier((part.reshape(-1, 128), grad_features))
    grad_one, grad_two = unpack(core, part, lax.ppermute(part, "c", SWAP), ins, mids, scale)
    return decoded, grad_features, grad_one.reshape(weight_one.shape), grad_two.reshape(weight_two.shape)


def solution(mesh):
    split = P(TM, HEIGHT, None, None)
    return jax.shard_map(
        body,
        mesh=fine_mesh(mesh),
        in_specs=(split, split, P(), P(), P(), P()),
        out_specs=(split, split, P(), P()),
        check_vma=False,
    )
```

```python
import functools

import jax
import jax.numpy as jnp
from jax import lax
from jax.experimental import pallas as pl
from jax.experimental.pallas import tpu as pltpu
from jax.sharding import Mesh
from jax.sharding import PartitionSpec as P

GROUPS = 32
EPSILON = 1e-05

TM = ("zh", "y")
HEIGHT = ("zl", "x", "c")
REST = ("zh", "y", "zl")

VMEM_LIMIT = 32 * 2**20


def fine_mesh(mesh):
    tm, height = mesh.shape["tm"], mesh.shape["height"]
    zh = 2 if tm % 2 == 0 else 1
    core = 2
    x = 4 if height % 8 == 0 else height // 2
    return Mesh(mesh.devices.reshape(zh, tm // zh, height // (core * x), x, core), TM + HEIGHT)


def neighbour(value, axis, steps):
    count = lax.axis_size(axis)
    first, last = max(0, -steps), min(count, count - steps)
    return lax.ppermute(value, axis, [(i, i + steps) for i in range(first, last)])


def conv(padded, weight):
    return lax.conv_general_dilated(
        padded[None],
        weight,
        (1, 1, 1),
        "VALID",
        dimension_numbers=("NDHWC", "DHWIO", "NDHWC"),
        preferred_element_type=jnp.float32,
    )[0]


def whole(count=1, space=pltpu.VMEM):
    return [pl.BlockSpec(memory_space=space)] * count


def group_sums(first, second, outs):
    member = lax.broadcasted_iota(jnp.int32, (2, outs, outs), 1) // (outs // GROUPS)
    other = lax.broadcasted_iota(jnp.int32, (2, outs, outs), 2) // (outs // GROUPS)
    same = (member[0] == other[0]).astype(jnp.float32)
    both = jnp.concatenate([first, second, jnp.zeros((6, outs), jnp.float32)], 0)
    return jnp.dot(both, same, precision=lax.Precision.HIGHEST, preferred_element_type=jnp.float32)[:2]


def cell_sums(field):
    return jnp.sum(field.reshape(-1, field.shape[-1]), 0, keepdims=True)


def inside(where, field):
    row = lax.broadcasted_iota(jnp.int32, field.shape, 1)
    last = field.shape[1] - 1
    out = ((row == 0) & (where[1] == 1)) | ((row == last) & (where[2] == 1))
    return jnp.where(out, 0.0, field)


def conv_one_kernel(cache, features, above, below, weight, pre_norm, sums, wide):
    frames, rows, cols, outs = pre_norm.shape
    cells_in, half, ins = features.shape[1], cols // 2, features.shape[-1]
    timed = jnp.concatenate([cache[...], features[...]], 0)
    rowed = jnp.concatenate([above[:, :half][:, None], timed, below[:, :half][:, None]], 1)
    by_tap = []
    for e in range(3):
        total = jnp.zeros((frames, rows, half, outs), jnp.float32)
        for b in range(3):
            product = sum(
                jnp.dot(
                    rowed[a : a + frames].reshape(-1, ins),
                    weight[a, b, e],
                    preferred_element_type=jnp.float32,
                )
                for a in range(3)
            ).reshape(frames, cells_in + 2, half, outs)
            total += jnp.stack([product[:, (r + b) // 2] for r in range(rows)], 1)
        by_tap.append(total.reshape(frames * rows, half, outs))
    wide[...] = jnp.zeros_like(wide)
    wide[:, 8 : 8 + half, :outs] = by_tap[0]
    even = wide[:, 7 : 7 + half, :outs] + by_tap[1] + by_tap[2]
    wide[:, 8 : 8 + half, :outs] = by_tap[2]
    odd = by_tap[0] + by_tap[1] + wide[:, 9 : 9 + half, :outs]
    wide[:, pl.ds(0, half, stride=2), :outs] = even
    wide[:, pl.ds(1, half, stride=2), :outs] = odd
    pre = wide[:, :cols, :outs].reshape(pre_norm.shape)
    pre_norm[...] = pre
    own = pre[:, 1:-1]
    both = group_sums(cell_sums(own), cell_sums(own * own), outs)
    sums[...] = jnp.broadcast_to(both[None], sums.shape)


def conv_one(cache, features, above, below, weight, copies):
    frames, cells_in, half, _ = features.shape
    outs = weight.shape[-1]
    rows, cols = 2 * cells_in + 2, 2 * half
    return pl.pallas_call(
        conv_one_kernel,
        out_shape=(
            jax.ShapeDtypeStruct((frames, rows, cols, outs), jnp.float32),
            jax.ShapeDtypeStruct((copies, 2, outs), jnp.float32),
        ),
        in_specs=whole(5),
        out_specs=whole(2),
        scratch_shapes=[pltpu.VMEM((frames * rows, cols + 16, 128), jnp.float32)],
        compiler_params=pltpu.CompilerParams(vmem_limit_bytes=VMEM_LIMIT),
        name="conv_one",
    )(cache, features, above, below, weight)


def grad_hidden_kernel(cot, later, above, below, weight, grad_hidden, shifted, wide):
    frames, rows, cols, ins = grad_hidden.shape
    outs = cot.shape[-1]
    half = cols // 2
    timed = jnp.concatenate([cot[...], later[...]], 0)
    pair = lambda part: jnp.stack([part[:, half:, :outs], part[:, half:, outs:]], 1)
    rowed = jnp.concatenate([pair(above), timed, pair(below)], 1).astype(jnp.float32)
    wide[...] = jnp.zeros_like(wide)
    wide[:, 8 : 8 + cols, :outs] = rowed.reshape(-1, cols, outs)
    total = jnp.zeros((frames * rows * cols, ins), jnp.float32)
    for e in range(3):
        part = wide[:, 9 - e : 9 - e + cols, :outs].astype(jnp.bfloat16)
        part = part.reshape(2 * frames, rows + 2, cols, outs)
        shifted[e] = part
        for a in range(3):
            for b in range(3):
                total += lax.dot_general(
                    part[2 - a : 2 - a + frames, 2 - b : 2 - b + rows].reshape(-1, outs),
                    weight[a, b, e],
                    (((1,), (1,)), ((), ())),
                    preferred_element_type=jnp.float32,
                )
    grad_hidden[...] = total.reshape(grad_hidden.shape)


def hidden_grads(cot, later, above, below, weight):
    frames, rows, cols, outs = cot.shape
    return pl.pallas_call(
        grad_hidden_kernel,
        out_shape=(
            jax.ShapeDtypeStruct((frames, rows + 2, cols, weight.shape[-2]), jnp.float32),
            jax.ShapeDtypeStruct((3, 2 * frames, rows + 4, cols, outs), jnp.bfloat16),
        ),
        in_specs=whole(5),
        out_specs=whole(2),
        scratch_shapes=[pltpu.VMEM((2 * frames * (rows + 4), cols + 16, 128), jnp.float32)],
        compiler_params=pltpu.CompilerParams(vmem_limit_bytes=VMEM_LIMIT),
        cost_estimate=pl.CostEstimate(flops=2**30, bytes_accessed=2**21, transcendentals=0),
        name="grad_hidden",
    )(cot, later, above, below, weight)


def middle_kernel(count, where, came, pre_norm, grad_hidden, gain, shift, hidden, grad_normed, normed, rstd, sums):
    outs = pre_norm.shape[-1]
    total = jnp.sum(came[...], 0)
    mean = total[:1] / count
    scaled = lax.rsqrt(total[1:2] / count - mean * mean + EPSILON)
    rstd[...] = scaled
    flat = (pre_norm[...].reshape(-1, outs) - mean) * scaled
    shifted = flat * gain[...] + shift[...]
    sigma = 1.0 / (1.0 + jnp.exp(-shifted))
    hidden[...] = inside(where, (shifted * sigma).reshape(pre_norm.shape)).astype(jnp.bfloat16)
    grad = grad_hidden[...].reshape(-1, outs) * sigma * (1.0 + shifted * (1.0 - sigma)) * gain[...]
    grad, flat = grad.reshape(pre_norm.shape), flat.reshape(pre_norm.shape)
    grad_normed[...] = grad
    normed[...] = flat
    own = grad[:, 1:-1]
    both = group_sums(cell_sums(own), cell_sums(own * flat[:, 1:-1]), outs)
    sums[...] = jnp.broadcast_to(both[None], sums.shape)


def middle(count, where, came, pre_norm, grad_hidden, gain, shift, copies):
    shape, outs = pre_norm.shape, pre_norm.shape[-1]
    return pl.pallas_call(
        functools.partial(middle_kernel, count),
        out_shape=(
            jax.ShapeDtypeStruct(shape, jnp.bfloat16),
            jax.ShapeDtypeStruct(shape, jnp.float32),
            jax.ShapeDtypeStruct(shape, jnp.float32),
            jax.ShapeDtypeStruct((1, outs), jnp.float32),
            jax.ShapeDtypeStruct((copies, 2, outs), jnp.float32),
        ),
        in_specs=whole(1, pltpu.SMEM) + whole(5),
        out_specs=whole(5),
        compiler_params=pltpu.CompilerParams(vmem_limit_bytes=VMEM_LIMIT),
        name="middle",
    )(where, came, pre_norm, grad_hidden, gain[None], shift[None])


def second_weight_kernel(hidden, shifted, out):
    frames, rows, cols, ins = hidden.shape
    outs = shifted.shape[-1]
    own = hidden[:, 1:-1].reshape(-1, ins).astype(jnp.float32).T.astype(jnp.bfloat16)
    for a in range(3):
        pieces = [
            shifted[e, 2 - a : 2 - a + frames, 3 - b : 3 - b + rows - 2].reshape(-1, outs)
            for b in range(3)
            for e in range(3)
        ]
        pieces.append(jnp.zeros((pieces[0].shape[0], 32), jnp.bfloat16))
        out[a] = jnp.dot(own, jnp.concatenate(pieces, 1), preferred_element_type=jnp.float32)


def second_weight(hidden, shifted):
    return pl.pallas_call(
        second_weight_kernel,
        out_shape=jax.ShapeDtypeStruct((3, hidden.shape[-1], 896), jnp.float32),
        in_specs=whole(2),
        out_specs=whole()[0],
        compiler_params=pltpu.CompilerParams(vmem_limit_bytes=VMEM_LIMIT),
        cost_estimate=pl.CostEstimate(flops=2**29, bytes_accessed=2**21, transcendentals=0),
        name="second_weight",
    )(hidden, shifted)


def col_sums(wide, cells):
    half = cells.shape[1] // 2
    wide[...] = jnp.zeros_like(wide)
    wide[:, 8 : 8 + cells.shape[1], : cells.shape[2]] = cells

    def every_second(start):
        return wide[:, pl.ds(start, half, stride=2), : cells.shape[2]]

    before, even, odd, after = (every_second(7 + k) for k in range(4))
    return odd + after, even + odd, before + even


def weight_grads_kernel(
    count, where, cache, features, above, below, came, grad_normed, normed, rstd, two, grad_pre, away, kept, wide
):
    frames, rows, cols, outs = grad_normed.shape
    ins, mids = features.shape[-1], two.shape[1]
    total = jnp.sum(came[...], 0) / count
    timed = jnp.concatenate([cache[...], features[...]], 0)
    rows_in = jnp.concatenate([above[:, : cols // 2][:, None], timed, below[:, : cols // 2][:, None]], 1)
    merged = (frames * rows * cols, outs)
    grad = grad_normed[...].reshape(merged) - total[:1] - normed[...].reshape(merged) * total[1:2]
    grad = inside(where, (grad * rstd[...]).reshape(grad_normed.shape)).astype(jnp.bfloat16)
    grad_pre[...] = grad
    grad = grad[:, 1:-1].astype(jnp.float32)
    rows = rows - 2
    by_tap = col_sums(wide, grad.reshape(frames * rows, cols, outs))
    pieces = []
    for b in range(3):
        for e in range(3):
            part = by_tap[e].reshape(frames, rows, cols // 2, outs)
            none = jnp.zeros_like(part[:, 0])
            r = [part[:, k] for k in range(rows)]
            stacked = (
                [r[0], r[1] + r[2], r[3], none],
                [none, r[0] + r[1], r[2] + r[3], none],
                [none, r[0], r[1] + r[2], r[3]],
            )[b]
            cells = jnp.stack(stacked, 1).astype(jnp.bfloat16)
            pieces.append(cells.reshape(-1, outs))
    pieces.append(jnp.zeros((pieces[0].shape[0], 32), jnp.bfloat16))
    cells = jnp.concatenate(pieces, 1)
    lower = where[0] == 0

    def write(at, low, high):
        away[at : at + low.shape[0]] = jnp.where(lower, high, low).astype(jnp.bfloat16)
        kept[at : at + low.shape[0]] = jnp.where(lower, low, high)

    at = 0
    for a in range(3):
        product = lax.dot_general(
            rows_in[a : a + frames].reshape(-1, ins),
            cells,
            (((0,), (0,)), ((), ())),
            preferred_element_type=jnp.float32,
        )
        for j in range(7):
            block = product[:, 128 * j : 128 * j + 128]
            write(at, block[: ins // 2], block[ins // 2 :])
            at += ins // 2
    for a in range(3):
        product = two[a]
        for j in range(7):
            block = product[:, 128 * j : 128 * j + 128]
            write(at, block[: mids // 2], block[mids // 2 :])
            at += mids // 2
    if at < kept.shape[0]:
        tail = jnp.zeros((kept.shape[0] - at, 128), jnp.float32)
        away[at:] = tail.astype(jnp.bfloat16)
        kept[at:] = tail


def weight_grads(count, where, cache, features, above, below, came, grad_normed, normed, rstd, two, half_rows):
    frames, rows, cols, outs = grad_normed.shape
    return pl.pallas_call(
        functools.partial(weight_grads_kernel, count),
        out_shape=(
            jax.ShapeDtypeStruct(grad_normed.shape, jnp.bfloat16),
            jax.ShapeDtypeStruct((half_rows, 128), jnp.bfloat16),
            jax.ShapeDtypeStruct((half_rows, 128), jnp.float32),
        ),
        in_specs=whole(1, pltpu.SMEM) + whole(9),
        out_specs=whole(3),
        scratch_shapes=[pltpu.VMEM((frames * (rows - 2), cols + 16, 128), jnp.float32)],
        compiler_params=pltpu.CompilerParams(vmem_limit_bytes=VMEM_LIMIT),
        name="weight_grads",
    )(where, cache, features, above, below, came, grad_normed, normed, rstd, two)


def unpack_kernel(scale, where, mine_one, other_one, mine_two, other_two, one, two):
    lower = where[0] == 0
    for mine, other, out in ((mine_one, other_one, one), (mine_two, other_two, two)):
        taps, rows, outs = out.shape
        half = rows // 2
        own = jnp.concatenate([mine[half * j : half * j + half] for j in range(7)], 1)
        far = jnp.concatenate([other[half * j : half * j + half] for j in range(7)], 1)
        own, far = own.astype(jnp.float32) * scale, far.astype(jnp.float32) * scale
        low, high = jnp.where(lower, own, far), jnp.where(lower, far, own)
        for k in range(taps):
            out[k, :half] = low[:, outs * k : outs * k + outs]
            out[k, half:] = high[:, outs * k : outs * k + outs]


def unpack(where, mine, other, ins, mids, scale):
    half_one, half_two = 7 * ins // 2, 7 * mids // 2
    skip = 3 * half_one // half_two
    block_one = pl.BlockSpec((half_one, 128), lambda a: (a, 0))
    block_two = pl.BlockSpec((half_two, 128), lambda a: (a + skip, 0))
    return pl.pallas_call(
        functools.partial(unpack_kernel, scale),
        grid=(3,),
        out_shape=(
            jax.ShapeDtypeStruct((27, ins, mids), jnp.float32),
            jax.ShapeDtypeStruct((27, mids, mids), jnp.float32),
        ),
        in_specs=[pl.BlockSpec(memory_space=pltpu.SMEM), block_one, block_one, block_two, block_two],
        out_specs=[
            pl.BlockSpec((9, ins, mids), lambda a: (a, 0, 0)),
            pl.BlockSpec((9, mids, mids), lambda a: (a, 0, 0)),
        ],
        compiler_params=pltpu.CompilerParams(vmem_limit_bytes=VMEM_LIMIT),
        name="unpack",
    )(where, mine, other, mine, other)


def feature_grads_kernel(grad_pre, weight, out, wide):
    frames, rows, cols, outs = grad_pre.shape
    own, cells_in, cols_in, ins = out.shape
    by_tap = col_sums(wide, grad_pre[...].astype(jnp.float32).reshape(frames * rows, cols, outs))
    total = jnp.zeros((own * cells_in * cols_in, ins), jnp.float32)
    for b in range(3):
        for e in range(3):
            part = by_tap[e].reshape(frames, rows, cols // 2, outs)
            cells = jnp.stack(
                [part[:, 2 * k + 2 - b] + part[:, 2 * k + 3 - b] for k in range(cells_in)], 1
            ).astype(jnp.bfloat16)
            for a in range(3):
                total += lax.dot_general(
                    cells[2 - a : 2 - a + own].reshape(-1, outs),
                    weight[a, b, e],
                    (((1,), (1,)), ((), ())),
                    preferred_element_type=jnp.float32,
                )
    out[...] = total.reshape(out.shape)


def feature_grads(grad_rowed, weight, shape):
    frames, rows, cols, _ = grad_rowed.shape
    return pl.pallas_call(
        feature_grads_kernel,
        out_shape=jax.ShapeDtypeStruct(shape, jnp.float32),
        in_specs=whole(2),
        out_specs=whole()[0],
        scratch_shapes=[pltpu.VMEM((frames * rows, cols + 16, 128), jnp.float32)],
        compiler_params=pltpu.CompilerParams(vmem_limit_bytes=VMEM_LIMIT),
        cost_estimate=pl.CostEstimate(flops=2**28, bytes_accessed=2**21, transcendentals=0),
        name="feature_grads",
    )(grad_rowed, weight)


def half_rows(ins, mids):
    unit = lax.axis_size("x") * lax.axis_size(REST)
    return -(-(21 * (ins + mids) // 2) // unit) * unit


SWAP = [(0, 1), (1, 0)]


def body(features, cotangent, weight_one, weight_two, norm_gain, norm_shift):
    frames, ins = features.shape[0], features.shape[-1]
    rows, cols, mids = cotangent.shape[1:]
    xs, rest, height = lax.axis_size("x"), lax.axis_size(REST), lax.axis_size(HEIGHT)
    cells = frames * rows * cols * 2 * xs * rest
    count = cells * (mids // GROUPS)
    at_row = lax.axis_index(HEIGHT)
    where = jnp.stack([lax.axis_index("c"), at_row == 0, at_row == height - 1]).astype(jnp.int32)
    barrier = lax.optimization_barrier

    def exchange(copies, axes):
        return lax.all_to_all(copies, axes, 0, 0)

    def spread(value, copies):
        return jnp.broadcast_to(value[None], (copies,) + value.shape)

    cache = neighbour(features, TM, 1)
    later = neighbour(cotangent, TM, -1)

    def edge(cell_row, cot_row):
        feature = jnp.concatenate([cache[:, cell_row], features[:, cell_row]], 0)
        pair = [jnp.concatenate([cotangent[:, k], later[:, k]], 0) for k in (cot_row, cot_row + 1)]
        return jnp.concatenate([feature, jnp.concatenate(pair, -1)], 1)

    above = neighbour(edge(-1, rows - 2), HEIGHT, 1)
    below = neighbour(edge(0, 0), HEIGHT, -1)
    pre_norm, sums = conv_one(cache, features, above, below, weight_one, height)
    came = exchange(sums, HEIGHT)
    grad_hidden, shifted_cot = hidden_grads(cotangent, later, above, below, weight_two)
    sums, grad_hidden, shifted_cot = barrier((came.sum(0), grad_hidden, shifted_cot))
    came = exchange(spread(sums, lax.axis_size(TM)), TM)
    pair, others = ("y", "c"), ("zh", "zl", "x")
    hidden, grad_normed, normed, rstd, sums = middle(
        count, where, came, pre_norm, grad_hidden, norm_gain, norm_shift, lax.axis_size(pair)
    )
    sums, hidden = barrier((sums, hidden))
    sums = exchange(sums, pair).sum(0)
    local_two = second_weight(hidden, shifted_cot)
    before = neighbour(hidden, TM, 1)
    sums, local_two, before = barrier((sums, local_two, before))
    came = exchange(spread(sums, lax.axis_size(others)), others)
    decoded = conv(
        jnp.pad(jnp.concatenate([before, hidden], 0), ((0, 0), (0, 0), (1, 1), (0, 0))), weight_two
    ).astype(jnp.bfloat16)
    came, decoded = barrier((came, decoded))

    scale = 1.0 / cells**0.5
    grad_pre, away, kept = weight_grads(
        count, where, cache, features, above, below, came, grad_normed, normed, rstd, local_two, half_rows(ins, mids)
    )

    part = kept + lax.ppermute(away, "c", SWAP).astype(jnp.float32)
    part = part.astype(jnp.bfloat16).reshape(xs, -1, 128)
    part, grad_pre = barrier((part, grad_pre))
    part = exchange(part, "x").astype(jnp.float32).sum(0)
    after = neighbour(grad_pre, TM, -1)
    part, after = barrier((part, after))
    part = exchange(part.reshape(rest, -1, 128), REST).sum(0).astype(jnp.bfloat16)
    grad_features = feature_grads(jnp.concatenate([grad_pre, after], 0), weight_one, features.shape)
    part, grad_features = barrier((part, grad_features))
    part = exchange(spread(part, rest), REST).reshape(-1, 128)
    part = exchange(spread(part, xs), "x").reshape(-1, 128)
    grad_one, grad_two = unpack(where, part, lax.ppermute(part, "c", SWAP), ins, mids, scale)
    return decoded, grad_features, grad_one.reshape(weight_one.shape), grad_two.reshape(weight_two.shape)


def solution(mesh):
    split = P(TM, HEIGHT, None, None)
    return jax.shard_map(
        body,
        mesh=fine_mesh(mesh),
        in_specs=(split, split, P(), P(), P(), P()),
        out_specs=(split, split, P(), P()),
        check_vma=False,
    )
```

```python
import functools

import jax
import jax.numpy as jnp
from jax import lax
from jax.experimental import pallas as pl
from jax.experimental.pallas import tpu as pltpu
from jax.sharding import Mesh
from jax.sharding import PartitionSpec as P

GROUPS = 32
EPSILON = 1e-05

TM = ("zh", "y")
HEIGHT = ("zl", "x", "c")
REST = ("zh", "y", "zl")

VMEM_LIMIT = 32 * 2**20


def fine_mesh(mesh):
    tm, height = mesh.shape["tm"], mesh.shape["height"]
    zh = 2 if tm % 2 == 0 else 1
    core = 2
    x = 4 if height % 8 == 0 else height // 2
    return Mesh(mesh.devices.reshape(zh, tm // zh, height // (core * x), x, core), TM + HEIGHT)


def neighbour(value, axis, steps):
    count = lax.axis_size(axis)
    first, last = max(0, -steps), min(count, count - steps)
    return lax.ppermute(value, axis, [(i, i + steps) for i in range(first, last)])


def conv(padded, weight):
    return lax.conv_general_dilated(
        padded[None],
        weight,
        (1, 1, 1),
        "VALID",
        dimension_numbers=("NDHWC", "DHWIO", "NDHWC"),
        preferred_element_type=jnp.float32,
    )[0]


def whole(count=1, space=pltpu.VMEM):
    return [pl.BlockSpec(memory_space=space)] * count


def group_sums(first, second, outs):
    member = lax.broadcasted_iota(jnp.int32, (2, outs, outs), 1) // (outs // GROUPS)
    other = lax.broadcasted_iota(jnp.int32, (2, outs, outs), 2) // (outs // GROUPS)
    same = (member[0] == other[0]).astype(jnp.float32)
    both = jnp.concatenate([first, second, jnp.zeros((6, outs), jnp.float32)], 0)
    return jnp.dot(both, same, precision=lax.Precision.HIGHEST, preferred_element_type=jnp.float32)[:2]


def cell_sums(field):
    return jnp.sum(field.reshape(-1, field.shape[-1]), 0, keepdims=True)


def inside(where, field):
    row = lax.broadcasted_iota(jnp.int32, field.shape, 1)
    last = field.shape[1] - 1
    out = ((row == 0) & (where[1] == 1)) | ((row == last) & (where[2] == 1))
    return jnp.where(out, 0.0, field)


def edges_kernel(cache, features, cot, later, downward, upward):
    cells, rows = features.shape[1], cot.shape[1]
    half = features.shape[2]
    for out, cell, row in ((downward, cells - 1, rows - 2), (upward, 0, 0)):
        out[:, :half] = jnp.concatenate([cache[:, cell], features[:, cell]], 0)
        pair = [jnp.concatenate([cot[:, k], later[:, k]], 0) for k in (row, row + 1)]
        out[:, half:] = jnp.concatenate(pair, 2)


def edges(cache, features, cot, later):
    frames, _, half, ins = features.shape
    shape = jax.ShapeDtypeStruct((2 * frames, half + cot.shape[2], ins), jnp.bfloat16)
    return pl.pallas_call(
        edges_kernel,
        out_shape=(shape, shape),
        in_specs=whole(4),
        out_specs=whole(2),
        compiler_params=pltpu.CompilerParams(vmem_limit_bytes=VMEM_LIMIT),
        name="edges",
    )(cache, features, cot, later)


def relay_kernel(came, out):
    out[...] = jnp.broadcast_to(jnp.sum(came[...], 0, keepdims=True), out.shape)


def relay(came, copies):
    return pl.pallas_call(
        relay_kernel,
        out_shape=jax.ShapeDtypeStruct((copies,) + came.shape[1:], came.dtype),
        in_specs=whole(1),
        out_specs=whole()[0],
        name="relay",
    )(came)


def conv_one_kernel(cache, features, above, below, weight, pre_norm, sums, wide):
    frames, rows, cols, outs = pre_norm.shape
    cells_in, half, ins = features.shape[1], cols // 2, features.shape[-1]
    timed = jnp.concatenate([cache[...], features[...]], 0)
    rowed = jnp.concatenate([above[:, :half][:, None], timed, below[:, :half][:, None]], 1)
    by_tap = []
    for e in range(3):
        total = jnp.zeros((frames, rows, half, outs), jnp.float32)
        for b in range(3):
            product = sum(
                jnp.dot(
                    rowed[a : a + frames].reshape(-1, ins),
                    weight[a, b, e],
                    preferred_element_type=jnp.float32,
                )
                for a in range(3)
            ).reshape(frames, cells_in + 2, half, outs)
            total += jnp.stack([product[:, (r + b) // 2] for r in range(rows)], 1)
        by_tap.append(total.reshape(frames * rows, half, outs))
    wide[...] = jnp.zeros_like(wide)
    wide[:, 8 : 8 + half, :outs] = by_tap[0]
    even = wide[:, 7 : 7 + half, :outs] + by_tap[1] + by_tap[2]
    wide[:, 8 : 8 + half, :outs] = by_tap[2]
    odd = by_tap[0] + by_tap[1] + wide[:, 9 : 9 + half, :outs]
    wide[:, pl.ds(0, half, stride=2), :outs] = even
    wide[:, pl.ds(1, half, stride=2), :outs] = odd
    pre = wide[:, :cols, :outs].reshape(pre_norm.shape)
    pre_norm[...] = pre
    own = pre[:, 1:-1]
    both = group_sums(cell_sums(own), cell_sums(own * own), outs)
    sums[...] = jnp.broadcast_to(both[None], sums.shape)


def conv_one(cache, features, above, below, weight, copies):
    frames, cells_in, half, _ = features.shape
    outs = weight.shape[-1]
    rows, cols = 2 * cells_in + 2, 2 * half
    return pl.pallas_call(
        conv_one_kernel,
        out_shape=(
            jax.ShapeDtypeStruct((frames, rows, cols, outs), jnp.float32),
            jax.ShapeDtypeStruct((copies, 2, outs), jnp.float32),
        ),
        in_specs=whole(5),
        out_specs=whole(2),
        scratch_shapes=[pltpu.VMEM((frames * rows, cols + 16, 128), jnp.float32)],
        compiler_params=pltpu.CompilerParams(vmem_limit_bytes=VMEM_LIMIT),
        name="conv_one",
    )(cache, features, above, below, weight)


def grad_hidden_kernel(cot, later, above, below, weight, grad_hidden, shifted, wide):
    frames, rows, cols, ins = grad_hidden.shape
    outs = cot.shape[-1]
    half = cols // 2
    timed = jnp.concatenate([cot[...], later[...]], 0)
    pair = lambda part: jnp.stack([part[:, half:, :outs], part[:, half:, outs:]], 1)
    rowed = jnp.concatenate([pair(above), timed, pair(below)], 1).astype(jnp.float32)
    wide[...] = jnp.zeros_like(wide)
    wide[:, 8 : 8 + cols, :outs] = rowed.reshape(-1, cols, outs)
    total = jnp.zeros((frames * rows * cols, ins), jnp.float32)
    for e in range(3):
        part = wide[:, 9 - e : 9 - e + cols, :outs].astype(jnp.bfloat16)
        part = part.reshape(2 * frames, rows + 2, cols, outs)
        shifted[e] = part
        for a in range(3):
            for b in range(3):
                total += lax.dot_general(
                    part[2 - a : 2 - a + frames, 2 - b : 2 - b + rows].reshape(-1, outs),
                    weight[a, b, e],
                    (((1,), (1,)), ((), ())),
                    preferred_element_type=jnp.float32,
                )
    grad_hidden[...] = total.reshape(grad_hidden.shape)


def hidden_grads(cot, later, above, below, weight):
    frames, rows, cols, outs = cot.shape
    return pl.pallas_call(
        grad_hidden_kernel,
        out_shape=(
            jax.ShapeDtypeStruct((frames, rows + 2, cols, weight.shape[-2]), jnp.float32),
            jax.ShapeDtypeStruct((3, 2 * frames, rows + 4, cols, outs), jnp.bfloat16),
        ),
        in_specs=whole(5),
        out_specs=whole(2),
        scratch_shapes=[pltpu.VMEM((2 * frames * (rows + 4), cols + 16, 128), jnp.float32)],
        compiler_params=pltpu.CompilerParams(vmem_limit_bytes=VMEM_LIMIT),
        cost_estimate=pl.CostEstimate(flops=2**30, bytes_accessed=2**21, transcendentals=0),
        name="grad_hidden",
    )(cot, later, above, below, weight)


def middle_kernel(count, where, came, pre_norm, grad_hidden, gain, shift, hidden, grad_normed, normed, rstd, sums):
    outs = pre_norm.shape[-1]
    total = jnp.sum(came[...], 0)
    mean = total[:1] / count
    scaled = lax.rsqrt(total[1:2] / count - mean * mean + EPSILON)
    rstd[...] = scaled
    flat = (pre_norm[...].reshape(-1, outs) - mean) * scaled
    shifted = flat * gain[...] + shift[...]
    sigma = 1.0 / (1.0 + jnp.exp(-shifted))
    hidden[...] = inside(where, (shifted * sigma).reshape(pre_norm.shape)).astype(jnp.bfloat16)
    grad = grad_hidden[...].reshape(-1, outs) * sigma * (1.0 + shifted * (1.0 - sigma)) * gain[...]
    grad, flat = grad.reshape(pre_norm.shape), flat.reshape(pre_norm.shape)
    grad_normed[...] = grad
    normed[...] = flat
    own = grad[:, 1:-1]
    both = group_sums(cell_sums(own), cell_sums(own * flat[:, 1:-1]), outs)
    sums[...] = jnp.broadcast_to(both[None], sums.shape)


def middle(count, where, came, pre_norm, grad_hidden, gain, shift, copies):
    shape, outs = pre_norm.shape, pre_norm.shape[-1]
    return pl.pallas_call(
        functools.partial(middle_kernel, count),
        out_shape=(
            jax.ShapeDtypeStruct(shape, jnp.bfloat16),
            jax.ShapeDtypeStruct(shape, jnp.float32),
            jax.ShapeDtypeStruct(shape, jnp.float32),
            jax.ShapeDtypeStruct((1, outs), jnp.float32),
            jax.ShapeDtypeStruct((copies, 2, outs), jnp.float32),
        ),
        in_specs=whole(1, pltpu.SMEM) + whole(5),
        out_specs=whole(5),
        compiler_params=pltpu.CompilerParams(vmem_limit_bytes=VMEM_LIMIT),
        name="middle",
    )(where, came, pre_norm, grad_hidden, gain[None], shift[None])


def second_weight_kernel(hidden, shifted, out):
    frames, rows, cols, ins = hidden.shape
    outs = shifted.shape[-1]
    own = hidden[:, 1:-1].reshape(-1, ins).astype(jnp.float32).T.astype(jnp.bfloat16)
    for a in range(3):
        pieces = [
            shifted[e, 2 - a : 2 - a + frames, 3 - b : 3 - b + rows - 2].reshape(-1, outs)
            for b in range(3)
            for e in range(3)
        ]
        pieces.append(jnp.zeros((pieces[0].shape[0], 32), jnp.bfloat16))
        out[a] = jnp.dot(own, jnp.concatenate(pieces, 1), preferred_element_type=jnp.float32)


def second_weight(hidden, shifted):
    return pl.pallas_call(
        second_weight_kernel,
        out_shape=jax.ShapeDtypeStruct((3, hidden.shape[-1], 896), jnp.float32),
        in_specs=whole(2),
        out_specs=whole()[0],
        compiler_params=pltpu.CompilerParams(vmem_limit_bytes=VMEM_LIMIT),
        cost_estimate=pl.CostEstimate(flops=2**29, bytes_accessed=2**21, transcendentals=0),
        name="second_weight",
    )(hidden, shifted)


def col_sums(wide, cells):
    half = cells.shape[1] // 2
    wide[...] = jnp.zeros_like(wide)
    wide[:, 8 : 8 + cells.shape[1], : cells.shape[2]] = cells

    def every_second(start):
        return wide[:, pl.ds(start, half, stride=2), : cells.shape[2]]

    before, even, odd, after = (every_second(7 + k) for k in range(4))
    return odd + after, even + odd, before + even


def weight_grads_kernel(
    count, where, cache, features, above, below, came, grad_normed, normed, rstd, two, grad_pre, away, kept, wide
):
    frames, rows, cols, outs = grad_normed.shape
    ins, mids = features.shape[-1], two.shape[1]
    total = jnp.sum(came[...], 0) / count
    timed = jnp.concatenate([cache[...], features[...]], 0)
    rows_in = jnp.concatenate([above[:, : cols // 2][:, None], timed, below[:, : cols // 2][:, None]], 1)
    merged = (frames * rows * cols, outs)
    grad = grad_normed[...].reshape(merged) - total[:1] - normed[...].reshape(merged) * total[1:2]
    grad = inside(where, (grad * rstd[...]).reshape(grad_normed.shape)).astype(jnp.bfloat16)
    grad_pre[...] = grad
    grad = grad[:, 1:-1].astype(jnp.float32)
    rows = rows - 2
    by_tap = col_sums(wide, grad.reshape(frames * rows, cols, outs))
    pieces = []
    for b in range(3):
        for e in range(3):
            part = by_tap[e].reshape(frames, rows, cols // 2, outs)
            none = jnp.zeros_like(part[:, 0])
            r = [part[:, k] for k in range(rows)]
            stacked = (
                [r[0], r[1] + r[2], r[3], none],
                [none, r[0] + r[1], r[2] + r[3], none],
                [none, r[0], r[1] + r[2], r[3]],
            )[b]
            cells = jnp.stack(stacked, 1).astype(jnp.bfloat16)
            pieces.append(cells.reshape(-1, outs))
    pieces.append(jnp.zeros((pieces[0].shape[0], 32), jnp.bfloat16))
    cells = jnp.concatenate(pieces, 1)
    lower = where[0] == 0

    def write(at, low, high):
        away[at : at + low.shape[0]] = jnp.where(lower, high, low).astype(jnp.bfloat16)
        kept[at : at + low.shape[0]] = jnp.where(lower, low, high)

    at = 0
    for a in range(3):
        product = lax.dot_general(
            rows_in[a : a + frames].reshape(-1, ins),
            cells,
            (((0,), (0,)), ((), ())),
            preferred_element_type=jnp.float32,
        )
        for j in range(7):
            block = product[:, 128 * j : 128 * j + 128]
            write(at, block[: ins // 2], block[ins // 2 :])
            at += ins // 2
    for a in range(3):
        product = two[a]
        for j in range(7):
            block = product[:, 128 * j : 128 * j + 128]
            write(at, block[: mids // 2], block[mids // 2 :])
            at += mids // 2
    if at < kept.shape[0]:
        tail = jnp.zeros((kept.shape[0] - at, 128), jnp.float32)
        away[at:] = tail.astype(jnp.bfloat16)
        kept[at:] = tail


def weight_grads(count, where, cache, features, above, below, came, grad_normed, normed, rstd, two, half_rows):
    frames, rows, cols, outs = grad_normed.shape
    return pl.pallas_call(
        functools.partial(weight_grads_kernel, count),
        out_shape=(
            jax.ShapeDtypeStruct(grad_normed.shape, jnp.bfloat16),
            jax.ShapeDtypeStruct((half_rows, 128), jnp.bfloat16),
            jax.ShapeDtypeStruct((half_rows, 128), jnp.float32),
        ),
        in_specs=whole(1, pltpu.SMEM) + whole(9),
        out_specs=whole(3),
        scratch_shapes=[pltpu.VMEM((frames * (rows - 2), cols + 16, 128), jnp.float32)],
        compiler_params=pltpu.CompilerParams(vmem_limit_bytes=VMEM_LIMIT),
        name="weight_grads",
    )(where, cache, features, above, below, came, grad_normed, normed, rstd, two)


def unpack_kernel(scale, half, part_one, part_two, *rest):
    one, two = rest[-2:]
    for part, out in ((part_one, one), (part_two, two)):
        taps, rows, outs = out.shape
        lanes = jnp.concatenate([part[rows * j : rows * j + rows] for j in range(7)], 1)
        lanes = lanes.astype(jnp.float32) * scale
        for k in range(taps):
            out[k] = lanes[:, outs * k : outs * k + outs]


def unpack(half, part, ins, mids, scale, begun=()):
    half_one, half_two = 7 * ins // 2, 7 * mids // 2
    skip = 3 * half_one // half_two
    return pl.pallas_call(
        functools.partial(unpack_kernel, scale),
        grid_spec=pltpu.PrefetchScalarGridSpec(
            num_scalar_prefetch=1,
            grid=(3,),
            in_specs=[
                pl.BlockSpec((half_one, 128), lambda a, half: (a, 0)),
                pl.BlockSpec((half_two, 128), lambda a, half: (a + skip, 0)),
            ]
            + whole(len(begun), pl.ANY),
            out_specs=[
                pl.BlockSpec((9, ins // 2, mids), lambda a, half: (a, half[0], 0)),
                pl.BlockSpec((9, mids // 2, mids), lambda a, half: (a, half[0], 0)),
            ],
        ),
        out_shape=(
            jax.ShapeDtypeStruct((27, ins, mids), jnp.float32),
            jax.ShapeDtypeStruct((27, mids, mids), jnp.float32),
        ),
        input_output_aliases={3 + k: k for k in range(len(begun))},
        compiler_params=pltpu.CompilerParams(vmem_limit_bytes=VMEM_LIMIT),
        cost_estimate=pl.CostEstimate(flops=2**20, bytes_accessed=2**22, transcendentals=0),
        name="unpack",
    )(half, part, part, *begun)


def feature_grads_kernel(grad_pre, weight, out, wide):
    frames, rows, cols, outs = grad_pre.shape
    own, cells_in, cols_in, ins = out.shape
    by_tap = col_sums(wide, grad_pre[...].astype(jnp.float32).reshape(frames * rows, cols, outs))
    total = jnp.zeros((own * cells_in * cols_in, ins), jnp.float32)
    for b in range(3):
        for e in range(3):
            part = by_tap[e].reshape(frames, rows, cols // 2, outs)
            cells = jnp.stack(
                [part[:, 2 * k + 2 - b] + part[:, 2 * k + 3 - b] for k in range(cells_in)], 1
            ).astype(jnp.bfloat16)
            for a in range(3):
                total += lax.dot_general(
                    cells[2 - a : 2 - a + own].reshape(-1, outs),
                    weight[a, b, e],
                    (((1,), (1,)), ((), ())),
                    preferred_element_type=jnp.float32,
                )
    out[...] = total.reshape(out.shape)


def feature_grads(grad_rowed, weight, shape):
    frames, rows, cols, _ = grad_rowed.shape
    return pl.pallas_call(
        feature_grads_kernel,
        out_shape=jax.ShapeDtypeStruct(shape, jnp.float32),
        in_specs=whole(2),
        out_specs=whole()[0],
        scratch_shapes=[pltpu.VMEM((frames * rows, cols + 16, 128), jnp.float32)],
        compiler_params=pltpu.CompilerParams(vmem_limit_bytes=VMEM_LIMIT),
        cost_estimate=pl.CostEstimate(flops=2**28, bytes_accessed=2**21, transcendentals=0),
        name="feature_grads",
    )(grad_rowed, weight)


def half_rows(ins, mids):
    unit = lax.axis_size("x") * lax.axis_size(REST)
    return -(-(21 * (ins + mids) // 2) // unit) * unit


SWAP = [(0, 1), (1, 0)]


def body(features, cotangent, weight_one, weight_two, norm_gain, norm_shift):
    frames, ins = features.shape[0], features.shape[-1]
    rows, cols, mids = cotangent.shape[1:]
    xs, rest, height = lax.axis_size("x"), lax.axis_size(REST), lax.axis_size(HEIGHT)
    cells = frames * rows * cols * 2 * xs * rest
    count = cells * (mids // GROUPS)
    at_row = lax.axis_index(HEIGHT)
    where = jnp.stack([lax.axis_index("c"), at_row == 0, at_row == height - 1]).astype(jnp.int32)
    barrier = lax.optimization_barrier

    def exchange(copies, axes):
        return lax.all_to_all(copies, axes, 0, 0)

    def spread(value, copies):
        return jnp.broadcast_to(value[None], (copies,) + value.shape)

    cache = neighbour(features, TM, 1)
    later = neighbour(cotangent, TM, -1)

    downward, upward = edges(cache, features, cotangent, later)
    above = neighbour(downward, HEIGHT, 1)
    below = neighbour(upward, HEIGHT, -1)
    pre_norm, sums = conv_one(cache, features, above, below, weight_one, height)
    came = exchange(sums, HEIGHT)
    grad_hidden, shifted_cot = hidden_grads(cotangent, later, above, below, weight_two)
    came, grad_hidden, shifted_cot = barrier((came, grad_hidden, shifted_cot))
    came = exchange(relay(came, lax.axis_size(TM)), TM)
    pair, others = ("y", "c"), ("zh", "zl", "x")
    hidden, grad_normed, normed, rstd, sums = middle(
        count, where, came, pre_norm, grad_hidden, norm_gain, norm_shift, lax.axis_size(pair)
    )
    sums, hidden = barrier((sums, hidden))
    came = exchange(sums, pair)
    local_two = second_weight(hidden, shifted_cot)
    before = neighbour(hidden, TM, 1)
    came, local_two, before = barrier((came, local_two, before))
    came = exchange(relay(came, lax.axis_size(others)), others)
    decoded = conv(
        jnp.pad(jnp.concatenate([before, hidden], 0), ((0, 0), (0, 0), (1, 1), (0, 0))), weight_two
    ).astype(jnp.bfloat16)
    came, decoded = barrier((came, decoded))

    scale = 1.0 / cells**0.5
    grad_pre, away, kept = weight_grads(
        count, where, cache, features, above, below, came, grad_normed, normed, rstd, local_two, half_rows(ins, mids)
    )

    part = kept + lax.ppermute(away, "c", SWAP).astype(jnp.float32)
    part = part.astype(jnp.bfloat16).reshape(xs, -1, 128)
    part, grad_pre = barrier((part, grad_pre))
    part = exchange(part, "x").astype(jnp.float32).sum(0).astype(jnp.bfloat16)
    after = neighbour(grad_pre, TM, -1)
    part, after = barrier((part, after))
    part = exchange(part.reshape(rest, -1, 128), REST).astype(jnp.float32).sum(0).astype(jnp.bfloat16)
    grad_features = feature_grads(jnp.concatenate([grad_pre, after], 0), weight_one, features.shape)
    part, grad_features = barrier((part, grad_features))
    part = exchange(spread(part, rest), REST).reshape(-1, 128)
    part = exchange(spread(part, xs), "x").reshape(-1, 128)
    other = lax.ppermute(part, "c", SWAP)
    core = where[:1]
    begun = unpack(core, part, ins, mids, scale)
    grad_one, grad_two = unpack(1 - core, other, ins, mids, scale, begun)
    return decoded, grad_features, grad_one.reshape(weight_one.shape), grad_two.reshape(weight_two.shape)


def solution(mesh):
    split = P(TM, HEIGHT, None, None)
    return jax.shard_map(
        body,
        mesh=fine_mesh(mesh),
        in_specs=(split, split, P(), P(), P(), P()),
        out_specs=(split, split, P(), P()),
        check_vma=False,
    )
```

```python
import functools

import jax
import jax.numpy as jnp
from jax import lax
from jax.experimental import pallas as pl
from jax.experimental.pallas import tpu as pltpu
from jax.sharding import Mesh
from jax.sharding import PartitionSpec as P

GROUPS = 32
EPSILON = 1e-05

TM = ("zh", "y")
HEIGHT = ("zl", "x", "c")
REST = ("zh", "y", "zl")

VMEM_LIMIT = 32 * 2**20


def fine_mesh(mesh):
    tm, height = mesh.shape["tm"], mesh.shape["height"]
    zh = 2 if tm % 2 == 0 else 1
    core = 2
    x = 4 if height % 8 == 0 else height // 2
    return Mesh(mesh.devices.reshape(zh, tm // zh, height // (core * x), x, core), TM + HEIGHT)


def neighbour(value, axis, steps):
    count = lax.axis_size(axis)
    first, last = max(0, -steps), min(count, count - steps)
    return lax.ppermute(value, axis, [(i, i + steps) for i in range(first, last)])


def conv(padded, weight):
    return lax.conv_general_dilated(
        padded[None],
        weight,
        (1, 1, 1),
        "VALID",
        dimension_numbers=("NDHWC", "DHWIO", "NDHWC"),
        preferred_element_type=jnp.float32,
    )[0]


def whole(count=1, space=pltpu.VMEM):
    return [pl.BlockSpec(memory_space=space)] * count


def group_sums(first, second, outs):
    member = lax.broadcasted_iota(jnp.int32, (2, outs, outs), 1) // (outs // GROUPS)
    other = lax.broadcasted_iota(jnp.int32, (2, outs, outs), 2) // (outs // GROUPS)
    same = (member[0] == other[0]).astype(jnp.float32)
    both = jnp.concatenate([first, second, jnp.zeros((6, outs), jnp.float32)], 0)
    return jnp.dot(both, same, precision=lax.Precision.HIGHEST, preferred_element_type=jnp.float32)[:2]


def cell_sums(field):
    return jnp.sum(field.reshape(-1, field.shape[-1]), 0, keepdims=True)


def inside(where, field):
    row = lax.broadcasted_iota(jnp.int32, field.shape, 1)
    last = field.shape[1] - 1
    out = ((row == 0) & (where[1] == 1)) | ((row == last) & (where[2] == 1))
    return jnp.where(out, 0.0, field)


def edges_kernel(cache, features, cot, later, downward, upward):
    cells, rows = features.shape[1], cot.shape[1]
    half = features.shape[2]
    for out, cell, row in ((downward, cells - 1, rows - 2), (upward, 0, 0)):
        out[:, :half] = jnp.concatenate([cache[:, cell], features[:, cell]], 0)
        pair = [jnp.concatenate([cot[:, k], later[:, k]], 0) for k in (row, row + 1)]
        out[:, half:] = jnp.concatenate(pair, 2)


def edges(cache, features, cot, later):
    frames, _, half, ins = features.shape
    shape = jax.ShapeDtypeStruct((2 * frames, half + cot.shape[2], ins), jnp.bfloat16)
    return pl.pallas_call(
        edges_kernel,
        out_shape=(shape, shape),
        in_specs=whole(4),
        out_specs=whole(2),
        compiler_params=pltpu.CompilerParams(vmem_limit_bytes=VMEM_LIMIT),
        name="edges",
    )(cache, features, cot, later)


def conv_one_kernel(cache, features, above, below, weight, cot, pre_norm, sums, wide):
    frames, rows, cols, outs = pre_norm.shape
    cells_in, half, ins = features.shape[1], cols // 2, features.shape[-1]
    timed = jnp.concatenate([cache[...], features[...]], 0)
    rowed = jnp.concatenate([above[:, :half][:, None], timed, below[:, :half][:, None]], 1)
    by_tap = []
    for e in range(3):
        total = jnp.zeros((frames, rows, half, outs), jnp.float32)
        for b in range(3):
            product = sum(
                jnp.dot(
                    rowed[a : a + frames].reshape(-1, ins),
                    weight[a, b, e],
                    preferred_element_type=jnp.float32,
                )
                for a in range(3)
            ).reshape(frames, cells_in + 2, half, outs)
            total += jnp.stack([product[:, (r + b) // 2] for r in range(rows)], 1)
        by_tap.append(total.reshape(frames * rows, half, outs))
    wide[...] = jnp.zeros_like(wide)
    wide[:, 8 : 8 + half, :outs] = by_tap[0]
    even = wide[:, 7 : 7 + half, :outs] + by_tap[1] + by_tap[2]
    wide[:, 8 : 8 + half, :outs] = by_tap[2]
    odd = by_tap[0] + by_tap[1] + wide[:, 9 : 9 + half, :outs]
    wide[:, pl.ds(0, half, stride=2), :outs] = even
    wide[:, pl.ds(1, half, stride=2), :outs] = odd
    pre = wide[:, :cols, :outs].reshape(pre_norm.shape)
    pre_norm[...] = pre
    own = pre[:, 1:-1]
    both = group_sums(cell_sums(own), cell_sums(own * own), outs)
    both = jnp.concatenate([both, cell_sums(cot[...].astype(jnp.float32)), jnp.zeros((1, outs), jnp.float32)], 0)
    sums[...] = jnp.broadcast_to(both[None], sums.shape)


def conv_one(cache, features, above, below, weight, cot, copies):
    frames, cells_in, half, _ = features.shape
    outs = weight.shape[-1]
    rows, cols = 2 * cells_in + 2, 2 * half
    return pl.pallas_call(
        conv_one_kernel,
        out_shape=(
            jax.ShapeDtypeStruct((frames, rows, cols, outs), jnp.float32),
            jax.ShapeDtypeStruct((copies, 4, outs), jnp.float32),
        ),
        in_specs=whole(6),
        out_specs=whole(2),
        scratch_shapes=[pltpu.VMEM((frames * rows, cols + 16, 128), jnp.float32)],
        compiler_params=pltpu.CompilerParams(vmem_limit_bytes=VMEM_LIMIT),
        name="conv_one",
    )(cache, features, above, below, weight, cot)


def grad_hidden_kernel(cot, later, above, below, weight, grad_hidden, shifted, all_taps, wide):
    frames, rows, cols, ins = grad_hidden.shape
    outs = cot.shape[-1]
    half = cols // 2
    timed = jnp.concatenate([cot[...], later[...]], 0)
    pair = lambda part: jnp.stack([part[:, half:, :outs], part[:, half:, outs:]], 1)
    rowed = jnp.concatenate([pair(above), timed, pair(below)], 1).astype(jnp.float32)
    wide[...] = jnp.zeros_like(wide)
    wide[:, 8 : 8 + cols, :outs] = rowed.reshape(-1, cols, outs)
    total = jnp.zeros((frames * rows * cols, ins), jnp.float32)
    for e in range(3):
        part = wide[:, 9 - e : 9 - e + cols, :outs].astype(jnp.bfloat16)
        part = part.reshape(2 * frames, rows + 2, cols, outs)
        shifted[e] = part
        for a in range(3):
            for b in range(3):
                total += lax.dot_general(
                    part[2 - a : 2 - a + frames, 2 - b : 2 - b + rows].reshape(-1, outs),
                    weight[a, b, e],
                    (((1,), (1,)), ((), ())),
                    preferred_element_type=jnp.float32,
                )
    grad_hidden[...] = total.reshape(grad_hidden.shape)
    all_taps[...] = sum(
        weight[a, b, e].astype(jnp.float32) for a in range(3) for b in range(3) for e in range(3)
    )


def hidden_grads(cot, later, above, below, weight):
    frames, rows, cols, outs = cot.shape
    return pl.pallas_call(
        grad_hidden_kernel,
        out_shape=(
            jax.ShapeDtypeStruct((frames, rows + 2, cols, weight.shape[-2]), jnp.float32),
            jax.ShapeDtypeStruct((3, 2 * frames, rows + 4, cols, outs), jnp.bfloat16),
            jax.ShapeDtypeStruct(weight.shape[-2:], jnp.float32),
        ),
        in_specs=whole(5),
        out_specs=whole(3),
        scratch_shapes=[pltpu.VMEM((2 * frames * (rows + 4), cols + 16, 128), jnp.float32)],
        compiler_params=pltpu.CompilerParams(vmem_limit_bytes=VMEM_LIMIT),
        cost_estimate=pl.CostEstimate(flops=2**30, bytes_accessed=2**21, transcendentals=0),
        name="grad_hidden",
    )(cot, later, above, below, weight)


def middle_kernel(count, where, came, pre_norm, grad_hidden, all_taps, gain, shift, hidden, grad_normed, normed, vectors):
    outs = pre_norm.shape[-1]
    total = jnp.sum(came[...], 0)
    mean = total[:1] / count
    scaled = lax.rsqrt(total[1:2] / count - mean * mean + EPSILON)
    flat = (pre_norm[...].reshape(-1, outs) - mean) * scaled
    shifted = flat * gain[...] + shift[...]
    sigma = 1.0 / (1.0 + jnp.exp(-shifted))
    hidden[...] = inside(where, (shifted * sigma).reshape(pre_norm.shape)).astype(jnp.bfloat16)
    grad = grad_hidden[...].reshape(-1, outs) * sigma * (1.0 + shifted * (1.0 - sigma)) * gain[...]
    grad, flat = grad.reshape(pre_norm.shape), flat.reshape(pre_norm.shape)
    grad_normed[...] = grad
    normed[...] = flat
    own = grad[:, 1:-1]

    cells = count / (outs // GROUPS)
    level = lax.dot_general(
        total[2:3] / cells,
        all_taps[...],
        (((1,), (1,)), ((), ())),
        precision=lax.Precision.HIGHEST,
        preferred_element_type=jnp.float32,
    )
    at = lax.broadcasted_iota(jnp.int32, (16, outs), 0).astype(jnp.float32) * 0.45 - 3.375
    share = jnp.exp(-0.5 * at * at)
    share = share / jnp.sum(share, 0, keepdims=True)
    point = at * gain[...] + shift[...]
    slope = 1.0 / (1.0 + jnp.exp(-point))
    slope = slope * (1.0 + point * (1.0 - slope)) * share
    level = level * gain[...] * (cells / count)
    offsets = group_sums(
        level * jnp.sum(slope, 0, keepdims=True), level * jnp.sum(slope * at, 0, keepdims=True), outs
    )
    rows = [scaled, offsets, cell_sums(own), cell_sums(own * flat[:, 1:-1])]
    vectors[...] = jnp.concatenate(rows + [jnp.zeros((3, outs), jnp.float32)], 0)


def middle(count, where, came, pre_norm, grad_hidden, all_taps, gain, shift):
    shape, outs = pre_norm.shape, pre_norm.shape[-1]
    return pl.pallas_call(
        functools.partial(middle_kernel, count),
        out_shape=(
            jax.ShapeDtypeStruct(shape, jnp.bfloat16),
            jax.ShapeDtypeStruct(shape, jnp.float32),
            jax.ShapeDtypeStruct(shape, jnp.float32),
            jax.ShapeDtypeStruct((8, outs), jnp.float32),
        ),
        in_specs=whole(1, pltpu.SMEM) + whole(6),
        out_specs=whole(4),
        compiler_params=pltpu.CompilerParams(vmem_limit_bytes=VMEM_LIMIT),
        name="middle",
    )(where, came, pre_norm, grad_hidden, all_taps, gain[None], shift[None])


def second_weight_kernel(hidden, shifted, out):
    frames, rows, cols, ins = hidden.shape
    outs = shifted.shape[-1]
    own = hidden[:, 1:-1].reshape(-1, ins).astype(jnp.float32).T.astype(jnp.bfloat16)
    for a in range(3):
        pieces = [
            shifted[e, 2 - a : 2 - a + frames, 3 - b : 3 - b + rows - 2].reshape(-1, outs)
            for b in range(3)
            for e in range(3)
        ]
        pieces.append(jnp.zeros((pieces[0].shape[0], 32), jnp.bfloat16))
        out[a] = jnp.dot(own, jnp.concatenate(pieces, 1), preferred_element_type=jnp.float32)


def second_weight(hidden, shifted):
    return pl.pallas_call(
        second_weight_kernel,
        out_shape=jax.ShapeDtypeStruct((3, hidden.shape[-1], 896), jnp.float32),
        in_specs=whole(2),
        out_specs=whole()[0],
        compiler_params=pltpu.CompilerParams(vmem_limit_bytes=VMEM_LIMIT),
        cost_estimate=pl.CostEstimate(flops=2**29, bytes_accessed=2**21, transcendentals=0),
        name="second_weight",
    )(hidden, shifted)


def col_sums(wide, cells):
    half = cells.shape[1] // 2
    wide[...] = jnp.zeros_like(wide)
    wide[:, 8 : 8 + cells.shape[1], : cells.shape[2]] = cells

    def every_second(start):
        return wide[:, pl.ds(start, half, stride=2), : cells.shape[2]]

    before, even, odd, after = (every_second(7 + k) for k in range(4))
    return odd + after, even + odd, before + even


def group_lanes(outs, first):
    lane = lax.broadcasted_iota(jnp.int32, (outs, 128), 1)
    group = lax.broadcasted_iota(jnp.int32, (outs, 128), 0) // (outs // GROUPS)
    return (lane == group + (64 if first else 64 + GROUPS)).astype(jnp.float32)


def exact(left, right, dims):
    return lax.dot_general(
        left, right, (dims, ((), ())), precision=lax.Precision.HIGHEST, preferred_element_type=jnp.float32
    )


def with_sums(tiles, sums):
    high = sums.astype(jnp.bfloat16).astype(jnp.float32)
    middle = (sums - high).astype(jnp.bfloat16).astype(jnp.float32)
    low = sums - high - middle
    row = lax.broadcasted_iota(jnp.int32, (8, 128), 0)
    lane = lax.broadcasted_iota(jnp.int32, (8, 128), 1)
    parts = jnp.where(row == 0, high, jnp.where(row == 1, middle, jnp.where(row == 2, low, 0.0)))
    return jnp.where((lane < 64)[None], tiles, parts[None])


def weight_grads_kernel(where, cache, features, above, below, grad_normed, normed, vectors, two, away, kept, wide):
    frames, rows, cols, outs = grad_normed.shape
    rows, half = rows - 2, cols // 2
    ins, mids, pieces, part_rows = features.shape[-1], two.shape[1], kept.shape[0], kept.shape[2]
    timed = jnp.concatenate([cache[...], features[...]], 0)
    rows_in = jnp.concatenate([above[:, :half][:, None], timed, below[:, :half][:, None]], 1)
    rstd, f0, s0 = (vectors[k : k + 1] for k in range(3))
    own = normed[:, 1:-1].reshape(-1, outs)
    grad = (grad_normed[:, 1:-1].reshape(-1, outs) - f0 - own * s0) * rstd
    lower = where[0] == 0

    def pool(field, last):
        by_tap = col_sums(wide, field.reshape(frames * rows, cols, outs))
        taps = []
        for b in range(3):
            for e in range(3):
                part = by_tap[e].reshape(frames, rows, half, outs)
                none = jnp.zeros_like(part[:, 0])
                r = [part[:, k] for k in range(rows)]
                stacked = (
                    [r[0], r[1] + r[2], r[3], none],
                    [none, r[0] + r[1], r[2] + r[3], none],
                    [none, r[0], r[1] + r[2], r[3]],
                )[b]
                taps.append(jnp.stack(stacked, 1).astype(jnp.bfloat16).reshape(-1, outs))
        return jnp.concatenate(taps + [last], 1)

    at = lax.broadcasted_iota(jnp.int32, (frames * 4 * half, 32), 0)
    tap = lax.broadcasted_iota(jnp.int32, (frames * 4 * half, 32), 1)
    b, e, row, col = tap // 3, tap % 3, at // half % 4, at % half
    two_rows = (row == 1) & (b < 2) | (row == 2) & (b > 0)
    one_row = (row == 0) & (b == 0) | (row == 2) & (b == 0) | (row == 1) & (b == 2) | (row == 3) & (b == 2)
    in_rows = jnp.where(two_rows, 2.0, jnp.where(one_row, 1.0, 0.0))
    in_cols = jnp.where((e == 0) & (col == half - 1) | (e == 2) & (col == 0), 1.0, 2.0)
    counts = jnp.where(tap < 9, in_rows * in_cols, 0.0).astype(jnp.bfloat16)

    def write(part, at, low, high):
        while low.shape[0]:
            x, row = at // part_rows, at % part_rows
            n = min(low.shape[0], part_rows - row)
            away[x, part, row : row + n] = jnp.where(lower, high[:n], low[:n]).astype(jnp.bfloat16)
            kept[x, part, row : row + n] = jnp.where(lower, low[:n], high[:n])
            low, high, at = low[n:], high[n:], at + n

    for part, field, last in ((0, grad, counts), (1, own * rstd, jnp.zeros_like(counts))):
        cells = pool(field, last)
        at = 0
        for a in range(3):
            product = lax.dot_general(
                rows_in[a : a + frames].reshape(-1, ins),
                cells,
                (((0,), (0,)), ((), ())),
                preferred_element_type=jnp.float32,
            )
            for j in range(7):
                block = product[:, 128 * j : 128 * j + 128]
                write(part, at, block[: ins // 2], block[ins // 2 :])
                at += ins // 2
        nothing = jnp.zeros((pieces * part_rows - at, 128), jnp.float32)
        write(part, at, nothing, nothing)

    sums = exact(vectors[3:4], group_lanes(outs, True), ((1,), (0,)))
    sums += exact(vectors[4:5], group_lanes(outs, False), ((1,), (0,)))
    blocks = [two[a, :, 128 * j : 128 * j + 128] for a in range(3) for j in range(7)]
    nothing = [jnp.zeros((pieces * part_rows // 2 - 21 * mids // 2, 128), jnp.float32)]
    halves = [jnp.concatenate([k[i : i + mids // 2] for k in blocks] + nothing, 0) for i in (0, mids // 2)]
    row = lax.broadcasted_iota(jnp.int32, (1, 8, 128), 1)
    tiled = []
    for half_rows in halves:
        tiles = half_rows.reshape(-1, 8, 128)
        turned = jnp.concatenate([tiles[:, 4:], tiles[:, :4]], 1)
        swap = lambda k: jnp.concatenate([k[..., 64:], k[..., :64]], 2)
        even = jnp.where(row < 4, tiles, swap(turned))
        odd = jnp.where(row < 4, turned, swap(tiles))
        tiled.append(with_sums(jnp.stack([even, odd], 1).reshape(-1, 8, 128), sums).reshape(-1, 128))
    write(2, 0, *tiled)


def weight_grads(where, cache, features, above, below, grad_normed, normed, vectors, two, pieces, part_rows):
    frames, rows, cols, _ = grad_normed.shape
    shape = (pieces, 3, part_rows, 128)
    return pl.pallas_call(
        weight_grads_kernel,
        out_shape=(jax.ShapeDtypeStruct(shape, jnp.bfloat16), jax.ShapeDtypeStruct(shape, jnp.float32)),
        in_specs=whole(1, pltpu.SMEM) + whole(8),
        out_specs=whole(2),
        scratch_shapes=[pltpu.VMEM((frames * (rows - 2), cols + 16, 128), jnp.float32)],
        compiler_params=pltpu.CompilerParams(vmem_limit_bytes=VMEM_LIMIT),
        name="weight_grads",
    )(where, cache, features, above, below, grad_normed, normed, vectors, two)


def sums_of(tile):
    return tile[0:1] + tile[1:2] + tile[2:3]


def add_pair_kernel(kept, came, out):
    total = kept[...] + came[...].astype(jnp.float32)
    out[:, :2] = total[:, :2].astype(jnp.bfloat16)
    tiles = total[:, 2].reshape(-1, 8, 128)
    tiles = with_sums(tiles, sums_of(tiles[0]))
    out[:, 2] = tiles.astype(jnp.bfloat16).reshape(out.shape[0], -1, 128)


def add_pair(kept, came):
    return pl.pallas_call(
        add_pair_kernel,
        out_shape=jax.ShapeDtypeStruct(kept.shape, jnp.bfloat16),
        in_specs=whole(2),
        out_specs=whole()[0],
        compiler_params=pltpu.CompilerParams(vmem_limit_bytes=VMEM_LIMIT),
        name="add_pair",
    )(kept, came)


def add_row_kernel(came, out):
    total = jnp.sum(came[...].astype(jnp.float32), 0)
    for part in range(3):
        tiles = total[part].reshape(-1, 8, 128)
        if part == 2:
            tiles = with_sums(tiles, sums_of(tiles[0]))
        out[:, part] = tiles.astype(jnp.bfloat16)


def add_row(came):
    return pl.pallas_call(
        add_row_kernel,
        out_shape=jax.ShapeDtypeStruct((came.shape[2] // 8, 3, 8, 128), jnp.bfloat16),
        in_specs=whole(1),
        out_specs=whole()[0],
        compiler_params=pltpu.CompilerParams(vmem_limit_bytes=VMEM_LIMIT),
        name="add_row",
    )(came)


def combine_kernel(count, tiles_per_block, where, came, vectors, piece, final, lanes):
    outs = vectors.shape[1]
    total = jnp.sum(came[...].astype(jnp.float32), 0)
    sums = sums_of(total[0, 2]) / count
    first = exact(sums, group_lanes(outs, True), ((1,), (1,)))
    second = exact(sums, group_lanes(outs, False), ((1,), (1,)))
    rest = (first - vectors[1:2]) * vectors[0:1]
    final[...] = jnp.concatenate([first, second, rest, jnp.zeros((5, outs), jnp.float32)], 0)
    lane = lax.broadcasted_iota(jnp.int32, (outs, 896), 1)
    channel = lax.broadcasted_iota(jnp.int32, (outs, 896), 0)
    spread = ((lane % outs == channel) & (lane < 9 * outs)).astype(jnp.float32)
    lanes[...] = jnp.broadcast_to(exact(second - vectors[2:3], spread, ((1,), (0,))), lanes.shape)
    for k in range(piece.shape[0]):
        block = (where[3] * piece.shape[0] + k) // tiles_per_block % 7
        change = lanes[0:1, pl.ds(pl.multiple_of(block * 128, 128), 128)]
        upper = jnp.concatenate([total[k, 2, :4, :64], total[k, 2, 4:, :64]], 1)
        grad = total[k, 0] - change * total[k, 1]
        piece[k] = jnp.concatenate([grad, upper], 0).astype(jnp.bfloat16)


def combine(count, ins, where, came, vectors):
    return pl.pallas_call(
        functools.partial(combine_kernel, count, ins // 16),
        out_shape=(
            jax.ShapeDtypeStruct((came.shape[1], 12, 128), jnp.bfloat16),
            jax.ShapeDtypeStruct(vectors.shape, jnp.float32),
        ),
        in_specs=whole(1, pltpu.SMEM) + whole(2),
        out_specs=whole(2),
        scratch_shapes=[pltpu.VMEM((8, 896), jnp.float32)],
        compiler_params=pltpu.CompilerParams(vmem_limit_bytes=VMEM_LIMIT),
        name="combine",
    )(where, came, vectors)


def grad_pre_kernel(where, grad_normed, normed, vectors, final, out):
    shape = grad_normed.shape
    flat = (-1, shape[-1])
    grad = grad_normed[...].reshape(flat) - final[:1] - normed[...].reshape(flat) * final[1:2]
    out[...] = inside(where, (grad * vectors[:1]).reshape(shape)).astype(jnp.bfloat16)


def grad_before_norm(where, grad_normed, normed, vectors, final):
    return pl.pallas_call(
        grad_pre_kernel,
        out_shape=jax.ShapeDtypeStruct(grad_normed.shape, jnp.bfloat16),
        in_specs=whole(1, pltpu.SMEM) + whole(4),
        out_specs=whole()[0],
        compiler_params=pltpu.CompilerParams(vmem_limit_bytes=VMEM_LIMIT),
        cost_estimate=pl.CostEstimate(flops=2**20, bytes_accessed=2**20, transcendentals=0),
        name="grad_pre",
    )(where, grad_normed, normed, vectors, final)


def unpack_kernel(scale, half, part, final, *rest):
    one, two, flat = rest[-3:]
    pieces, rows = part.shape[0], part.shape[1]
    for x in range(pieces):
        flat[rows * 2 // 3 * x : rows * 2 // 3 * (x + 1)] = part[x, : rows * 2 // 3]
        at = pieces * (rows * 2 // 3) + rows // 3 * x
        flat[at : at + rows // 3] = part[x, rows * 2 // 3 :]
    at = 0
    for out in (one, two):
        taps, channels, outs = out.shape
        for a in range(3):
            blocks = [flat[at + channels * j : at + channels * j + channels] for j in range(7)]
            lanes = jnp.concatenate(blocks, 1).astype(jnp.float32) * scale
            for k in range(9):
                grad = lanes[:, outs * k : outs * k + outs]
                if out is one:
                    grad = grad - lanes[:, 9 * outs + k : 9 * outs + k + 1] * final[2:3]
                out[9 * a + k] = grad
            at += 7 * channels
        at = pieces * (rows * 2 // 3)


def unpack(half, part, final, ins, mids, scale, begun=()):
    return pl.pallas_call(
        functools.partial(unpack_kernel, scale),
        grid_spec=pltpu.PrefetchScalarGridSpec(
            num_scalar_prefetch=1,
            grid=(1,),
            in_specs=whole(2) + whole(len(begun), pl.ANY),
            out_specs=[
                pl.BlockSpec((27, ins // 2, mids), lambda a, half: (0, half[0], 0)),
                pl.BlockSpec((27, mids // 2, mids), lambda a, half: (0, half[0], 0)),
            ],
            scratch_shapes=[pltpu.VMEM((part.shape[0] * part.shape[1], 128), jnp.bfloat16)],
        ),
        out_shape=(
            jax.ShapeDtypeStruct((27, ins, mids), jnp.float32),
            jax.ShapeDtypeStruct((27, mids, mids), jnp.float32),
        ),
        input_output_aliases={3 + k: k for k in range(len(begun))},
        compiler_params=pltpu.CompilerParams(vmem_limit_bytes=VMEM_LIMIT),
        cost_estimate=pl.CostEstimate(flops=2**20, bytes_accessed=2**22, transcendentals=0),
        name="unpack",
    )(half, part, final, *begun)


def feature_grads_kernel(grad_pre, weight, out, wide):
    frames, rows, cols, outs = grad_pre.shape
    own, cells_in, cols_in, ins = out.shape
    by_tap = col_sums(wide, grad_pre[...].astype(jnp.float32).reshape(frames * rows, cols, outs))
    total = jnp.zeros((own * cells_in * cols_in, ins), jnp.float32)
    for b in range(3):
        for e in range(3):
            part = by_tap[e].reshape(frames, rows, cols // 2, outs)
            cells = jnp.stack(
                [part[:, 2 * k + 2 - b] + part[:, 2 * k + 3 - b] for k in range(cells_in)], 1
            ).astype(jnp.bfloat16)
            for a in range(3):
                total += lax.dot_general(
                    cells[2 - a : 2 - a + own].reshape(-1, outs),
                    weight[a, b, e],
                    (((1,), (1,)), ((), ())),
                    preferred_element_type=jnp.float32,
                )
    out[...] = total.reshape(out.shape)


def feature_grads(grad_rowed, weight, shape):
    frames, rows, cols, _ = grad_rowed.shape
    return pl.pallas_call(
        feature_grads_kernel,
        out_shape=jax.ShapeDtypeStruct(shape, jnp.float32),
        in_specs=whole(2),
        out_specs=whole()[0],
        scratch_shapes=[pltpu.VMEM((frames * rows, cols + 16, 128), jnp.float32)],
        compiler_params=pltpu.CompilerParams(vmem_limit_bytes=VMEM_LIMIT),
        cost_estimate=pl.CostEstimate(flops=2**28, bytes_accessed=2**21, transcendentals=0),
        name="feature_grads",
    )(grad_rowed, weight)


SWAP = [(0, 1), (1, 0)]


def body(features, cotangent, weight_one, weight_two, norm_gain, norm_shift):
    frames, ins = features.shape[0], features.shape[-1]
    rows, cols, mids = cotangent.shape[1:]
    xs, rest, height = lax.axis_size("x"), lax.axis_size(REST), lax.axis_size(HEIGHT)
    cells = frames * rows * cols * 2 * xs * rest
    count = cells * (mids // GROUPS)
    at_row = lax.axis_index(HEIGHT)
    owned = lax.axis_index("x") * rest + lax.axis_index(REST)
    where = jnp.stack([lax.axis_index("c"), at_row == 0, at_row == height - 1, owned]).astype(jnp.int32)
    barrier = lax.optimization_barrier

    def exchange(copies, axes):
        return lax.all_to_all(copies, axes, 0, 0)

    def spread(value, copies):
        return jnp.broadcast_to(value[None], (copies,) + value.shape)

    cache = neighbour(features, TM, 1)
    later = neighbour(cotangent, TM, -1)

    downward, upward = edges(cache, features, cotangent, later)
    above = neighbour(downward, HEIGHT, 1)
    below = neighbour(upward, HEIGHT, -1)
    pre_norm, sums = conv_one(cache, features, above, below, weight_one, cotangent, height)
    came = exchange(sums, HEIGHT)
    grad_hidden, shifted_cot, all_taps = hidden_grads(cotangent, later, above, below, weight_two)
    sums, grad_hidden, shifted_cot = barrier((came.sum(0), grad_hidden, shifted_cot))
    came = exchange(spread(sums, lax.axis_size(TM)), TM)
    hidden, grad_normed, normed, vectors = middle(
        count, where, came, pre_norm, grad_hidden, all_taps, norm_gain, norm_shift
    )
    local_two = second_weight(hidden, shifted_cot)

    scale = 1.0 / cells**0.5
    part_rows = -(-21 * ins // (2 * 8 * xs * rest)) * 8 * rest
    away, kept = weight_grads(
        where, cache, features, above, below, grad_normed, normed, vectors, local_two, xs, part_rows
    )
    part = add_pair(kept, lax.ppermute(away, "c", SWAP))
    part, hidden = barrier((part, hidden))
    part = add_row(exchange(part, "x"))
    before = neighbour(hidden, TM, 1)
    part, before = barrier((part, before))
    came = exchange(part.reshape(rest, -1, 3, 8, 128), REST)
    decoded = conv(
        jnp.pad(jnp.concatenate([before, hidden], 0), ((0, 0), (0, 0), (1, 1), (0, 0))), weight_two
    ).astype(jnp.bfloat16)
    came, decoded = barrier((came, decoded))
    part, final = combine(count, ins, where, came, vectors)
    grad_pre = grad_before_norm(where, grad_normed, normed, vectors, final)
    part = exchange(spread(part, rest), REST)
    after = neighbour(grad_pre, TM, -1)
    part, after = barrier((part, after))
    part = jnp.concatenate([part[:, :, :8].reshape(-1, 128), part[:, :, 8:].reshape(-1, 128)], 0)
    part = exchange(spread(part, xs), "x")
    grad_features = feature_grads(jnp.concatenate([grad_pre, after], 0), weight_one, features.shape)
    part, grad_features = barrier((part, grad_features))
    other = lax.ppermute(part, "c", SWAP)
    core = where[:1]
    begun = unpack(core, part, final, ins, mids, scale)
    grad_one, grad_two = unpack(1 - core, other, final, ins, mids, scale, begun)
    return decoded, grad_features, grad_one.reshape(weight_one.shape), grad_two.reshape(weight_two.shape)


def solution(mesh):
    split = P(TM, HEIGHT, None, None)
    return jax.shard_map(
        body,
        mesh=fine_mesh(mesh),
        in_specs=(split, split, P(), P(), P(), P()),
        out_specs=(split, split, P(), P()),
        check_vma=False,
    )
```

```python
import functools

import jax
import jax.numpy as jnp
from jax import lax
from jax.experimental import pallas as pl
from jax.experimental.pallas import tpu as pltpu
from jax.sharding import Mesh
from jax.sharding import PartitionSpec as P

GROUPS = 32
EPSILON = 1e-05

TM = ("zh", "y")
HEIGHT = ("zl", "x", "c")
REST = ("zh", "y", "zl")

VMEM_LIMIT = 32 * 2**20


def fine_mesh(mesh):
    tm, height = mesh.shape["tm"], mesh.shape["height"]
    zh = 2 if tm % 2 == 0 else 1
    core = 2
    x = 4 if height % 8 == 0 else height // 2
    return Mesh(mesh.devices.reshape(zh, tm // zh, height // (core * x), x, core), TM + HEIGHT)


def neighbour(value, axis, steps):
    count = lax.axis_size(axis)
    first, last = max(0, -steps), min(count, count - steps)
    return lax.ppermute(value, axis, [(i, i + steps) for i in range(first, last)])


def conv(padded, weight):
    return lax.conv_general_dilated(
        padded[None],
        weight,
        (1, 1, 1),
        "VALID",
        dimension_numbers=("NDHWC", "DHWIO", "NDHWC"),
        preferred_element_type=jnp.float32,
    )[0]


def whole(count=1, space=pltpu.VMEM):
    return [pl.BlockSpec(memory_space=space)] * count


def group_sums(first, second, outs):
    member = lax.broadcasted_iota(jnp.int32, (2, outs, outs), 1) // (outs // GROUPS)
    other = lax.broadcasted_iota(jnp.int32, (2, outs, outs), 2) // (outs // GROUPS)
    same = (member[0] == other[0]).astype(jnp.float32)
    both = jnp.concatenate([first, second, jnp.zeros((6, outs), jnp.float32)], 0)
    return jnp.dot(both, same, precision=lax.Precision.HIGHEST, preferred_element_type=jnp.float32)[:2]


def cell_sums(field):
    return jnp.sum(field.reshape(-1, field.shape[-1]), 0, keepdims=True)


def inside(where, field):
    row = lax.broadcasted_iota(jnp.int32, field.shape, 1)
    last = field.shape[1] - 1
    out = ((row == 0) & (where[1] == 1)) | ((row == last) & (where[2] == 1))
    return jnp.where(out, 0.0, field)


def resident_kernel(*refs):
    sources, copies, sems = refs[:4], refs[4:8], refs[8]
    moves = [pltpu.make_async_copy(sources[k], copies[k], sems.at[k]) for k in range(4)]
    for move in moves:
        move.start()
    for move in moves:
        move.wait()


def resident(*arrays):
    return pl.pallas_call(
        resident_kernel,
        out_shape=[jax.ShapeDtypeStruct(k.shape, k.dtype) for k in arrays],
        in_specs=whole(4, pltpu.HBM),
        out_specs=whole(4),
        scratch_shapes=[pltpu.SemaphoreType.DMA((4,))],
        compiler_params=pltpu.CompilerParams(vmem_limit_bytes=VMEM_LIMIT),
        cost_estimate=pl.CostEstimate(flops=0, bytes_accessed=2**22, transcendentals=0),
        name="resident",
    )(*arrays)


def edges_kernel(cache, features, cot, later, downward, upward):
    cells, rows = features.shape[1], cot.shape[1]
    half = features.shape[2]
    for out, cell, row in ((downward, cells - 1, rows - 2), (upward, 0, 0)):
        out[:, :half] = jnp.concatenate([cache[:, cell], features[:, cell]], 0)
        pair = [jnp.concatenate([cot[:, k], later[:, k]], 0) for k in (row, row + 1)]
        out[:, half:] = jnp.concatenate(pair, 2)


def edges(cache, features, cot, later):
    frames, _, half, ins = features.shape
    shape = jax.ShapeDtypeStruct((2 * frames, half + cot.shape[2], ins), jnp.bfloat16)
    return pl.pallas_call(
        edges_kernel,
        out_shape=(shape, shape),
        in_specs=whole(4),
        out_specs=whole(2),
        compiler_params=pltpu.CompilerParams(vmem_limit_bytes=VMEM_LIMIT),
        name="edges",
    )(cache, features, cot, later)


def conv_one_kernel(cache, features, above, below, weight, cot, pre_norm, sums, wide):
    frames, rows, cols, outs = pre_norm.shape
    cells_in, half, ins = features.shape[1], cols // 2, features.shape[-1]
    timed = jnp.concatenate([cache[...], features[...]], 0)
    rowed = jnp.concatenate([above[:, :half][:, None], timed, below[:, :half][:, None]], 1)
    by_tap = []
    for e in range(3):
        total = jnp.zeros((frames, rows, half, outs), jnp.float32)
        for b in range(3):
            product = sum(
                jnp.dot(
                    rowed[a : a + frames].reshape(-1, ins),
                    weight[a, b, e],
                    preferred_element_type=jnp.float32,
                )
                for a in range(3)
            ).reshape(frames, cells_in + 2, half, outs)
            total += jnp.stack([product[:, (r + b) // 2] for r in range(rows)], 1)
        by_tap.append(total.reshape(frames * rows, half, outs))
    wide[...] = jnp.zeros_like(wide)
    wide[:, 8 : 8 + half, :outs] = by_tap[0]
    even = wide[:, 7 : 7 + half, :outs] + by_tap[1] + by_tap[2]
    wide[:, 8 : 8 + half, :outs] = by_tap[2]
    odd = by_tap[0] + by_tap[1] + wide[:, 9 : 9 + half, :outs]
    wide[:, pl.ds(0, half, stride=2), :outs] = even
    wide[:, pl.ds(1, half, stride=2), :outs] = odd
    pre = wide[:, :cols, :outs].reshape(pre_norm.shape)
    pre_norm[...] = pre
    own = pre[:, 1:-1]
    both = group_sums(cell_sums(own), cell_sums(own * own), outs)
    both = jnp.concatenate([both, cell_sums(cot[...].astype(jnp.float32)), jnp.zeros((1, outs), jnp.float32)], 0)
    sums[...] = jnp.broadcast_to(both[None], sums.shape)


def conv_one(cache, features, above, below, weight, cot, copies):
    frames, cells_in, half, _ = features.shape
    outs = weight.shape[-1]
    rows, cols = 2 * cells_in + 2, 2 * half
    return pl.pallas_call(
        conv_one_kernel,
        out_shape=(
            jax.ShapeDtypeStruct((frames, rows, cols, outs), jnp.float32),
            jax.ShapeDtypeStruct((copies, 4, outs), jnp.float32),
        ),
        in_specs=whole(6),
        out_specs=whole(2),
        scratch_shapes=[pltpu.VMEM((frames * rows, cols + 16, 128), jnp.float32)],
        compiler_params=pltpu.CompilerParams(vmem_limit_bytes=VMEM_LIMIT),
        name="conv_one",
    )(cache, features, above, below, weight, cot)


def grad_hidden_kernel(cot, later, above, below, weight, grad_hidden, shifted, all_taps, wide):
    frames, rows, cols, ins = grad_hidden.shape
    outs = cot.shape[-1]
    half = cols // 2
    timed = jnp.concatenate([cot[...], later[...]], 0)
    pair = lambda part: jnp.stack([part[:, half:, :outs], part[:, half:, outs:]], 1)
    rowed = jnp.concatenate([pair(above), timed, pair(below)], 1).astype(jnp.float32)
    wide[...] = jnp.zeros_like(wide)
    wide[:, 8 : 8 + cols, :outs] = rowed.reshape(-1, cols, outs)
    total = jnp.zeros((frames * rows * cols, ins), jnp.float32)
    for e in range(3):
        part = wide[:, 9 - e : 9 - e + cols, :outs].astype(jnp.bfloat16)
        part = part.reshape(2 * frames, rows + 2, cols, outs)
        shifted[e] = part
        for a in range(3):
            for b in range(3):
                total += lax.dot_general(
                    part[2 - a : 2 - a + frames, 2 - b : 2 - b + rows].reshape(-1, outs),
                    weight[a, b, e],
                    (((1,), (1,)), ((), ())),
                    preferred_element_type=jnp.float32,
                )
    grad_hidden[...] = total.reshape(grad_hidden.shape)
    all_taps[...] = sum(
        weight[a, b, e].astype(jnp.float32) for a in range(3) for b in range(3) for e in range(3)
    )


def hidden_grads(cot, later, above, below, weight):
    frames, rows, cols, outs = cot.shape
    return pl.pallas_call(
        grad_hidden_kernel,
        out_shape=(
            jax.ShapeDtypeStruct((frames, rows + 2, cols, weight.shape[-2]), jnp.float32),
            jax.ShapeDtypeStruct((3, 2 * frames, rows + 4, cols, outs), jnp.bfloat16),
            jax.ShapeDtypeStruct(weight.shape[-2:], jnp.float32),
        ),
        in_specs=whole(5),
        out_specs=whole(3),
        scratch_shapes=[pltpu.VMEM((2 * frames * (rows + 4), cols + 16, 128), jnp.float32)],
        compiler_params=pltpu.CompilerParams(vmem_limit_bytes=VMEM_LIMIT),
        cost_estimate=pl.CostEstimate(flops=2**30, bytes_accessed=2**21, transcendentals=0),
        name="grad_hidden",
    )(cot, later, above, below, weight)


def middle_kernel(count, where, came, pre_norm, grad_hidden, all_taps, gain, shift, hidden, grad_normed, normed, vectors):
    outs = pre_norm.shape[-1]
    total = jnp.sum(came[...], 0)
    mean = total[:1] / count
    scaled = lax.rsqrt(total[1:2] / count - mean * mean + EPSILON)
    flat = (pre_norm[...].reshape(-1, outs) - mean) * scaled
    shifted = flat * gain[...] + shift[...]
    sigma = 1.0 / (1.0 + jnp.exp(-shifted))
    hidden[...] = inside(where, (shifted * sigma).reshape(pre_norm.shape)).astype(jnp.bfloat16)
    grad = grad_hidden[...].reshape(-1, outs) * sigma * (1.0 + shifted * (1.0 - sigma)) * gain[...]
    grad, flat = grad.reshape(pre_norm.shape), flat.reshape(pre_norm.shape)
    grad_normed[...] = grad
    normed[...] = flat
    own = grad[:, 1:-1]

    cells = count / (outs // GROUPS)
    level = lax.dot_general(
        total[2:3] / cells,
        all_taps[...],
        (((1,), (1,)), ((), ())),
        precision=lax.Precision.HIGHEST,
        preferred_element_type=jnp.float32,
    )
    at = lax.broadcasted_iota(jnp.int32, (16, outs), 0).astype(jnp.float32) * 0.45 - 3.375
    share = jnp.exp(-0.5 * at * at)
    share = share / jnp.sum(share, 0, keepdims=True)
    point = at * gain[...] + shift[...]
    slope = 1.0 / (1.0 + jnp.exp(-point))
    slope = slope * (1.0 + point * (1.0 - slope)) * share
    level = level * gain[...] * (cells / count)
    offsets = group_sums(
        level * jnp.sum(slope, 0, keepdims=True), level * jnp.sum(slope * at, 0, keepdims=True), outs
    )
    rows = [scaled, offsets, cell_sums(own), cell_sums(own * flat[:, 1:-1])]
    vectors[...] = jnp.concatenate(rows + [jnp.zeros((3, outs), jnp.float32)], 0)


def middle(count, where, came, pre_norm, grad_hidden, all_taps, gain, shift):
    shape, outs = pre_norm.shape, pre_norm.shape[-1]
    return pl.pallas_call(
        functools.partial(middle_kernel, count),
        out_shape=(
            jax.ShapeDtypeStruct(shape, jnp.bfloat16),
            jax.ShapeDtypeStruct(shape, jnp.float32),
            jax.ShapeDtypeStruct(shape, jnp.float32),
            jax.ShapeDtypeStruct((8, outs), jnp.float32),
        ),
        in_specs=whole(1, pltpu.SMEM) + whole(6),
        out_specs=whole(4),
        compiler_params=pltpu.CompilerParams(vmem_limit_bytes=VMEM_LIMIT),
        name="middle",
    )(where, came, pre_norm, grad_hidden, all_taps, gain[None], shift[None])


def second_weight_kernel(hidden, shifted, out):
    frames, rows, cols, ins = hidden.shape
    outs = shifted.shape[-1]
    own = hidden[:, 1:-1].reshape(-1, ins).astype(jnp.float32).T.astype(jnp.bfloat16)
    for a in range(3):
        pieces = [
            shifted[e, 2 - a : 2 - a + frames, 3 - b : 3 - b + rows - 2].reshape(-1, outs)
            for b in range(3)
            for e in range(3)
        ]
        pieces.append(jnp.zeros((pieces[0].shape[0], 32), jnp.bfloat16))
        out[a] = jnp.dot(own, jnp.concatenate(pieces, 1), preferred_element_type=jnp.float32)


def second_weight(hidden, shifted):
    return pl.pallas_call(
        second_weight_kernel,
        out_shape=jax.ShapeDtypeStruct((3, hidden.shape[-1], 896), jnp.float32),
        in_specs=whole(2),
        out_specs=whole()[0],
        compiler_params=pltpu.CompilerParams(vmem_limit_bytes=VMEM_LIMIT),
        cost_estimate=pl.CostEstimate(flops=2**29, bytes_accessed=2**21, transcendentals=0),
        name="second_weight",
    )(hidden, shifted)


def col_sums(wide, cells):
    half = cells.shape[1] // 2
    wide[...] = jnp.zeros_like(wide)
    wide[:, 8 : 8 + cells.shape[1], : cells.shape[2]] = cells

    def every_second(start):
        return wide[:, pl.ds(start, half, stride=2), : cells.shape[2]]

    before, even, odd, after = (every_second(7 + k) for k in range(4))
    return odd + after, even + odd, before + even


def group_lanes(outs, first):
    lane = lax.broadcasted_iota(jnp.int32, (outs, 128), 1)
    group = lax.broadcasted_iota(jnp.int32, (outs, 128), 0) // (outs // GROUPS)
    return (lane == group + (64 if first else 64 + GROUPS)).astype(jnp.float32)


def exact(left, right, dims):
    return lax.dot_general(
        left, right, (dims, ((), ())), precision=lax.Precision.HIGHEST, preferred_element_type=jnp.float32
    )


def in_parts(sums, rows):
    high = sums.astype(jnp.bfloat16).astype(jnp.float32)
    middle = (sums - high).astype(jnp.bfloat16).astype(jnp.float32)
    low = sums - high - middle
    row = lax.broadcasted_iota(jnp.int32, (rows, 128), 0)
    return jnp.where(row == 0, high, jnp.where(row == 1, middle, jnp.where(row == 2, low, 0.0)))


def sums_of(tile):
    return tile[0:1] + tile[1:2] + tile[2:3]


def weight_grads_kernel(where, cache, features, above, below, grad_normed, normed, vectors, two, away, kept, wide):
    frames, rows, cols, outs = grad_normed.shape
    rows, half = rows - 2, cols // 2
    ins, mids, pieces, part_rows = features.shape[-1], two.shape[1], kept.shape[0], (kept.shape[1] - 16) * 2 // 5
    timed = jnp.concatenate([cache[...], features[...]], 0)
    rows_in = jnp.concatenate([above[:, :half][:, None], timed, below[:, :half][:, None]], 1)
    rstd, f0, s0 = (vectors[k : k + 1] for k in range(3))
    own = normed[:, 1:-1].reshape(-1, outs)
    grad = (grad_normed[:, 1:-1].reshape(-1, outs) - f0 - own * s0) * rstd
    lower = where[0] == 0

    def pool(field, last):
        by_tap = col_sums(wide, field.reshape(frames * rows, cols, outs))
        taps = []
        for b in range(3):
            for e in range(3):
                part = by_tap[e].reshape(frames, rows, half, outs)
                none = jnp.zeros_like(part[:, 0])
                r = [part[:, k] for k in range(rows)]
                stacked = (
                    [r[0], r[1] + r[2], r[3], none],
                    [none, r[0] + r[1], r[2] + r[3], none],
                    [none, r[0], r[1] + r[2], r[3]],
                )[b]
                taps.append(jnp.stack(stacked, 1).astype(jnp.bfloat16).reshape(-1, outs))
        return jnp.concatenate(taps + [last], 1)

    at = lax.broadcasted_iota(jnp.int32, (frames * 4 * half, 32), 0)
    tap = lax.broadcasted_iota(jnp.int32, (frames * 4 * half, 32), 1)
    b, e, row, col = tap // 3, tap % 3, at // half % 4, at % half
    two_rows = (row == 1) & (b < 2) | (row == 2) & (b > 0)
    one_row = (row == 0) & (b == 0) | (row == 2) & (b == 0) | (row == 1) & (b == 2) | (row == 3) & (b == 2)
    in_rows = jnp.where(two_rows, 2.0, jnp.where(one_row, 1.0, 0.0))
    in_cols = jnp.where((e == 0) & (col == half - 1) | (e == 2) & (col == 0), 1.0, 2.0)
    counts = jnp.where(tap < 9, in_rows * in_cols, 0.0).astype(jnp.bfloat16)

    def write(part, at, low, high):
        deep = part_rows if part < 2 else part_rows // 2
        while low.shape[0]:
            x, row = at // deep, part_rows * part + at % deep
            n = min(low.shape[0], deep - at % deep)
            away[x, row : row + n] = jnp.where(lower, high[:n], low[:n]).astype(jnp.bfloat16)
            kept[x, row : row + n] = jnp.where(lower, low[:n], high[:n])
            low, high, at = low[n:], high[n:], at + n

    for part, field, last in ((0, grad, counts), (1, own * rstd, jnp.zeros_like(counts))):
        cells = pool(field, last)
        at = 0
        for a in range(3):
            product = lax.dot_general(
                rows_in[a : a + frames].reshape(-1, ins),
                cells,
                (((0,), (0,)), ((), ())),
                preferred_element_type=jnp.float32,
            )
            for j in range(7):
                block = product[:, 128 * j : 128 * j + 128]
                write(part, at, block[: ins // 2], block[ins // 2 :])
                at += ins // 2
        nothing = jnp.zeros((pieces * part_rows - at, 128), jnp.float32)
        write(part, at, nothing, nothing)

    sums = exact(vectors[3:4], group_lanes(outs, True), ((1,), (0,)))
    sums += exact(vectors[4:5], group_lanes(outs, False), ((1,), (0,)))
    sums = in_parts(sums, 16)
    at = 0
    for a in range(3):
        for j in range(7):
            block = two[a, :, 128 * j : 128 * j + 128]
            write(2, at, block[: mids // 2], block[mids // 2 :])
            at += mids // 2
    nothing = jnp.zeros((pieces * part_rows // 2 - at, 128), jnp.float32)
    write(2, at, nothing, nothing)
    for x in range(pieces):
        away[x, part_rows * 5 // 2 :] = sums.astype(jnp.bfloat16)
        kept[x, part_rows * 5 // 2 :] = sums


def weight_grads(where, cache, features, above, below, grad_normed, normed, vectors, two, pieces, part_rows):
    frames, rows, cols, _ = grad_normed.shape
    shape = (pieces, part_rows * 5 // 2 + 16, 128)
    return pl.pallas_call(
        weight_grads_kernel,
        out_shape=(jax.ShapeDtypeStruct(shape, jnp.bfloat16), jax.ShapeDtypeStruct(shape, jnp.float32)),
        in_specs=whole(1, pltpu.SMEM) + whole(8),
        out_specs=whole(2),
        scratch_shapes=[pltpu.VMEM((frames * (rows - 2), cols + 16, 128), jnp.float32)],
        compiler_params=pltpu.CompilerParams(vmem_limit_bytes=VMEM_LIMIT),
        name="weight_grads",
    )(where, cache, features, above, below, grad_normed, normed, vectors, two)


def add_pair_kernel(kept, came, out):
    total = kept[...] + came[...].astype(jnp.float32)
    out[...] = total.astype(jnp.bfloat16)
    sums = in_parts(sums_of(total[0, -16:]), 16).astype(jnp.bfloat16)
    for x in range(out.shape[0]):
        out[x, out.shape[1] - 16 :] = sums


def add_pair(kept, came):
    return pl.pallas_call(
        add_pair_kernel,
        out_shape=jax.ShapeDtypeStruct(kept.shape, jnp.bfloat16),
        in_specs=whole(2),
        out_specs=whole()[0],
        compiler_params=pltpu.CompilerParams(vmem_limit_bytes=VMEM_LIMIT),
        name="add_pair",
    )(kept, came)


def add_row_kernel(came, out):
    total = jnp.sum(came[...].astype(jnp.float32), 0)
    n = out.shape[0] * 8
    out[:, 0] = total[:n].astype(jnp.bfloat16).reshape(-1, 8, 128)
    out[:, 1] = total[n : 2 * n].astype(jnp.bfloat16).reshape(-1, 8, 128)
    tiles = total[2 * n : n * 5 // 2].reshape(-1, 8, 128)
    row = lax.broadcasted_iota(jnp.int32, (1, 8, 128), 1)
    lane = lax.broadcasted_iota(jnp.int32, (1, 8, 128), 2)
    turned = jnp.concatenate([tiles[:, 4:], tiles[:, :4]], 1)
    swap = lambda k: jnp.concatenate([k[..., 64:], k[..., :64]], 2)
    even = jnp.where(row < 4, tiles, swap(turned))
    odd = jnp.where(row < 4, turned, swap(tiles))
    both = jnp.stack([even, odd], 1).reshape(-1, 8, 128)
    sums = in_parts(sums_of(total[n * 5 // 2 :]), 8)
    out[:, 2] = jnp.where(lane < 64, both, sums[None]).astype(jnp.bfloat16)


def add_row(came):
    tiles = (came.shape[1] - 16) // 20
    return pl.pallas_call(
        add_row_kernel,
        out_shape=jax.ShapeDtypeStruct((tiles, 3, 8, 128), jnp.bfloat16),
        in_specs=whole(1),
        out_specs=whole()[0],
        compiler_params=pltpu.CompilerParams(vmem_limit_bytes=VMEM_LIMIT),
        name="add_row",
    )(came)


def combine_kernel(count, tiles_per_block, where, came, vectors, piece, final, lanes):
    outs = vectors.shape[1]
    total = jnp.sum(came[...].astype(jnp.float32), 0)
    sums = sums_of(total[0, 2]) / count
    first = exact(sums, group_lanes(outs, True), ((1,), (1,)))
    second = exact(sums, group_lanes(outs, False), ((1,), (1,)))
    rest = (first - vectors[1:2]) * vectors[0:1]
    final[...] = jnp.concatenate([first, second, rest, jnp.zeros((5, outs), jnp.float32)], 0)
    lane = lax.broadcasted_iota(jnp.int32, (outs, 896), 1)
    channel = lax.broadcasted_iota(jnp.int32, (outs, 896), 0)
    spread = ((lane % outs == channel) & (lane < 9 * outs)).astype(jnp.float32)
    lanes[...] = jnp.broadcast_to(exact(second - vectors[2:3], spread, ((1,), (0,))), lanes.shape)
    for k in range(piece.shape[0]):
        block = (where[3] * piece.shape[0] + k) // tiles_per_block % 7
        change = lanes[0:1, pl.ds(pl.multiple_of(block * 128, 128), 128)]
        upper = jnp.concatenate([total[k, 2, :4, :64], total[k, 2, 4:, :64]], 1)
        grad = total[k, 0] - change * total[k, 1]
        piece[k] = jnp.concatenate([grad, upper], 0).astype(jnp.bfloat16)


def combine(count, ins, where, came, vectors):
    return pl.pallas_call(
        functools.partial(combine_kernel, count, ins // 16),
        out_shape=(
            jax.ShapeDtypeStruct((came.shape[1], 12, 128), jnp.bfloat16),
            jax.ShapeDtypeStruct(vectors.shape, jnp.float32),
        ),
        in_specs=whole(1, pltpu.SMEM) + whole(2),
        out_specs=whole(2),
        scratch_shapes=[pltpu.VMEM((8, 896), jnp.float32)],
        compiler_params=pltpu.CompilerParams(vmem_limit_bytes=VMEM_LIMIT),
        name="combine",
    )(where, came, vectors)


def grad_pre_kernel(where, grad_normed, normed, vectors, final, out):
    shape = grad_normed.shape
    flat = (-1, shape[-1])
    grad = grad_normed[...].reshape(flat) - final[:1] - normed[...].reshape(flat) * final[1:2]
    out[...] = inside(where, (grad * vectors[:1]).reshape(shape)).astype(jnp.bfloat16)


def grad_before_norm(where, grad_normed, normed, vectors, final):
    return pl.pallas_call(
        grad_pre_kernel,
        out_shape=jax.ShapeDtypeStruct(grad_normed.shape, jnp.bfloat16),
        in_specs=whole(1, pltpu.SMEM) + whole(4),
        out_specs=whole()[0],
        compiler_params=pltpu.CompilerParams(vmem_limit_bytes=VMEM_LIMIT),
        cost_estimate=pl.CostEstimate(flops=2**20, bytes_accessed=2**20, transcendentals=0),
        name="grad_pre",
    )(where, grad_normed, normed, vectors, final)


def unpack_kernel(scale, half, part, final, *rest):
    one, two, flat = rest[-3:]
    pieces, rows = part.shape[0], part.shape[1]
    split = rows * 2 // 3
    step = pl.program_id(0)

    @pl.when(step == 0)
    def _():
        for x in range(pieces):
            flat[split * x : split * (x + 1)] = part[x, :split]
            at = pieces * split + (rows - split) * x
            flat[at : at + rows - split] = part[x, split:]

    for out, begin in ((one, 0), (two, pieces * split)):
        taps, channels, outs = out.shape
        blocks = []
        for j in range(7):
            at = pl.multiple_of(begin + (step * 7 + j) * channels, 16)
            blocks.append(flat[pl.ds(at, channels)].astype(jnp.float32))
        lanes = jnp.concatenate(blocks, 1) * scale
        if out is one:
            change = jnp.concatenate([final[2:3]] * taps + [jnp.zeros((1, 32), jnp.float32)], 1)
            tap = lax.broadcasted_iota(jnp.int32, (32, change.shape[1]), 0)
            lane = lax.broadcasted_iota(jnp.int32, (32, change.shape[1]), 1)
            change = jnp.where(lane // outs == tap, change, 0.0)
            lanes -= exact(lanes[:, outs * taps :], change, ((1,), (0,)))
        for k in range(taps):
            out[k] = lanes[:, outs * k : outs * k + outs]


def unpack(half, part, final, ins, mids, scale, begun=()):
    return pl.pallas_call(
        functools.partial(unpack_kernel, scale),
        grid_spec=pltpu.PrefetchScalarGridSpec(
            num_scalar_prefetch=1,
            grid=(3,),
            in_specs=whole(2) + whole(len(begun), pl.ANY),
            out_specs=[
                pl.BlockSpec((9, ins // 2, mids), lambda a, half: (a, half[0], 0)),
                pl.BlockSpec((9, mids // 2, mids), lambda a, half: (a, half[0], 0)),
            ],
            scratch_shapes=[pltpu.VMEM((part.shape[0] * part.shape[1], 128), jnp.bfloat16)],
        ),
        out_shape=(
            jax.ShapeDtypeStruct((27, ins, mids), jnp.float32),
            jax.ShapeDtypeStruct((27, mids, mids), jnp.float32),
        ),
        input_output_aliases={3 + k: k for k in range(len(begun))},
        compiler_params=pltpu.CompilerParams(vmem_limit_bytes=VMEM_LIMIT),
        cost_estimate=pl.CostEstimate(flops=2**20, bytes_accessed=2**22, transcendentals=0),
        name="unpack",
    )(half, part, final, *begun)


def feature_grads_kernel(grad_pre, weight, out, wide):
    frames, rows, cols, outs = grad_pre.shape
    own, cells_in, cols_in, ins = out.shape
    by_tap = col_sums(wide, grad_pre[...].astype(jnp.float32).reshape(frames * rows, cols, outs))
    total = jnp.zeros((own * cells_in * cols_in, ins), jnp.float32)
    for b in range(3):
        for e in range(3):
            part = by_tap[e].reshape(frames, rows, cols // 2, outs)
            cells = jnp.stack(
                [part[:, 2 * k + 2 - b] + part[:, 2 * k + 3 - b] for k in range(cells_in)], 1
            ).astype(jnp.bfloat16)
            for a in range(3):
                total += lax.dot_general(
                    cells[2 - a : 2 - a + own].reshape(-1, outs),
                    weight[a, b, e],
                    (((1,), (1,)), ((), ())),
                    preferred_element_type=jnp.float32,
                )
    out[...] = total.reshape(out.shape)


def feature_grads(grad_rowed, weight, shape):
    frames, rows, cols, _ = grad_rowed.shape
    return pl.pallas_call(
        feature_grads_kernel,
        out_shape=jax.ShapeDtypeStruct(shape, jnp.float32),
        in_specs=whole(2),
        out_specs=whole()[0],
        scratch_shapes=[pltpu.VMEM((frames * rows, cols + 16, 128), jnp.float32)],
        compiler_params=pltpu.CompilerParams(vmem_limit_bytes=VMEM_LIMIT),
        cost_estimate=pl.CostEstimate(flops=2**28, bytes_accessed=2**21, transcendentals=0),
        name="feature_grads",
    )(grad_rowed, weight)


SWAP = [(0, 1), (1, 0)]


def body(features, cotangent, weight_one, weight_two, norm_gain, norm_shift):
    frames, ins = features.shape[0], features.shape[-1]
    rows, cols, mids = cotangent.shape[1:]
    xs, rest, height = lax.axis_size("x"), lax.axis_size(REST), lax.axis_size(HEIGHT)
    cells = frames * rows * cols * 2 * xs * rest
    count = cells * (mids // GROUPS)
    at_row = lax.axis_index(HEIGHT)
    owned = lax.axis_index("x") * rest + lax.axis_index(REST)
    where = jnp.stack([lax.axis_index("c"), at_row == 0, at_row == height - 1, owned]).astype(jnp.int32)
    barrier = lax.optimization_barrier

    def exchange(copies, axes):
        return lax.all_to_all(copies, axes, 0, 0)

    def spread(value, copies):
        return jnp.broadcast_to(value[None], (copies,) + value.shape)

    cache = neighbour(features, TM, 1)
    later = neighbour(cotangent, TM, -1)

    features, cotangent, weight_one, weight_two = resident(features, cotangent, weight_one, weight_two)
    downward, upward = edges(cache, features, cotangent, later)
    above = neighbour(downward, HEIGHT, 1)
    below = neighbour(upward, HEIGHT, -1)
    pre_norm, sums = conv_one(cache, features, above, below, weight_one, cotangent, height)
    came = exchange(sums, HEIGHT)
    grad_hidden, shifted_cot, all_taps = hidden_grads(cotangent, later, above, below, weight_two)
    sums, grad_hidden, shifted_cot = barrier((came.sum(0), grad_hidden, shifted_cot))
    came = exchange(spread(sums, lax.axis_size(TM)), TM)
    hidden, grad_normed, normed, vectors = middle(
        count, where, came, pre_norm, grad_hidden, all_taps, norm_gain, norm_shift
    )
    local_two = second_weight(hidden, shifted_cot)

    scale = 1.0 / cells**0.5
    part_rows = -(-21 * ins // (2 * 8 * xs * rest)) * 8 * rest
    away, kept = weight_grads(
        where, cache, features, above, below, grad_normed, normed, vectors, local_two, xs, part_rows
    )
    part = add_pair(kept, lax.ppermute(away, "c", SWAP))
    part, hidden = barrier((part, hidden))
    part = add_row(exchange(part, "x"))
    before = neighbour(hidden, TM, 1)
    part, before = barrier((part, before))
    came = exchange(part.reshape(rest, -1, 3, 8, 128), REST)
    decoded = conv(
        jnp.pad(jnp.concatenate([before, hidden], 0), ((0, 0), (0, 0), (1, 1), (0, 0))), weight_two
    ).astype(jnp.bfloat16)
    came, decoded = barrier((came, decoded))
    part, final = combine(count, ins, where, came, vectors)
    grad_pre = grad_before_norm(where, grad_normed, normed, vectors, final)
    part = exchange(spread(part, rest), REST)
    after = neighbour(grad_pre, TM, -1)
    part, after = barrier((part, after))
    part = jnp.concatenate([part[:, :, :8].reshape(-1, 128), part[:, :, 8:].reshape(-1, 128)], 0)
    part = exchange(spread(part, xs), "x")
    grad_features = feature_grads(jnp.concatenate([grad_pre, after], 0), weight_one, features.shape)
    part, grad_features = barrier((part, grad_features))
    other = lax.ppermute(part, "c", SWAP)
    core = where[:1]
    begun = unpack(core, part, final, ins, mids, scale)
    grad_one, grad_two = unpack(1 - core, other, final, ins, mids, scale, begun)
    return decoded, grad_features, grad_one.reshape(weight_one.shape), grad_two.reshape(weight_two.shape)


def solution(mesh):
    split = P(TM, HEIGHT, None, None)
    return jax.shard_map(
        body,
        mesh=fine_mesh(mesh),
        in_specs=(split, split, P(), P(), P(), P()),
        out_specs=(split, split, P(), P()),
        check_vma=False,
    )
```

```python
import functools

import jax
import jax.numpy as jnp
from jax import lax
from jax.experimental import pallas as pl
from jax.experimental.pallas import tpu as pltpu
from jax.sharding import Mesh
from jax.sharding import PartitionSpec as P

GROUPS = 32
EPSILON = 1e-05

TM = ("zh", "y")
HEIGHT = ("zl", "x", "c")
REST = ("zh", "y", "zl")

VMEM_LIMIT = 32 * 2**20


def fine_mesh(mesh):
    tm, height = mesh.shape["tm"], mesh.shape["height"]
    zh = 2 if tm % 2 == 0 else 1
    core = 2
    x = 4 if height % 8 == 0 else height // 2
    return Mesh(mesh.devices.reshape(zh, tm // zh, height // (core * x), x, core), TM + HEIGHT)


def neighbour(value, axis, steps):
    count = lax.axis_size(axis)
    first, last = max(0, -steps), min(count, count - steps)
    return lax.ppermute(value, axis, [(i, i + steps) for i in range(first, last)])


def conv(padded, weight):
    return lax.conv_general_dilated(
        padded[None],
        weight,
        (1, 1, 1),
        "VALID",
        dimension_numbers=("NDHWC", "DHWIO", "NDHWC"),
        preferred_element_type=jnp.float32,
    )[0]


def whole(count=1, space=pltpu.VMEM):
    return [pl.BlockSpec(memory_space=space)] * count


def group_sums(first, second, outs):
    member = lax.broadcasted_iota(jnp.int32, (2, outs, outs), 1) // (outs // GROUPS)
    other = lax.broadcasted_iota(jnp.int32, (2, outs, outs), 2) // (outs // GROUPS)
    same = (member[0] == other[0]).astype(jnp.float32)
    both = jnp.concatenate([first, second, jnp.zeros((6, outs), jnp.float32)], 0)
    return jnp.dot(both, same, precision=lax.Precision.HIGHEST, preferred_element_type=jnp.float32)[:2]


def cell_sums(field):
    return jnp.sum(field.reshape(-1, field.shape[-1]), 0, keepdims=True)


def inside(where, field):
    row = lax.broadcasted_iota(jnp.int32, field.shape, 1)
    last = field.shape[1] - 1
    out = ((row == 0) & (where[1] == 1)) | ((row == last) & (where[2] == 1))
    return jnp.where(out, 0.0, field)


def resident_kernel(*refs):
    count = len(refs) // 2
    sems = refs[-1]
    moves = [pltpu.make_async_copy(refs[k], refs[count + k], sems.at[k]) for k in range(count)]
    for move in moves:
        move.start()
    for move in moves:
        move.wait()


def resident(*arrays):
    count = len(arrays)
    return pl.pallas_call(
        resident_kernel,
        out_shape=[jax.ShapeDtypeStruct(k.shape, k.dtype) for k in arrays],
        in_specs=whole(count, pltpu.HBM),
        out_specs=whole(count),
        scratch_shapes=[pltpu.SemaphoreType.DMA((count,))],
        compiler_params=pltpu.CompilerParams(vmem_limit_bytes=VMEM_LIMIT),
        cost_estimate=pl.CostEstimate(flops=0, bytes_accessed=2**22, transcendentals=0),
        name="resident",
    )(*arrays)


def edges_kernel(cache, features, cot, later, downward, upward):
    cells, rows = features.shape[1], cot.shape[1]
    half = features.shape[2]
    for out, cell, row in ((downward, cells - 1, rows - 2), (upward, 0, 0)):
        out[:, :half] = jnp.concatenate([cache[:, cell], features[:, cell]], 0)
        pair = [jnp.concatenate([cot[:, k], later[:, k]], 0) for k in (row, row + 1)]
        out[:, half:] = jnp.concatenate(pair, 2)


def edges(cache, features, cot, later):
    frames, _, half, ins = features.shape
    shape = jax.ShapeDtypeStruct((2 * frames, half + cot.shape[2], ins), jnp.bfloat16)
    return pl.pallas_call(
        edges_kernel,
        out_shape=(shape, shape),
        in_specs=whole(4),
        out_specs=whole(2),
        compiler_params=pltpu.CompilerParams(vmem_limit_bytes=VMEM_LIMIT),
        name="edges",
    )(cache, features, cot, later)


def conv_one_kernel(cache, features, above, below, weight, cot, pre_norm, sums, wide):
    frames, rows, cols, outs = pre_norm.shape
    cells_in, half, ins = features.shape[1], cols // 2, features.shape[-1]
    timed = jnp.concatenate([cache[...], features[...]], 0)
    rowed = jnp.concatenate([above[:, :half][:, None], timed, below[:, :half][:, None]], 1)
    by_tap = []
    for e in range(3):
        total = jnp.zeros((frames, rows, half, outs), jnp.float32)
        for b in range(3):
            product = sum(
                jnp.dot(
                    rowed[a : a + frames].reshape(-1, ins),
                    weight[a, b, e],
                    preferred_element_type=jnp.float32,
                )
                for a in range(3)
            ).reshape(frames, cells_in + 2, half, outs)
            total += jnp.stack([product[:, (r + b) // 2] for r in range(rows)], 1)
        by_tap.append(total.reshape(frames * rows, half, outs))
    wide[...] = jnp.zeros_like(wide)
    wide[:, 8 : 8 + half, :outs] = by_tap[0]
    even = wide[:, 7 : 7 + half, :outs] + by_tap[1] + by_tap[2]
    wide[:, 8 : 8 + half, :outs] = by_tap[2]
    odd = by_tap[0] + by_tap[1] + wide[:, 9 : 9 + half, :outs]
    wide[:, pl.ds(0, half, stride=2), :outs] = even
    wide[:, pl.ds(1, half, stride=2), :outs] = odd
    pre = wide[:, :cols, :outs].reshape(pre_norm.shape)
    pre_norm[...] = pre
    own = pre[:, 1:-1]
    both = group_sums(cell_sums(own), cell_sums(own * own), outs)
    both = jnp.concatenate([both, cell_sums(cot[...].astype(jnp.float32)), jnp.zeros((1, outs), jnp.float32)], 0)
    sums[...] = jnp.broadcast_to(both[None], sums.shape)


def conv_one(cache, features, above, below, weight, cot, copies):
    frames, cells_in, half, _ = features.shape
    outs = weight.shape[-1]
    rows, cols = 2 * cells_in + 2, 2 * half
    return pl.pallas_call(
        conv_one_kernel,
        out_shape=(
            jax.ShapeDtypeStruct((frames, rows, cols, outs), jnp.float32),
            jax.ShapeDtypeStruct((copies, 4, outs), jnp.float32),
        ),
        in_specs=whole(6),
        out_specs=whole(2),
        scratch_shapes=[pltpu.VMEM((frames * rows, cols + 16, 128), jnp.float32)],
        compiler_params=pltpu.CompilerParams(vmem_limit_bytes=VMEM_LIMIT),
        name="conv_one",
    )(cache, features, above, below, weight, cot)


def fill_cot(wide, cot, later, above, below):
    cols, outs = cot.shape[2:]
    half = cols // 2
    timed = jnp.concatenate([cot[...], later[...]], 0)
    pair = lambda part: jnp.stack([part[:, half:, :outs], part[:, half:, outs:]], 1)
    rowed = jnp.concatenate([pair(above), timed, pair(below)], 1).astype(jnp.float32)
    wide[...] = jnp.zeros_like(wide)
    wide[:, 8 : 8 + cols, :outs] = rowed.reshape(-1, cols, outs)


def col_tap(wide, e, shape):
    part = wide[:, 9 - e : 9 - e + shape[2], : shape[3]].astype(jnp.bfloat16)
    return part.reshape(2 * shape[0], shape[1] + 4, shape[2], shape[3])


def grad_hidden_kernel(cot, later, above, below, weight, grad_hidden, all_taps, wide):
    frames, rows, cols, ins = grad_hidden.shape
    outs = cot.shape[-1]
    fill_cot(wide, cot, later, above, below)
    total = jnp.zeros((frames * rows * cols, ins), jnp.float32)
    for e in range(3):
        part = col_tap(wide, e, cot.shape)
        for a in range(3):
            for b in range(3):
                total += lax.dot_general(
                    part[2 - a : 2 - a + frames, 2 - b : 2 - b + rows].reshape(-1, outs),
                    weight[a, b, e],
                    (((1,), (1,)), ((), ())),
                    preferred_element_type=jnp.float32,
                )
    grad_hidden[...] = total.reshape(grad_hidden.shape)
    all_taps[...] = sum(
        weight[a, b, e].astype(jnp.float32) for a in range(3) for b in range(3) for e in range(3)
    )


def hidden_grads(cot, later, above, below, weight):
    frames, rows, cols, outs = cot.shape
    return pl.pallas_call(
        grad_hidden_kernel,
        out_shape=(
            jax.ShapeDtypeStruct((frames, rows + 2, cols, weight.shape[-2]), jnp.float32),
            jax.ShapeDtypeStruct(weight.shape[-2:], jnp.float32),
        ),
        in_specs=whole(5),
        out_specs=whole(2),
        scratch_shapes=[pltpu.VMEM((2 * frames * (rows + 4), cols + 16, 128), jnp.float32)],
        compiler_params=pltpu.CompilerParams(vmem_limit_bytes=VMEM_LIMIT),
        cost_estimate=pl.CostEstimate(flops=2**30, bytes_accessed=2**21, transcendentals=0),
        name="grad_hidden",
    )(cot, later, above, below, weight)


def middle_kernel(count, where, came, pre_norm, grad_hidden, all_taps, gain, shift, hidden, grad_normed, normed, vectors):
    outs = pre_norm.shape[-1]
    total = jnp.sum(came[...], 0)
    mean = total[:1] / count
    scaled = lax.rsqrt(total[1:2] / count - mean * mean + EPSILON)
    flat = (pre_norm[...].reshape(-1, outs) - mean) * scaled
    shifted = flat * gain[...] + shift[...]
    sigma = 1.0 / (1.0 + jnp.exp(-shifted))
    hidden[...] = inside(where, (shifted * sigma).reshape(pre_norm.shape)).astype(jnp.bfloat16)
    grad = grad_hidden[...].reshape(-1, outs) * sigma * (1.0 + shifted * (1.0 - sigma)) * gain[...]
    grad, flat = grad.reshape(pre_norm.shape), flat.reshape(pre_norm.shape)
    grad_normed[...] = grad
    normed[...] = flat
    own = grad[:, 1:-1]

    cells = count / (outs // GROUPS)
    level = lax.dot_general(
        total[2:3] / cells,
        all_taps[...],
        (((1,), (1,)), ((), ())),
        precision=lax.Precision.HIGHEST,
        preferred_element_type=jnp.float32,
    )
    at = lax.broadcasted_iota(jnp.int32, (16, outs), 0).astype(jnp.float32) * 0.45 - 3.375
    share = jnp.exp(-0.5 * at * at)
    share = share / jnp.sum(share, 0, keepdims=True)
    point = at * gain[...] + shift[...]
    slope = 1.0 / (1.0 + jnp.exp(-point))
    slope = slope * (1.0 + point * (1.0 - slope)) * share
    level = level * gain[...] * (cells / count)
    offsets = group_sums(
        level * jnp.sum(slope, 0, keepdims=True), level * jnp.sum(slope * at, 0, keepdims=True), outs
    )
    rows = [scaled, offsets, cell_sums(own), cell_sums(own * flat[:, 1:-1])]
    vectors[...] = jnp.concatenate(rows + [jnp.zeros((3, outs), jnp.float32)], 0)


def middle(count, where, came, pre_norm, grad_hidden, all_taps, gain, shift):
    shape, outs = pre_norm.shape, pre_norm.shape[-1]
    return pl.pallas_call(
        functools.partial(middle_kernel, count),
        out_shape=(
            jax.ShapeDtypeStruct(shape, jnp.bfloat16),
            jax.ShapeDtypeStruct(shape, jnp.float32),
            jax.ShapeDtypeStruct(shape, jnp.float32),
            jax.ShapeDtypeStruct((8, outs), jnp.float32),
        ),
        in_specs=whole(1, pltpu.SMEM) + whole(6),
        out_specs=whole(4),
        compiler_params=pltpu.CompilerParams(vmem_limit_bytes=VMEM_LIMIT),
        name="middle",
    )(where, came, pre_norm, grad_hidden, all_taps, gain[None], shift[None])


def second_weight_kernel(hidden, cot, later, above, below, out, wide):
    frames, rows, cols, ins = hidden.shape
    outs = cot.shape[-1]
    own = hidden[:, 1:-1].reshape(-1, ins).astype(jnp.float32).T.astype(jnp.bfloat16)
    fill_cot(wide, cot, later, above, below)
    shifted = [col_tap(wide, e, cot.shape) for e in range(3)]
    for a in range(3):
        pieces = [
            shifted[e][2 - a : 2 - a + frames, 3 - b : 3 - b + rows - 2].reshape(-1, outs)
            for b in range(3)
            for e in range(3)
        ]
        pieces.append(jnp.zeros((pieces[0].shape[0], 32), jnp.bfloat16))
        out[a] = jnp.dot(own, jnp.concatenate(pieces, 1), preferred_element_type=jnp.float32)


def second_weight(hidden, cot, later, above, below):
    frames, rows, cols, _ = cot.shape
    return pl.pallas_call(
        second_weight_kernel,
        out_shape=jax.ShapeDtypeStruct((3, hidden.shape[-1], 896), jnp.float32),
        in_specs=whole(5),
        out_specs=whole()[0],
        scratch_shapes=[pltpu.VMEM((2 * frames * (rows + 4), cols + 16, 128), jnp.float32)],
        compiler_params=pltpu.CompilerParams(vmem_limit_bytes=VMEM_LIMIT),
        name="second_weight",
    )(hidden, cot, later, above, below)


def col_sums(wide, cells):
    half = cells.shape[1] // 2
    wide[...] = jnp.zeros_like(wide)
    wide[:, 8 : 8 + cells.shape[1], : cells.shape[2]] = cells

    def every_second(start):
        return wide[:, pl.ds(start, half, stride=2), : cells.shape[2]]

    before, even, odd, after = (every_second(7 + k) for k in range(4))
    return odd + after, even + odd, before + even


def group_lanes(outs, first):
    lane = lax.broadcasted_iota(jnp.int32, (outs, 128), 1)
    group = lax.broadcasted_iota(jnp.int32, (outs, 128), 0) // (outs // GROUPS)
    return (lane == group + (64 if first else 64 + GROUPS)).astype(jnp.float32)


def exact(left, right, dims):
    return lax.dot_general(
        left, right, (dims, ((), ())), precision=lax.Precision.HIGHEST, preferred_element_type=jnp.float32
    )


def in_parts(sums, rows):
    high = sums.astype(jnp.bfloat16).astype(jnp.float32)
    middle = (sums - high).astype(jnp.bfloat16).astype(jnp.float32)
    low = sums - high - middle
    row = lax.broadcasted_iota(jnp.int32, (rows, 128), 0)
    return jnp.where(row == 0, high, jnp.where(row == 1, middle, jnp.where(row == 2, low, 0.0)))


def sums_of(tile):
    return tile[0:1] + tile[1:2] + tile[2:3]


def weight_grads_kernel(where, cache, features, above, below, grad_normed, normed, vectors, two, away, kept, wide):
    frames, rows, cols, outs = grad_normed.shape
    rows, half = rows - 2, cols // 2
    ins, mids, pieces, part_rows = features.shape[-1], two.shape[1], kept.shape[0], (kept.shape[1] - 16) * 2 // 5
    timed = jnp.concatenate([cache[...], features[...]], 0)
    rows_in = jnp.concatenate([above[:, :half][:, None], timed, below[:, :half][:, None]], 1)
    rstd, f0, s0 = (vectors[k : k + 1] for k in range(3))
    own = normed[:, 1:-1].reshape(-1, outs)
    grad = (grad_normed[:, 1:-1].reshape(-1, outs) - f0 - own * s0) * rstd
    lower = where[0] == 0

    def pool(field, last):
        by_tap = col_sums(wide, field.reshape(frames * rows, cols, outs))
        taps = []
        for b in range(3):
            for e in range(3):
                part = by_tap[e].reshape(frames, rows, half, outs)
                none = jnp.zeros_like(part[:, 0])
                r = [part[:, k] for k in range(rows)]
                stacked = (
                    [r[0], r[1] + r[2], r[3], none],
                    [none, r[0] + r[1], r[2] + r[3], none],
                    [none, r[0], r[1] + r[2], r[3]],
                )[b]
                taps.append(jnp.stack(stacked, 1).astype(jnp.bfloat16).reshape(-1, outs))
        return jnp.concatenate(taps + [last], 1)

    at = lax.broadcasted_iota(jnp.int32, (frames * 4 * half, 32), 0)
    tap = lax.broadcasted_iota(jnp.int32, (frames * 4 * half, 32), 1)
    b, e, row, col = tap // 3, tap % 3, at // half % 4, at % half
    two_rows = (row == 1) & (b < 2) | (row == 2) & (b > 0)
    one_row = (row == 0) & (b == 0) | (row == 2) & (b == 0) | (row == 1) & (b == 2) | (row == 3) & (b == 2)
    in_rows = jnp.where(two_rows, 2.0, jnp.where(one_row, 1.0, 0.0))
    in_cols = jnp.where((e == 0) & (col == half - 1) | (e == 2) & (col == 0), 1.0, 2.0)
    counts = jnp.where(tap < 9, in_rows * in_cols, 0.0).astype(jnp.bfloat16)

    def write(part, at, low, high):
        deep = part_rows if part < 2 else part_rows // 2
        while low.shape[0]:
            x, row = at // deep, part_rows * part + at % deep
            n = min(low.shape[0], deep - at % deep)
            away[x, row : row + n] = jnp.where(lower, high[:n], low[:n]).astype(jnp.bfloat16)
            kept[x, row : row + n] = jnp.where(lower, low[:n], high[:n])
            low, high, at = low[n:], high[n:], at + n

    for part, field, last in ((0, grad, counts), (1, own * rstd, jnp.zeros_like(counts))):
        cells = pool(field, last)
        at = 0
        for a in range(3):
            product = lax.dot_general(
                rows_in[a : a + frames].reshape(-1, ins),
                cells,
                (((0,), (0,)), ((), ())),
                preferred_element_type=jnp.float32,
            )
            for j in range(7):
                block = product[:, 128 * j : 128 * j + 128]
                write(part, at, block[: ins // 2], block[ins // 2 :])
                at += ins // 2
        nothing = jnp.zeros((pieces * part_rows - at, 128), jnp.float32)
        write(part, at, nothing, nothing)

    sums = exact(vectors[3:4], group_lanes(outs, True), ((1,), (0,)))
    sums += exact(vectors[4:5], group_lanes(outs, False), ((1,), (0,)))
    sums = in_parts(sums, 16)
    at = 0
    for a in range(3):
        for j in range(7):
            block = two[a, :, 128 * j : 128 * j + 128]
            write(2, at, block[: mids // 2], block[mids // 2 :])
            at += mids // 2
    nothing = jnp.zeros((pieces * part_rows // 2 - at, 128), jnp.float32)
    write(2, at, nothing, nothing)
    for x in range(pieces):
        away[x, part_rows * 5 // 2 :] = sums.astype(jnp.bfloat16)
        kept[x, part_rows * 5 // 2 :] = sums


def weight_grads(where, cache, features, above, below, grad_normed, normed, vectors, two, pieces, part_rows):
    frames, rows, cols, _ = grad_normed.shape
    shape = (pieces, part_rows * 5 // 2 + 16, 128)
    return pl.pallas_call(
        weight_grads_kernel,
        out_shape=(jax.ShapeDtypeStruct(shape, jnp.bfloat16), jax.ShapeDtypeStruct(shape, jnp.float32)),
        in_specs=whole(1, pltpu.SMEM) + whole(8),
        out_specs=whole(2),
        scratch_shapes=[pltpu.VMEM((frames * (rows - 2), cols + 16, 128), jnp.float32)],
        compiler_params=pltpu.CompilerParams(vmem_limit_bytes=VMEM_LIMIT),
        name="weight_grads",
    )(where, cache, features, above, below, grad_normed, normed, vectors, two)


def add_pair_kernel(kept, came, out, total, sems):
    deep = kept.shape[1] - 16
    sums = in_parts(sums_of(kept[0, deep:] + came[0, deep:].astype(jnp.float32)), 16).astype(jnp.bfloat16)
    moves = []
    for x in range(kept.shape[0]):
        total[x, :deep] = (kept[x, :deep] + came[x, :deep].astype(jnp.float32)).astype(jnp.bfloat16)
        total[x, deep:] = sums
        moves.append(pltpu.make_async_copy(total.at[x], out.at[x], sems.at[x]))
        moves[x].start()
    for move in moves:
        move.wait()


def add_pair(kept, came):
    return pl.pallas_call(
        add_pair_kernel,
        out_shape=jax.ShapeDtypeStruct(kept.shape, jnp.bfloat16),
        in_specs=whole(2),
        out_specs=whole(1, pltpu.HBM)[0],
        scratch_shapes=[pltpu.VMEM(kept.shape, jnp.bfloat16), pltpu.SemaphoreType.DMA((kept.shape[0],))],
        compiler_params=pltpu.CompilerParams(vmem_limit_bytes=VMEM_LIMIT),
        name="add_pair",
    )(kept, came)


def add_row_kernel(came, out):
    total = jnp.sum(came[...].astype(jnp.float32), 0)
    n = out.shape[0] * 8
    out[:, 0] = total[:n].astype(jnp.bfloat16).reshape(-1, 8, 128)
    out[:, 1] = total[n : 2 * n].astype(jnp.bfloat16).reshape(-1, 8, 128)
    tiles = total[2 * n : n * 5 // 2].reshape(-1, 8, 128)
    row = lax.broadcasted_iota(jnp.int32, (1, 8, 128), 1)
    lane = lax.broadcasted_iota(jnp.int32, (1, 8, 128), 2)
    turned = jnp.concatenate([tiles[:, 4:], tiles[:, :4]], 1)
    swap = lambda k: jnp.concatenate([k[..., 64:], k[..., :64]], 2)
    even = jnp.where(row < 4, tiles, swap(turned))
    odd = jnp.where(row < 4, turned, swap(tiles))
    both = jnp.stack([even, odd], 1).reshape(-1, 8, 128)
    sums = in_parts(sums_of(total[n * 5 // 2 :]), 8)
    out[:, 2] = jnp.where(lane < 64, both, sums[None]).astype(jnp.bfloat16)


def add_row(came):
    tiles = (came.shape[1] - 16) // 20
    return pl.pallas_call(
        add_row_kernel,
        out_shape=jax.ShapeDtypeStruct((tiles, 3, 8, 128), jnp.bfloat16),
        in_specs=whole(1),
        out_specs=whole()[0],
        compiler_params=pltpu.CompilerParams(vmem_limit_bytes=VMEM_LIMIT),
        name="add_row",
    )(came)


def combine_kernel(count, tiles_per_block, where, came, vectors, piece, final, lanes):
    outs = vectors.shape[1]
    total = jnp.sum(came[...].astype(jnp.float32), 0)
    sums = sums_of(total[0, 2]) / count
    first = exact(sums, group_lanes(outs, True), ((1,), (1,)))
    second = exact(sums, group_lanes(outs, False), ((1,), (1,)))
    rest = (first - vectors[1:2]) * vectors[0:1]
    final[...] = jnp.concatenate([first, second, rest, jnp.zeros((5, outs), jnp.float32)], 0)
    lane = lax.broadcasted_iota(jnp.int32, (outs, 896), 1)
    channel = lax.broadcasted_iota(jnp.int32, (outs, 896), 0)
    spread = ((lane % outs == channel) & (lane < 9 * outs)).astype(jnp.float32)
    lanes[...] = jnp.broadcast_to(exact(second - vectors[2:3], spread, ((1,), (0,))), lanes.shape)
    for k in range(piece.shape[0]):
        block = (where[3] * piece.shape[0] + k) // tiles_per_block % 7
        change = lanes[0:1, pl.ds(pl.multiple_of(block * 128, 128), 128)]
        upper = jnp.concatenate([total[k, 2, :4, :64], total[k, 2, 4:, :64]], 1)
        grad = total[k, 0] - change * total[k, 1]
        piece[k] = jnp.concatenate([grad, upper], 0).astype(jnp.bfloat16)


def combine(count, ins, where, came, vectors):
    return pl.pallas_call(
        functools.partial(combine_kernel, count, ins // 16),
        out_shape=(
            jax.ShapeDtypeStruct((came.shape[1], 12, 128), jnp.bfloat16),
            jax.ShapeDtypeStruct(vectors.shape, jnp.float32),
        ),
        in_specs=whole(1, pltpu.SMEM) + whole(2),
        out_specs=whole(2),
        scratch_shapes=[pltpu.VMEM((8, 896), jnp.float32)],
        compiler_params=pltpu.CompilerParams(vmem_limit_bytes=VMEM_LIMIT),
        name="combine",
    )(where, came, vectors)


def grad_pre_kernel(where, grad_normed, normed, vectors, final, out):
    shape = grad_normed.shape
    flat = (-1, shape[-1])
    grad = grad_normed[...].reshape(flat) - final[:1] - normed[...].reshape(flat) * final[1:2]
    out[...] = inside(where, (grad * vectors[:1]).reshape(shape)).astype(jnp.bfloat16)


def grad_before_norm(where, grad_normed, normed, vectors, final):
    return pl.pallas_call(
        grad_pre_kernel,
        out_shape=jax.ShapeDtypeStruct(grad_normed.shape, jnp.bfloat16),
        in_specs=whole(1, pltpu.SMEM) + whole(4),
        out_specs=whole()[0],
        compiler_params=pltpu.CompilerParams(vmem_limit_bytes=VMEM_LIMIT),
        cost_estimate=pl.CostEstimate(flops=2**20, bytes_accessed=2**20, transcendentals=0),
        name="grad_pre",
    )(where, grad_normed, normed, vectors, final)


def unpack_kernel(scale, half, part, final, *rest):
    one, two, flat = rest[-3:]
    pieces, rows = part.shape[0], part.shape[1]
    split = rows * 2 // 3
    step = pl.program_id(0)

    @pl.when(step == 0)
    def _():
        for x in range(pieces):
            flat[split * x : split * (x + 1)] = part[x, :split]
            at = pieces * split + (rows - split) * x
            flat[at : at + rows - split] = part[x, split:]

    for out, begin in ((one, 0), (two, pieces * split)):
        taps, channels, outs = out.shape
        blocks = []
        for j in range(7):
            at = pl.multiple_of(begin + (step * 7 + j) * channels, 16)
            blocks.append(flat[pl.ds(at, channels)].astype(jnp.float32))
        lanes = jnp.concatenate(blocks, 1) * scale
        if out is one:
            change = jnp.concatenate([final[2:3]] * taps + [jnp.zeros((1, 32), jnp.float32)], 1)
            tap = lax.broadcasted_iota(jnp.int32, (32, change.shape[1]), 0)
            lane = lax.broadcasted_iota(jnp.int32, (32, change.shape[1]), 1)
            change = jnp.where(lane // outs == tap, change, 0.0)
            high = change.astype(jnp.bfloat16)
            low = (change - high.astype(jnp.float32)).astype(jnp.bfloat16)
            met = jnp.concatenate([blocks[-1][:, 96:]] * 2, 1).astype(jnp.bfloat16)
            change = jnp.concatenate([high, low], 0)
            lanes -= jnp.dot(met, change, preferred_element_type=jnp.float32) * scale
        for k in range(taps):
            out[k] = lanes[:, outs * k : outs * k + outs]


def unpack(half, part, final, ins, mids, scale, begun=()):
    return pl.pallas_call(
        functools.partial(unpack_kernel, scale),
        grid_spec=pltpu.PrefetchScalarGridSpec(
            num_scalar_prefetch=1,
            grid=(3,),
            in_specs=whole(2) + whole(len(begun), pl.ANY),
            out_specs=[
                pl.BlockSpec((9, ins // 2, mids), lambda a, half: (a, half[0], 0)),
                pl.BlockSpec((9, mids // 2, mids), lambda a, half: (a, half[0], 0)),
            ],
            scratch_shapes=[pltpu.VMEM((part.shape[0] * part.shape[1], 128), jnp.bfloat16)],
        ),
        out_shape=(
            jax.ShapeDtypeStruct((27, ins, mids), jnp.float32),
            jax.ShapeDtypeStruct((27, mids, mids), jnp.float32),
        ),
        input_output_aliases={3 + k: k for k in range(len(begun))},
        compiler_params=pltpu.CompilerParams(vmem_limit_bytes=VMEM_LIMIT),
        cost_estimate=pl.CostEstimate(flops=2**20, bytes_accessed=2**22, transcendentals=0),
        name="unpack",
    )(half, part, final, *begun)


def feature_grads_kernel(grad_pre, weight, out, wide):
    frames, rows, cols, outs = grad_pre.shape
    own, cells_in, cols_in, ins = out.shape
    by_tap = col_sums(wide, grad_pre[...].astype(jnp.float32).reshape(frames * rows, cols, outs))
    total = jnp.zeros((own * cells_in * cols_in, ins), jnp.float32)
    for b in range(3):
        for e in range(3):
            part = by_tap[e].reshape(frames, rows, cols // 2, outs)
            cells = jnp.stack(
                [part[:, 2 * k + 2 - b] + part[:, 2 * k + 3 - b] for k in range(cells_in)], 1
            ).astype(jnp.bfloat16)
            for a in range(3):
                total += lax.dot_general(
                    cells[2 - a : 2 - a + own].reshape(-1, outs),
                    weight[a, b, e],
                    (((1,), (1,)), ((), ())),
                    preferred_element_type=jnp.float32,
                )
    out[...] = total.reshape(out.shape)


def feature_grads(grad_rowed, weight, shape):
    frames, rows, cols, _ = grad_rowed.shape
    return pl.pallas_call(
        feature_grads_kernel,
        out_shape=jax.ShapeDtypeStruct(shape, jnp.float32),
        in_specs=whole(2),
        out_specs=whole()[0],
        scratch_shapes=[pltpu.VMEM((frames * rows, cols + 16, 128), jnp.float32)],
        compiler_params=pltpu.CompilerParams(vmem_limit_bytes=VMEM_LIMIT),
        cost_estimate=pl.CostEstimate(flops=2**28, bytes_accessed=2**21, transcendentals=0),
        name="feature_grads",
    )(grad_rowed, weight)


SWAP = [(0, 1), (1, 0)]


def body(features, cotangent, weight_one, weight_two, norm_gain, norm_shift):
    frames, ins = features.shape[0], features.shape[-1]
    rows, cols, mids = cotangent.shape[1:]
    xs, rest, height = lax.axis_size("x"), lax.axis_size(REST), lax.axis_size(HEIGHT)
    cells = frames * rows * cols * 2 * xs * rest
    count = cells * (mids // GROUPS)
    at_row = lax.axis_index(HEIGHT)
    owned = lax.axis_index("x") * rest + lax.axis_index(REST)
    where = jnp.stack([lax.axis_index("c"), at_row == 0, at_row == height - 1, owned]).astype(jnp.int32)
    barrier = lax.optimization_barrier

    def exchange(copies, axes):
        return lax.all_to_all(copies, axes, 0, 0)

    def spread(value, copies):
        return jnp.broadcast_to(value[None], (copies,) + value.shape)

    cache = neighbour(features, TM, 1)
    later = neighbour(cotangent, TM, -1)

    features, cotangent = resident(features, cotangent)
    downward, upward = edges(cache, features, cotangent, later)
    downward, upward, weight_one, weight_two = barrier((downward, upward, weight_one, weight_two))
    weight_one, weight_two = resident(weight_one, weight_two)
    above = neighbour(downward, HEIGHT, 1)
    below = neighbour(upward, HEIGHT, -1)
    pre_norm, sums = conv_one(cache, features, above, below, weight_one, cotangent, height)
    came = exchange(sums, HEIGHT)
    grad_hidden, all_taps = hidden_grads(cotangent, later, above, below, weight_two)
    sums, grad_hidden = barrier((came.sum(0), grad_hidden))
    came = exchange(spread(sums, lax.axis_size(TM)), TM)
    hidden, grad_normed, normed, vectors = middle(
        count, where, came, pre_norm, grad_hidden, all_taps, norm_gain, norm_shift
    )
    local_two = second_weight(hidden, cotangent, later, above, below)

    scale = 1.0 / cells**0.5
    part_rows = -(-21 * ins // (2 * 8 * xs * rest)) * 8 * rest
    away, kept = weight_grads(
        where, cache, features, above, below, grad_normed, normed, vectors, local_two, xs, part_rows
    )
    part = add_pair(kept, lax.ppermute(away, "c", SWAP))
    part, hidden = barrier((part, hidden))
    part = add_row(exchange(part, "x"))
    before = neighbour(hidden, TM, 1)
    part, before = barrier((part, before))
    came = exchange(part.reshape(rest, -1, 3, 8, 128), REST)
    decoded = conv(
        jnp.pad(jnp.concatenate([before, hidden], 0), ((0, 0), (0, 0), (1, 1), (0, 0))), weight_two
    ).astype(jnp.bfloat16)
    came, decoded = barrier((came, decoded))
    part, final = combine(count, ins, where, came, vectors)
    grad_pre = grad_before_norm(where, grad_normed, normed, vectors, final)
    part = exchange(spread(part, rest), REST)
    after = neighbour(grad_pre, TM, -1)
    part, after = barrier((part, after))
    part = jnp.concatenate([part[:, :, :8].reshape(-1, 128), part[:, :, 8:].reshape(-1, 128)], 0)
    part = exchange(spread(part, xs), "x")
    grad_features = feature_grads(jnp.concatenate([grad_pre, after], 0), weight_one, features.shape)
    part, grad_features = barrier((part, grad_features))
    other = lax.ppermute(part, "c", SWAP)
    core = where[:1]
    begun = unpack(core, part, final, ins, mids, scale)
    grad_one, grad_two = unpack(1 - core, other, final, ins, mids, scale, begun)
    return decoded, grad_features, grad_one.reshape(weight_one.shape), grad_two.reshape(weight_two.shape)


def solution(mesh):
    split = P(TM, HEIGHT, None, None)
    return jax.shard_map(
        body,
        mesh=fine_mesh(mesh),
        in_specs=(split, split, P(), P(), P(), P()),
        out_specs=(split, split, P(), P()),
        check_vma=False,
    )
```

```python
import functools

import jax
import jax.numpy as jnp
from jax import lax
from jax.experimental import pallas as pl
from jax.experimental.pallas import tpu as pltpu
from jax.sharding import Mesh
from jax.sharding import PartitionSpec as P

GROUPS = 32
EPSILON = 1e-05

TM = ("zh", "y")
HEIGHT = ("zl", "x", "c")
REST = ("zh", "y", "zl")

VMEM_LIMIT = 32 * 2**20


def fine_mesh(mesh):
    tm, height = mesh.shape["tm"], mesh.shape["height"]
    zh = 2 if tm % 2 == 0 else 1
    core = 2
    x = 4 if height % 8 == 0 else height // 2
    return Mesh(mesh.devices.reshape(zh, tm // zh, height // (core * x), x, core), TM + HEIGHT)


def neighbour(value, axis, steps):
    count = lax.axis_size(axis)
    first, last = max(0, -steps), min(count, count - steps)
    return lax.ppermute(value, axis, [(i, i + steps) for i in range(first, last)])


def conv(padded, weight):
    return lax.conv_general_dilated(
        padded[None],
        weight,
        (1, 1, 1),
        "VALID",
        dimension_numbers=("NDHWC", "DHWIO", "NDHWC"),
        preferred_element_type=jnp.float32,
    )[0]


def whole(count=1, space=pltpu.VMEM):
    return [pl.BlockSpec(memory_space=space)] * count


def group_sums(first, second, outs):
    member = lax.broadcasted_iota(jnp.int32, (2, outs, outs), 1) // (outs // GROUPS)
    other = lax.broadcasted_iota(jnp.int32, (2, outs, outs), 2) // (outs // GROUPS)
    same = (member[0] == other[0]).astype(jnp.float32)
    both = jnp.concatenate([first, second, jnp.zeros((6, outs), jnp.float32)], 0)
    return jnp.dot(both, same, precision=lax.Precision.HIGHEST, preferred_element_type=jnp.float32)[:2]


def cell_sums(field):
    return jnp.sum(field.reshape(-1, field.shape[-1]), 0, keepdims=True)


def inside(where, field):
    row = lax.broadcasted_iota(jnp.int32, field.shape, 1)
    last = field.shape[1] - 1
    out = ((row == 0) & (where[1] == 1)) | ((row == last) & (where[2] == 1))
    return jnp.where(out, 0.0, field)


def resident_kernel(*refs):
    count = len(refs) // 2
    sems = refs[-1]
    moves = [pltpu.make_async_copy(refs[k], refs[count + k], sems.at[k]) for k in range(count)]
    for move in moves:
        move.start()
    for move in moves:
        move.wait()


def resident(*arrays):
    count = len(arrays)
    return pl.pallas_call(
        resident_kernel,
        out_shape=[jax.ShapeDtypeStruct(k.shape, k.dtype) for k in arrays],
        in_specs=whole(count, pltpu.HBM),
        out_specs=whole(count),
        scratch_shapes=[pltpu.SemaphoreType.DMA((count,))],
        compiler_params=pltpu.CompilerParams(vmem_limit_bytes=VMEM_LIMIT),
        cost_estimate=pl.CostEstimate(flops=0, bytes_accessed=2**22, transcendentals=0),
        name="resident",
    )(*arrays)


def edges_kernel(cache, features, cot, later, downward, upward):
    cells, rows = features.shape[1], cot.shape[1]
    half = features.shape[2]
    for out, cell, row in ((downward, cells - 1, rows - 2), (upward, 0, 0)):
        out[:, :half] = jnp.concatenate([cache[:, cell], features[:, cell]], 0)
        pair = [jnp.concatenate([cot[:, k], later[:, k]], 0) for k in (row, row + 1)]
        out[:, half:] = jnp.concatenate(pair, 2)


def edges(cache, features, cot, later):
    frames, _, half, ins = features.shape
    shape = jax.ShapeDtypeStruct((2 * frames, half + cot.shape[2], ins), jnp.bfloat16)
    return pl.pallas_call(
        edges_kernel,
        out_shape=(shape, shape),
        in_specs=whole(4),
        out_specs=whole(2),
        compiler_params=pltpu.CompilerParams(vmem_limit_bytes=VMEM_LIMIT),
        name="edges",
    )(cache, features, cot, later)


def conv_one_kernel(cache, features, above, below, weight, cot, pre_norm, sums, wide):
    frames, rows, cols, outs = pre_norm.shape
    cells_in, half, ins = features.shape[1], cols // 2, features.shape[-1]
    timed = jnp.concatenate([cache[...], features[...]], 0)
    rowed = jnp.concatenate([above[:, :half][:, None], timed, below[:, :half][:, None]], 1)
    by_tap = []
    for e in range(3):
        total = jnp.zeros((frames, rows, half, outs), jnp.float32)
        for b in range(3):
            product = sum(
                jnp.dot(
                    rowed[a : a + frames].reshape(-1, ins),
                    weight[a, b, e],
                    preferred_element_type=jnp.float32,
                )
                for a in range(3)
            ).reshape(frames, cells_in + 2, half, outs)
            total += jnp.stack([product[:, (r + b) // 2] for r in range(rows)], 1)
        by_tap.append(total.reshape(frames * rows, half, outs))
    wide[...] = jnp.zeros_like(wide)
    wide[:, 8 : 8 + half, :outs] = by_tap[0]
    even = wide[:, 7 : 7 + half, :outs] + by_tap[1] + by_tap[2]
    wide[:, 8 : 8 + half, :outs] = by_tap[2]
    odd = by_tap[0] + by_tap[1] + wide[:, 9 : 9 + half, :outs]
    wide[:, pl.ds(0, half, stride=2), :outs] = even
    wide[:, pl.ds(1, half, stride=2), :outs] = odd
    pre = wide[:, :cols, :outs].reshape(pre_norm.shape)
    pre_norm[...] = pre
    own = pre[:, 1:-1]
    both = group_sums(cell_sums(own), cell_sums(own * own), outs)
    sums[...] = jnp.concatenate([both, cell_sums(cot[...].astype(jnp.float32)), jnp.zeros((5, outs), jnp.float32)], 0)


def conv_one(cache, features, above, below, weight, cot):
    frames, cells_in, half, _ = features.shape
    outs = weight.shape[-1]
    rows, cols = 2 * cells_in + 2, 2 * half
    return pl.pallas_call(
        conv_one_kernel,
        out_shape=(
            jax.ShapeDtypeStruct((frames, rows, cols, outs), jnp.float32),
            jax.ShapeDtypeStruct((8, outs), jnp.float32),
        ),
        in_specs=whole(6),
        out_specs=whole(2),
        scratch_shapes=[pltpu.VMEM((frames * rows, cols + 16, 128), jnp.float32)],
        compiler_params=pltpu.CompilerParams(vmem_limit_bytes=VMEM_LIMIT),
        name="conv_one",
    )(cache, features, above, below, weight, cot)


def fill_cot(wide, cot, later, above, below):
    cols, outs = cot.shape[2:]
    half = cols // 2
    timed = jnp.concatenate([cot[...], later[...]], 0)
    pair = lambda part: jnp.stack([part[:, half:, :outs], part[:, half:, outs:]], 1)
    rowed = jnp.concatenate([pair(above), timed, pair(below)], 1).astype(jnp.float32)
    wide[...] = jnp.zeros_like(wide)
    wide[:, 8 : 8 + cols, :outs] = rowed.reshape(-1, cols, outs)


def col_tap(wide, e, shape):
    part = wide[:, 9 - e : 9 - e + shape[2], : shape[3]].astype(jnp.bfloat16)
    return part.reshape(2 * shape[0], shape[1] + 4, shape[2], shape[3])


def grad_hidden_kernel(cot, later, above, below, weight, grad_hidden, all_taps, wide):
    frames, rows, cols, ins = grad_hidden.shape
    outs = cot.shape[-1]
    fill_cot(wide, cot, later, above, below)
    total = jnp.zeros((frames * rows * cols, ins), jnp.float32)
    for e in range(3):
        part = col_tap(wide, e, cot.shape)
        for a in range(3):
            for b in range(3):
                total += lax.dot_general(
                    part[2 - a : 2 - a + frames, 2 - b : 2 - b + rows].reshape(-1, outs),
                    weight[a, b, e],
                    (((1,), (1,)), ((), ())),
                    preferred_element_type=jnp.float32,
                )
    grad_hidden[...] = total.reshape(grad_hidden.shape)
    all_taps[...] = sum(
        weight[a, b, e].astype(jnp.float32) for a in range(3) for b in range(3) for e in range(3)
    )


def hidden_grads(cot, later, above, below, weight):
    frames, rows, cols, outs = cot.shape
    return pl.pallas_call(
        grad_hidden_kernel,
        out_shape=(
            jax.ShapeDtypeStruct((frames, rows + 2, cols, weight.shape[-2]), jnp.float32),
            jax.ShapeDtypeStruct(weight.shape[-2:], jnp.float32),
        ),
        in_specs=whole(5),
        out_specs=whole(2),
        scratch_shapes=[pltpu.VMEM((2 * frames * (rows + 4), cols + 16, 128), jnp.float32)],
        compiler_params=pltpu.CompilerParams(vmem_limit_bytes=VMEM_LIMIT),
        cost_estimate=pl.CostEstimate(flops=2**30, bytes_accessed=2**21, transcendentals=0),
        name="grad_hidden",
    )(cot, later, above, below, weight)


def middle_kernel(count, where, known, pre_norm, grad_hidden, all_taps, hidden, grad_normed, normed, vectors):
    outs = pre_norm.shape[-1]
    total, gain, shift = known[:3], known[4:5], known[5:6]
    mean = total[:1] / count
    scaled = lax.rsqrt(total[1:2] / count - mean * mean + EPSILON)
    flat = (pre_norm[...].reshape(-1, outs) - mean) * scaled
    shifted = flat * gain + shift
    sigma = 1.0 / (1.0 + jnp.exp(-shifted))
    hidden[...] = inside(where, (shifted * sigma).reshape(pre_norm.shape)).astype(jnp.bfloat16)
    grad = grad_hidden[...].reshape(-1, outs) * sigma * (1.0 + shifted * (1.0 - sigma)) * gain
    grad, flat = grad.reshape(pre_norm.shape), flat.reshape(pre_norm.shape)
    grad_normed[...] = grad
    normed[...] = flat
    own = grad[:, 1:-1]

    cells = count / (outs // GROUPS)
    level = lax.dot_general(
        total[2:3] / cells,
        all_taps[...],
        (((1,), (1,)), ((), ())),
        precision=lax.Precision.HIGHEST,
        preferred_element_type=jnp.float32,
    )
    at = lax.broadcasted_iota(jnp.int32, (16, outs), 0).astype(jnp.float32) * 0.45 - 3.375
    share = jnp.exp(-0.5 * at * at)
    share = share / jnp.sum(share, 0, keepdims=True)
    point = at * gain + shift
    slope = 1.0 / (1.0 + jnp.exp(-point))
    slope = slope * (1.0 + point * (1.0 - slope)) * share
    level = level * gain * (cells / count)
    offsets = group_sums(
        level * jnp.sum(slope, 0, keepdims=True), level * jnp.sum(slope * at, 0, keepdims=True), outs
    )
    rows = [scaled, offsets, cell_sums(own), cell_sums(own * flat[:, 1:-1])]
    vectors[...] = jnp.concatenate(rows + [jnp.zeros((3, outs), jnp.float32)], 0)


def middle(count, where, known, pre_norm, grad_hidden, all_taps):
    shape, outs = pre_norm.shape, pre_norm.shape[-1]
    return pl.pallas_call(
        functools.partial(middle_kernel, count),
        out_shape=(
            jax.ShapeDtypeStruct(shape, jnp.bfloat16),
            jax.ShapeDtypeStruct(shape, jnp.float32),
            jax.ShapeDtypeStruct(shape, jnp.float32),
            jax.ShapeDtypeStruct((8, outs), jnp.float32),
        ),
        in_specs=whole(1, pltpu.SMEM) + whole(4),
        out_specs=whole(4),
        compiler_params=pltpu.CompilerParams(vmem_limit_bytes=VMEM_LIMIT),
        name="middle",
    )(where, known, pre_norm, grad_hidden, all_taps)


def second_weight_kernel(hidden, cot, later, above, below, out, wide):
    frames, rows, cols, ins = hidden.shape
    outs = cot.shape[-1]
    own = hidden[:, 1:-1].reshape(-1, ins).astype(jnp.float32).T.astype(jnp.bfloat16)
    fill_cot(wide, cot, later, above, below)
    shifted = [col_tap(wide, e, cot.shape) for e in range(3)]
    for a in range(3):
        pieces = [
            shifted[e][2 - a : 2 - a + frames, 3 - b : 3 - b + rows - 2].reshape(-1, outs)
            for b in range(3)
            for e in range(3)
        ]
        pieces.append(jnp.zeros((pieces[0].shape[0], 32), jnp.bfloat16))
        out[a] = jnp.dot(own, jnp.concatenate(pieces, 1), preferred_element_type=jnp.float32)


def second_weight(hidden, cot, later, above, below):
    frames, rows, cols, _ = cot.shape
    return pl.pallas_call(
        second_weight_kernel,
        out_shape=jax.ShapeDtypeStruct((3, hidden.shape[-1], 896), jnp.float32),
        in_specs=whole(5),
        out_specs=whole()[0],
        scratch_shapes=[pltpu.VMEM((2 * frames * (rows + 4), cols + 16, 128), jnp.float32)],
        compiler_params=pltpu.CompilerParams(vmem_limit_bytes=VMEM_LIMIT),
        name="second_weight",
    )(hidden, cot, later, above, below)


def col_sums(wide, cells):
    half = cells.shape[1] // 2
    wide[...] = jnp.zeros_like(wide)
    wide[:, 8 : 8 + cells.shape[1], : cells.shape[2]] = cells

    def every_second(start):
        return wide[:, pl.ds(start, half, stride=2), : cells.shape[2]]

    before, even, odd, after = (every_second(7 + k) for k in range(4))
    return odd + after, even + odd, before + even


def group_lanes(outs, first):
    lane = lax.broadcasted_iota(jnp.int32, (outs, 128), 1)
    group = lax.broadcasted_iota(jnp.int32, (outs, 128), 0) // (outs // GROUPS)
    return (lane == group + (64 if first else 64 + GROUPS)).astype(jnp.float32)


def exact(left, right, dims):
    return lax.dot_general(
        left, right, (dims, ((), ())), precision=lax.Precision.HIGHEST, preferred_element_type=jnp.float32
    )


def in_parts(sums, rows):
    high = sums.astype(jnp.bfloat16).astype(jnp.float32)
    middle = (sums - high).astype(jnp.bfloat16).astype(jnp.float32)
    low = sums - high - middle
    row = lax.broadcasted_iota(jnp.int32, (rows, 128), 0)
    return jnp.where(row == 0, high, jnp.where(row == 1, middle, jnp.where(row == 2, low, 0.0)))


def sums_of(tile):
    return tile[0:1] + tile[1:2] + tile[2:3]


def weight_grads_kernel(where, cache, features, above, below, grad_normed, normed, vectors, two, away, kept, wide):
    frames, rows, cols, outs = grad_normed.shape
    rows, half = rows - 2, cols // 2
    ins, mids, pieces, part_rows = features.shape[-1], two.shape[1], kept.shape[0], (kept.shape[1] - 16) * 2 // 5
    timed = jnp.concatenate([cache[...], features[...]], 0)
    rows_in = jnp.concatenate([above[:, :half][:, None], timed, below[:, :half][:, None]], 1)
    rstd, f0, s0 = (vectors[k : k + 1] for k in range(3))
    own = normed[:, 1:-1].reshape(-1, outs)
    grad = (grad_normed[:, 1:-1].reshape(-1, outs) - f0 - own * s0) * rstd
    lower = where[0] == 0

    def pool(field, last):
        by_tap = col_sums(wide, field.reshape(frames * rows, cols, outs))
        taps = []
        for b in range(3):
            for e in range(3):
                part = by_tap[e].reshape(frames, rows, half, outs)
                none = jnp.zeros_like(part[:, 0])
                r = [part[:, k] for k in range(rows)]
                stacked = (
                    [r[0], r[1] + r[2], r[3], none],
                    [none, r[0] + r[1], r[2] + r[3], none],
                    [none, r[0], r[1] + r[2], r[3]],
                )[b]
                taps.append(jnp.stack(stacked, 1).astype(jnp.bfloat16).reshape(-1, outs))
        return jnp.concatenate(taps + [last], 1)

    at = lax.broadcasted_iota(jnp.int32, (frames * 4 * half, 32), 0)
    tap = lax.broadcasted_iota(jnp.int32, (frames * 4 * half, 32), 1)
    b, e, row, col = tap // 3, tap % 3, at // half % 4, at % half
    two_rows = (row == 1) & (b < 2) | (row == 2) & (b > 0)
    one_row = (row == 0) & (b == 0) | (row == 2) & (b == 0) | (row == 1) & (b == 2) | (row == 3) & (b == 2)
    in_rows = jnp.where(two_rows, 2.0, jnp.where(one_row, 1.0, 0.0))
    in_cols = jnp.where((e == 0) & (col == half - 1) | (e == 2) & (col == 0), 1.0, 2.0)
    counts = jnp.where(tap < 9, in_rows * in_cols, 0.0).astype(jnp.bfloat16)

    def write(part, at, low, high):
        deep = part_rows if part < 2 else part_rows // 2
        while low.shape[0]:
            x, row = at // deep, part_rows * part + at % deep
            n = min(low.shape[0], deep - at % deep)
            away[x, row : row + n] = jnp.where(lower, high[:n], low[:n]).astype(jnp.bfloat16)
            kept[x, row : row + n] = jnp.where(lower, low[:n], high[:n])
            low, high, at = low[n:], high[n:], at + n

    for part, field, last in ((0, grad, counts), (1, own * rstd, jnp.zeros_like(counts))):
        cells = pool(field, last)
        at = 0
        for a in range(3):
            product = lax.dot_general(
                rows_in[a : a + frames].reshape(-1, ins),
                cells,
                (((0,), (0,)), ((), ())),
                preferred_element_type=jnp.float32,
            )
            for j in range(7):
                block = product[:, 128 * j : 128 * j + 128]
                write(part, at, block[: ins // 2], block[ins // 2 :])
                at += ins // 2
        nothing = jnp.zeros((pieces * part_rows - at, 128), jnp.float32)
        write(part, at, nothing, nothing)

    sums = exact(vectors[3:4], group_lanes(outs, True), ((1,), (0,)))
    sums += exact(vectors[4:5], group_lanes(outs, False), ((1,), (0,)))
    sums = in_parts(sums, 16)
    at = 0
    for a in range(3):
        for j in range(7):
            block = two[a, :, 128 * j : 128 * j + 128]
            write(2, at, block[: mids // 2], block[mids // 2 :])
            at += mids // 2
    nothing = jnp.zeros((pieces * part_rows // 2 - at, 128), jnp.float32)
    write(2, at, nothing, nothing)
    for x in range(pieces):
        away[x, part_rows * 5 // 2 :] = sums.astype(jnp.bfloat16)
        kept[x, part_rows * 5 // 2 :] = sums


def weight_grads(where, cache, features, above, below, grad_normed, normed, vectors, two, pieces, part_rows):
    frames, rows, cols, _ = grad_normed.shape
    shape = (pieces, part_rows * 5 // 2 + 16, 128)
    return pl.pallas_call(
        weight_grads_kernel,
        out_shape=(jax.ShapeDtypeStruct(shape, jnp.bfloat16), jax.ShapeDtypeStruct(shape, jnp.float32)),
        in_specs=whole(1, pltpu.SMEM) + whole(8),
        out_specs=whole(2),
        scratch_shapes=[pltpu.VMEM((frames * (rows - 2), cols + 16, 128), jnp.float32)],
        compiler_params=pltpu.CompilerParams(vmem_limit_bytes=VMEM_LIMIT),
        name="weight_grads",
    )(where, cache, features, above, below, grad_normed, normed, vectors, two)


def add_pair_kernel(kept, came, out, total, sems):
    deep = kept.shape[1] - 16
    sums = in_parts(sums_of(kept[0, deep:] + came[0, deep:].astype(jnp.float32)), 16).astype(jnp.bfloat16)
    moves = []
    for x in range(kept.shape[0]):
        total[x, :deep] = (kept[x, :deep] + came[x, :deep].astype(jnp.float32)).astype(jnp.bfloat16)
        total[x, deep:] = sums
        moves.append(pltpu.make_async_copy(total.at[x], out.at[x], sems.at[x]))
        moves[x].start()
    for move in moves:
        move.wait()


def add_pair(kept, came):
    return pl.pallas_call(
        add_pair_kernel,
        out_shape=jax.ShapeDtypeStruct(kept.shape, jnp.bfloat16),
        in_specs=whole(2),
        out_specs=whole(1, pltpu.HBM)[0],
        scratch_shapes=[pltpu.VMEM(kept.shape, jnp.bfloat16), pltpu.SemaphoreType.DMA((kept.shape[0],))],
        compiler_params=pltpu.CompilerParams(vmem_limit_bytes=VMEM_LIMIT),
        name="add_pair",
    )(kept, came)


def add_row_kernel(came, out):
    total = jnp.sum(came[...].astype(jnp.float32), 0)
    n = out.shape[0] * 8
    tiles = total[2 * n : n * 5 // 2].reshape(-1, 8, 128)
    row = lax.broadcasted_iota(jnp.int32, (1, 8, 128), 1)
    lane = lax.broadcasted_iota(jnp.int32, (1, 8, 128), 2)
    turned = jnp.concatenate([tiles[:, 4:], tiles[:, :4]], 1)
    swap = lambda k: jnp.concatenate([k[..., 64:], k[..., :64]], 2)
    even = jnp.where(row < 4, tiles, swap(turned))
    odd = jnp.where(row < 4, turned, swap(tiles))
    both = jnp.stack([even, odd], 1).reshape(-1, 8, 128)
    sums = in_parts(sums_of(total[n * 5 // 2 :]), 8)
    both = jnp.where(lane < 64, both, sums[None])
    parts = [total[:n].reshape(-1, 8, 128), total[n : 2 * n].reshape(-1, 8, 128), both, jnp.zeros_like(both)]
    out[...] = jnp.concatenate(parts, 1).astype(jnp.bfloat16)


def add_row(came):
    tiles = (came.shape[1] - 16) // 20
    return pl.pallas_call(
        add_row_kernel,
        out_shape=jax.ShapeDtypeStruct((tiles, 32, 128), jnp.bfloat16),
        in_specs=whole(1),
        out_specs=whole()[0],
        compiler_params=pltpu.CompilerParams(vmem_limit_bytes=VMEM_LIMIT),
        name="add_row",
    )(came)


def combine_kernel(count, tiles_per_block, where, came, vectors, piece, final, lanes):
    outs = vectors.shape[1]
    total = jnp.sum(came[...].astype(jnp.float32), 0)
    sums = sums_of(total[0, 16:]) / count
    first = exact(sums, group_lanes(outs, True), ((1,), (1,)))
    second = exact(sums, group_lanes(outs, False), ((1,), (1,)))
    rest = (first - vectors[1:2]) * vectors[0:1]
    final[...] = jnp.concatenate([first, second, rest, jnp.zeros((5, outs), jnp.float32)], 0)
    lane = lax.broadcasted_iota(jnp.int32, (outs, 896), 1)
    channel = lax.broadcasted_iota(jnp.int32, (outs, 896), 0)
    spread = ((lane % outs == channel) & (lane < 9 * outs)).astype(jnp.float32)
    lanes[...] = jnp.broadcast_to(exact(second - vectors[2:3], spread, ((1,), (0,))), lanes.shape)
    for k in range(piece.shape[0]):
        block = (where[3] * piece.shape[0] + k) // tiles_per_block % 7
        change = lanes[0:1, pl.ds(pl.multiple_of(block * 128, 128), 128)]
        upper = jnp.concatenate([total[k, 16:20, :64], total[k, 20:24, :64]], 1)
        grad = total[k, :8] - change * total[k, 8:16]
        piece[k] = jnp.concatenate([grad, upper, jnp.zeros_like(upper)], 0).astype(jnp.bfloat16)


def combine(count, ins, where, came, vectors):
    return pl.pallas_call(
        functools.partial(combine_kernel, count, ins // 16),
        out_shape=(
            jax.ShapeDtypeStruct((came.shape[1], 16, 128), jnp.bfloat16),
            jax.ShapeDtypeStruct(vectors.shape, jnp.float32),
        ),
        in_specs=whole(1, pltpu.SMEM) + whole(2),
        out_specs=whole(2),
        scratch_shapes=[pltpu.VMEM((8, 896), jnp.float32)],
        compiler_params=pltpu.CompilerParams(vmem_limit_bytes=VMEM_LIMIT),
        name="combine",
    )(where, came, vectors)


def grad_pre_kernel(where, grad_normed, normed, vectors, final, out):
    shape = grad_normed.shape
    flat = (-1, shape[-1])
    grad = grad_normed[...].reshape(flat) - final[:1] - normed[...].reshape(flat) * final[1:2]
    out[...] = inside(where, (grad * vectors[:1]).reshape(shape)).astype(jnp.bfloat16)


def grad_before_norm(where, grad_normed, normed, vectors, final):
    return pl.pallas_call(
        grad_pre_kernel,
        out_shape=jax.ShapeDtypeStruct(grad_normed.shape, jnp.bfloat16),
        in_specs=whole(1, pltpu.SMEM) + whole(4),
        out_specs=whole()[0],
        compiler_params=pltpu.CompilerParams(vmem_limit_bytes=VMEM_LIMIT),
        cost_estimate=pl.CostEstimate(flops=2**20, bytes_accessed=2**20, transcendentals=0),
        name="grad_pre",
    )(where, grad_normed, normed, vectors, final)


def unpack_kernel(scale, half, part, final, *rest):
    one, two, flat = rest[-3:]
    pieces, rows = part.shape[0], part.shape[1]
    split = rows * 2 // 3
    step = pl.program_id(0)

    @pl.when(step == 0)
    def _():
        for x in range(pieces):
            flat[split * x : split * (x + 1)] = part[x, :split]
            at = pieces * split + (rows - split) * x
            flat[at : at + rows - split] = part[x, split:]

    for out, begin in ((one, 0), (two, pieces * split)):
        taps, channels, outs = out.shape
        blocks = []
        for j in range(7):
            at = pl.multiple_of(begin + (step * 7 + j) * channels, 16)
            blocks.append(flat[pl.ds(at, channels)].astype(jnp.float32))
        lanes = jnp.concatenate(blocks, 1) * scale
        if out is one:
            change = jnp.concatenate([final[2:3]] * taps + [jnp.zeros((1, 32), jnp.float32)], 1)
            tap = lax.broadcasted_iota(jnp.int32, (32, change.shape[1]), 0)
            lane = lax.broadcasted_iota(jnp.int32, (32, change.shape[1]), 1)
            change = jnp.where(lane // outs == tap, change, 0.0)
            high = change.astype(jnp.bfloat16)
            low = (change - high.astype(jnp.float32)).astype(jnp.bfloat16)
            met = jnp.concatenate([blocks[-1][:, 96:]] * 2, 1).astype(jnp.bfloat16)
            change = jnp.concatenate([high, low], 0)
            lanes -= jnp.dot(met, change, preferred_element_type=jnp.float32) * scale
        for k in range(taps):
            out[k] = lanes[:, outs * k : outs * k + outs]


def unpack(half, part, final, ins, mids, scale, begun=()):
    return pl.pallas_call(
        functools.partial(unpack_kernel, scale),
        grid_spec=pltpu.PrefetchScalarGridSpec(
            num_scalar_prefetch=1,
            grid=(3,),
            in_specs=whole(2) + whole(len(begun), pl.ANY),
            out_specs=[
                pl.BlockSpec((9, ins // 2, mids), lambda a, half: (a, half[0], 0)),
                pl.BlockSpec((9, mids // 2, mids), lambda a, half: (a, half[0], 0)),
            ],
            scratch_shapes=[pltpu.VMEM((part.shape[0] * part.shape[1], 128), jnp.bfloat16)],
        ),
        out_shape=(
            jax.ShapeDtypeStruct((27, ins, mids), jnp.float32),
            jax.ShapeDtypeStruct((27, mids, mids), jnp.float32),
        ),
        input_output_aliases={3 + k: k for k in range(len(begun))},
        compiler_params=pltpu.CompilerParams(vmem_limit_bytes=VMEM_LIMIT),
        cost_estimate=pl.CostEstimate(flops=2**20, bytes_accessed=2**22, transcendentals=0),
        name="unpack",
    )(half, part, final, *begun)


def feature_grads_kernel(grad_pre, weight, out, wide):
    frames, rows, cols, outs = grad_pre.shape
    own, cells_in, cols_in, ins = out.shape
    by_tap = col_sums(wide, grad_pre[...].astype(jnp.float32).reshape(frames * rows, cols, outs))
    total = jnp.zeros((own * cells_in * cols_in, ins), jnp.float32)
    for b in range(3):
        for e in range(3):
            part = by_tap[e].reshape(frames, rows, cols // 2, outs)
            cells = jnp.stack(
                [part[:, 2 * k + 2 - b] + part[:, 2 * k + 3 - b] for k in range(cells_in)], 1
            ).astype(jnp.bfloat16)
            for a in range(3):
                total += lax.dot_general(
                    cells[2 - a : 2 - a + own].reshape(-1, outs),
                    weight[a, b, e],
                    (((1,), (1,)), ((), ())),
                    preferred_element_type=jnp.float32,
                )
    out[...] = total.reshape(out.shape)


def feature_grads(grad_rowed, weight, shape):
    frames, rows, cols, _ = grad_rowed.shape
    return pl.pallas_call(
        feature_grads_kernel,
        out_shape=jax.ShapeDtypeStruct(shape, jnp.float32),
        in_specs=whole(2),
        out_specs=whole()[0],
        scratch_shapes=[pltpu.VMEM((frames * rows, cols + 16, 128), jnp.float32)],
        compiler_params=pltpu.CompilerParams(vmem_limit_bytes=VMEM_LIMIT),
        cost_estimate=pl.CostEstimate(flops=2**28, bytes_accessed=2**21, transcendentals=0),
        name="feature_grads",
    )(grad_rowed, weight)


SWAP = [(0, 1), (1, 0)]


def body(features, cotangent, weight_one, weight_two, norm_gain, norm_shift):
    frames, ins = features.shape[0], features.shape[-1]
    rows, cols, mids = cotangent.shape[1:]
    xs, rest, height = lax.axis_size("x"), lax.axis_size(REST), lax.axis_size(HEIGHT)
    cells = frames * rows * cols * 2 * xs * rest
    count = cells * (mids // GROUPS)
    at_row = lax.axis_index(HEIGHT)
    owned = lax.axis_index("x") * rest + lax.axis_index(REST)
    where = jnp.stack([lax.axis_index("c"), at_row == 0, at_row == height - 1, owned]).astype(jnp.int32)
    barrier = lax.optimization_barrier

    def exchange(copies, axes):
        return lax.all_to_all(copies, axes, 0, 0)

    def spread(value, copies):
        return jnp.broadcast_to(value[None], (copies,) + value.shape)

    cache = neighbour(features, TM, 1)
    later = neighbour(cotangent, TM, -1)

    features, cotangent = resident(features, cotangent)
    downward, upward = edges(cache, features, cotangent, later)
    downward, upward, weight_one, weight_two = barrier((downward, upward, weight_one, weight_two))
    weight_one, weight_two = resident(weight_one, weight_two)
    above = neighbour(downward, HEIGHT, 1)
    below = neighbour(upward, HEIGHT, -1)
    pre_norm, sums = conv_one(cache, features, above, below, weight_one, cotangent)
    came = exchange(spread(sums[:4], height), HEIGHT)
    grad_hidden, all_taps = hidden_grads(cotangent, later, above, below, weight_two)
    sums, grad_hidden = barrier((came.sum(0), grad_hidden))
    came = exchange(spread(sums, lax.axis_size(TM)), TM)
    known = jnp.concatenate([came.sum(0), norm_gain[None], norm_shift[None], jnp.zeros((2, mids), jnp.float32)], 0)
    hidden, grad_normed, normed, vectors = middle(count, where, known, pre_norm, grad_hidden, all_taps)
    local_two = second_weight(hidden, cotangent, later, above, below)

    scale = 1.0 / cells**0.5
    part_rows = -(-21 * ins // (2 * 8 * xs * rest)) * 8 * rest
    away, kept = weight_grads(
        where, cache, features, above, below, grad_normed, normed, vectors, local_two, xs, part_rows
    )
    part = add_pair(kept, lax.ppermute(away, "c", SWAP))
    part, hidden = barrier((part, hidden))
    part = add_row(exchange(part, "x"))
    before = neighbour(hidden, TM, 1)
    part, before = barrier((part, before))
    came = exchange(part.reshape(rest, -1, 32, 128), REST)
    decoded = conv(
        jnp.pad(jnp.concatenate([before, hidden], 0), ((0, 0), (0, 0), (1, 1), (0, 0))), weight_two
    ).astype(jnp.bfloat16)
    came, decoded = barrier((came, decoded))
    part, final = combine(count, ins, where, came, vectors)
    grad_pre = grad_before_norm(where, grad_normed, normed, vectors, final)
    part = exchange(spread(part[:, :12], rest), REST)
    after = neighbour(grad_pre, TM, -1)
    part, after = barrier((part, after))
    part = jnp.concatenate([part[:, :, :8].reshape(-1, 128), part[:, :, 8:].reshape(-1, 128)], 0)
    part = exchange(spread(part, xs), "x")
    grad_features = feature_grads(jnp.concatenate([grad_pre, after], 0), weight_one, features.shape)
    part, grad_features = barrier((part, grad_features))
    other = lax.ppermute(part, "c", SWAP)
    core = where[:1]
    begun = unpack(core, part, final, ins, mids, scale)
    grad_one, grad_two = unpack(1 - core, other, final, ins, mids, scale, begun)
    return decoded, grad_features, grad_one.reshape(weight_one.shape), grad_two.reshape(weight_two.shape)


def solution(mesh):
    split = P(TM, HEIGHT, None, None)
    return jax.shard_map(
        body,
        mesh=fine_mesh(mesh),
        in_specs=(split, split, P(), P(), P(), P()),
        out_specs=(split, split, P(), P()),
        check_vma=False,
    )
```

```python
import functools

import jax
import jax.numpy as jnp
from jax import lax
from jax.experimental import pallas as pl
from jax.experimental.pallas import tpu as pltpu
from jax.sharding import Mesh
from jax.sharding import PartitionSpec as P

GROUPS = 32
EPSILON = 1e-05

TM = ("zh", "y")
HEIGHT = ("zl", "x", "c")
REST = ("zh", "y", "zl")

VMEM_LIMIT = 32 * 2**20


def fine_mesh(mesh):
    tm, height = mesh.shape["tm"], mesh.shape["height"]
    zh = 2 if tm % 2 == 0 else 1
    core = 2
    x = 4 if height % 8 == 0 else height // 2
    return Mesh(mesh.devices.reshape(zh, tm // zh, height // (core * x), x, core), TM + HEIGHT)


def neighbour(value, axis, steps):
    count = lax.axis_size(axis)
    first, last = max(0, -steps), min(count, count - steps)
    return lax.ppermute(value, axis, [(i, i + steps) for i in range(first, last)])


def conv(padded, weight):
    return lax.conv_general_dilated(
        padded[None],
        weight,
        (1, 1, 1),
        "VALID",
        dimension_numbers=("NDHWC", "DHWIO", "NDHWC"),
        preferred_element_type=jnp.float32,
    )[0]


def whole(count=1, space=pltpu.VMEM):
    return [pl.BlockSpec(memory_space=space)] * count


def group_sums(first, second, outs):
    member = lax.broadcasted_iota(jnp.int32, (2, outs, outs), 1) // (outs // GROUPS)
    other = lax.broadcasted_iota(jnp.int32, (2, outs, outs), 2) // (outs // GROUPS)
    same = (member[0] == other[0]).astype(jnp.float32)
    both = jnp.concatenate([first, second, jnp.zeros((6, outs), jnp.float32)], 0)
    return jnp.dot(both, same, precision=lax.Precision.HIGHEST, preferred_element_type=jnp.float32)[:2]


def cell_sums(field):
    return jnp.sum(field.reshape(-1, field.shape[-1]), 0, keepdims=True)


def inside(where, field):
    row = lax.broadcasted_iota(jnp.int32, field.shape, 1)
    last = field.shape[1] - 1
    out = ((row == 0) & (where[1] == 1)) | ((row == last) & (where[2] == 1))
    return jnp.where(out, 0.0, field)


def resident_kernel(*refs):
    count = len(refs) // 2
    sems = refs[-1]
    moves = [pltpu.make_async_copy(refs[k], refs[count + k], sems.at[k]) for k in range(count)]
    for move in moves:
        move.start()
    for move in moves:
        move.wait()


def resident(*arrays):
    count = len(arrays)
    return pl.pallas_call(
        resident_kernel,
        out_shape=[jax.ShapeDtypeStruct(k.shape, k.dtype) for k in arrays],
        in_specs=whole(count, pltpu.HBM),
        out_specs=whole(count),
        scratch_shapes=[pltpu.SemaphoreType.DMA((count,))],
        compiler_params=pltpu.CompilerParams(vmem_limit_bytes=VMEM_LIMIT),
        cost_estimate=pl.CostEstimate(flops=0, bytes_accessed=2**22, transcendentals=0),
        name="resident",
    )(*arrays)


def edges_kernel(cache, features, cot, later, downward, upward):
    cells, rows = features.shape[1], cot.shape[1]
    half = features.shape[2]
    for out, cell, row in ((downward, cells - 1, rows - 2), (upward, 0, 0)):
        out[:, :half] = jnp.concatenate([cache[:, cell], features[:, cell]], 0)
        pair = [jnp.concatenate([cot[:, k], later[:, k]], 0) for k in (row, row + 1)]
        out[:, half:] = jnp.concatenate(pair, 2)


def edges(cache, features, cot, later):
    frames, _, half, ins = features.shape
    shape = jax.ShapeDtypeStruct((2 * frames, half + cot.shape[2], ins), jnp.bfloat16)
    return pl.pallas_call(
        edges_kernel,
        out_shape=(shape, shape),
        in_specs=whole(4),
        out_specs=whole(2),
        compiler_params=pltpu.CompilerParams(vmem_limit_bytes=VMEM_LIMIT),
        name="edges",
    )(cache, features, cot, later)


def conv_one_kernel(cache, features, above, below, weight, cot, pre_norm, sums, wide):
    frames, rows, cols, outs = pre_norm.shape
    cells_in, half, ins = features.shape[1], cols // 2, features.shape[-1]
    timed = jnp.concatenate([cache[...], features[...]], 0)
    rowed = jnp.concatenate([above[:, :half][:, None], timed, below[:, :half][:, None]], 1)
    by_tap = []
    for e in range(3):
        total = jnp.zeros((frames, rows, half, outs), jnp.float32)
        for b in range(3):
            product = sum(
                jnp.dot(
                    rowed[a : a + frames].reshape(-1, ins),
                    weight[a, b, e],
                    preferred_element_type=jnp.float32,
                )
                for a in range(3)
            ).reshape(frames, cells_in + 2, half, outs)
            total += jnp.stack([product[:, (r + b) // 2] for r in range(rows)], 1)
        by_tap.append(total.reshape(frames * rows, half, outs))
    wide[...] = jnp.zeros_like(wide)
    wide[:, 8 : 8 + half, :outs] = by_tap[0]
    even = wide[:, 7 : 7 + half, :outs] + by_tap[1] + by_tap[2]
    wide[:, 8 : 8 + half, :outs] = by_tap[2]
    odd = by_tap[0] + by_tap[1] + wide[:, 9 : 9 + half, :outs]
    wide[:, pl.ds(0, half, stride=2), :outs] = even
    wide[:, pl.ds(1, half, stride=2), :outs] = odd
    pre = wide[:, :cols, :outs].reshape(pre_norm.shape)
    pre_norm[...] = pre
    own = pre[:, 1:-1]
    both = group_sums(cell_sums(own), cell_sums(own * own), outs)
    both = jnp.concatenate([both, cell_sums(cot[...].astype(jnp.float32)), jnp.zeros((1, outs), jnp.float32)], 0)
    sums[...] = jnp.broadcast_to(both[None], sums.shape)


def conv_one(cache, features, above, below, weight, cot, copies):
    frames, cells_in, half, _ = features.shape
    outs = weight.shape[-1]
    rows, cols = 2 * cells_in + 2, 2 * half
    return pl.pallas_call(
        conv_one_kernel,
        out_shape=(
            jax.ShapeDtypeStruct((frames, rows, cols, outs), jnp.float32),
            jax.ShapeDtypeStruct((copies, 4, outs), jnp.float32),
        ),
        in_specs=whole(6),
        out_specs=whole(2),
        scratch_shapes=[pltpu.VMEM((frames * rows, cols + 16, 128), jnp.float32)],
        compiler_params=pltpu.CompilerParams(vmem_limit_bytes=VMEM_LIMIT),
        name="conv_one",
    )(cache, features, above, below, weight, cot)


def fill_cot(wide, cot, later, above, below):
    cols, outs = cot.shape[2:]
    half = cols // 2
    timed = jnp.concatenate([cot[...], later[...]], 0)
    pair = lambda part: jnp.stack([part[:, half:, :outs], part[:, half:, outs:]], 1)
    rowed = jnp.concatenate([pair(above), timed, pair(below)], 1).astype(jnp.float32)
    wide[...] = jnp.zeros_like(wide)
    wide[:, 8 : 8 + cols, :outs] = rowed.reshape(-1, cols, outs)


def col_tap(wide, e, shape):
    part = wide[:, 9 - e : 9 - e + shape[2], : shape[3]].astype(jnp.bfloat16)
    return part.reshape(2 * shape[0], shape[1] + 4, shape[2], shape[3])


def grad_hidden_kernel(cot, later, above, below, weight, grad_hidden, all_taps, wide):
    frames, rows, cols, ins = grad_hidden.shape
    outs = cot.shape[-1]
    fill_cot(wide, cot, later, above, below)
    total = jnp.zeros((frames * rows * cols, ins), jnp.float32)
    for e in range(3):
        part = col_tap(wide, e, cot.shape)
        for a in range(3):
            for b in range(3):
                total += lax.dot_general(
                    part[2 - a : 2 - a + frames, 2 - b : 2 - b + rows].reshape(-1, outs),
                    weight[a, b, e],
                    (((1,), (1,)), ((), ())),
                    preferred_element_type=jnp.float32,
                )
    grad_hidden[...] = total.reshape(grad_hidden.shape)
    all_taps[...] = sum(
        weight[a, b, e].astype(jnp.float32) for a in range(3) for b in range(3) for e in range(3)
    )


def hidden_grads(cot, later, above, below, weight):
    frames, rows, cols, outs = cot.shape
    return pl.pallas_call(
        grad_hidden_kernel,
        out_shape=(
            jax.ShapeDtypeStruct((frames, rows + 2, cols, weight.shape[-2]), jnp.float32),
            jax.ShapeDtypeStruct(weight.shape[-2:], jnp.float32),
        ),
        in_specs=whole(5),
        out_specs=whole(2),
        scratch_shapes=[pltpu.VMEM((2 * frames * (rows + 4), cols + 16, 128), jnp.float32)],
        compiler_params=pltpu.CompilerParams(vmem_limit_bytes=VMEM_LIMIT),
        cost_estimate=pl.CostEstimate(flops=2**30, bytes_accessed=2**21, transcendentals=0),
        name="grad_hidden",
    )(cot, later, above, below, weight)


def middle_kernel(count, where, came, pre_norm, grad_hidden, all_taps, gain, shift, hidden, grad_normed, normed, vectors):
    outs = pre_norm.shape[-1]
    total = jnp.sum(came[...], 0)
    mean = total[:1] / count
    scaled = lax.rsqrt(total[1:2] / count - mean * mean + EPSILON)
    flat = (pre_norm[...].reshape(-1, outs) - mean) * scaled
    shifted = flat * gain[...] + shift[...]
    sigma = 1.0 / (1.0 + jnp.exp(-shifted))
    hidden[...] = inside(where, (shifted * sigma).reshape(pre_norm.shape)).astype(jnp.bfloat16)
    grad = grad_hidden[...].reshape(-1, outs) * sigma * (1.0 + shifted * (1.0 - sigma)) * gain[...]
    grad, flat = grad.reshape(pre_norm.shape), flat.reshape(pre_norm.shape)
    grad_normed[...] = grad
    normed[...] = flat
    own = grad[:, 1:-1]

    cells = count / (outs // GROUPS)
    level = lax.dot_general(
        total[2:3] / cells,
        all_taps[...],
        (((1,), (1,)), ((), ())),
        precision=lax.Precision.HIGHEST,
        preferred_element_type=jnp.float32,
    )
    at = lax.broadcasted_iota(jnp.int32, (16, outs), 0).astype(jnp.float32) * 0.45 - 3.375
    share = jnp.exp(-0.5 * at * at)
    share = share / jnp.sum(share, 0, keepdims=True)
    point = at * gain[...] + shift[...]
    slope = 1.0 / (1.0 + jnp.exp(-point))
    slope = slope * (1.0 + point * (1.0 - slope)) * share
    level = level * gain[...] * (cells / count)
    offsets = group_sums(
        level * jnp.sum(slope, 0, keepdims=True), level * jnp.sum(slope * at, 0, keepdims=True), outs
    )
    rows = [scaled, offsets, cell_sums(own), cell_sums(own * flat[:, 1:-1])]
    vectors[...] = jnp.concatenate(rows + [jnp.zeros((3, outs), jnp.float32)], 0)


def middle(count, where, came, pre_norm, grad_hidden, all_taps, gain, shift):
    shape, outs = pre_norm.shape, pre_norm.shape[-1]
    return pl.pallas_call(
        functools.partial(middle_kernel, count),
        out_shape=(
            jax.ShapeDtypeStruct(shape, jnp.bfloat16),
            jax.ShapeDtypeStruct(shape, jnp.float32),
            jax.ShapeDtypeStruct(shape, jnp.float32),
            jax.ShapeDtypeStruct((8, outs), jnp.float32),
        ),
        in_specs=whole(1, pltpu.SMEM) + whole(6),
        out_specs=whole(4),
        compiler_params=pltpu.CompilerParams(vmem_limit_bytes=VMEM_LIMIT),
        name="middle",
    )(where, came, pre_norm, grad_hidden, all_taps, gain[None], shift[None])


def second_weight_kernel(hidden, cot, later, above, below, out, wide):
    frames, rows, cols, ins = hidden.shape
    outs = cot.shape[-1]
    own = hidden[:, 1:-1].reshape(-1, ins).astype(jnp.float32).T.astype(jnp.bfloat16)
    fill_cot(wide, cot, later, above, below)
    shifted = [col_tap(wide, e, cot.shape) for e in range(3)]
    for a in range(3):
        pieces = [
            shifted[e][2 - a : 2 - a + frames, 3 - b : 3 - b + rows - 2].reshape(-1, outs)
            for b in range(3)
            for e in range(3)
        ]
        pieces.append(jnp.zeros((pieces[0].shape[0], 32), jnp.bfloat16))
        out[a] = jnp.dot(own, jnp.concatenate(pieces, 1), preferred_element_type=jnp.float32)


def second_weight(hidden, cot, later, above, below):
    frames, rows, cols, _ = cot.shape
    return pl.pallas_call(
        second_weight_kernel,
        out_shape=jax.ShapeDtypeStruct((3, hidden.shape[-1], 896), jnp.float32),
        in_specs=whole(5),
        out_specs=whole()[0],
        scratch_shapes=[pltpu.VMEM((2 * frames * (rows + 4), cols + 16, 128), jnp.float32)],
        compiler_params=pltpu.CompilerParams(vmem_limit_bytes=VMEM_LIMIT),
        name="second_weight",
    )(hidden, cot, later, above, below)


def col_sums(wide, cells):
    half = cells.shape[1] // 2
    wide[...] = jnp.zeros_like(wide)
    wide[:, 8 : 8 + cells.shape[1], : cells.shape[2]] = cells

    def every_second(start):
        return wide[:, pl.ds(start, half, stride=2), : cells.shape[2]]

    before, even, odd, after = (every_second(7 + k) for k in range(4))
    return odd + after, even + odd, before + even


def group_lanes(outs, first):
    lane = lax.broadcasted_iota(jnp.int32, (outs, 128), 1)
    group = lax.broadcasted_iota(jnp.int32, (outs, 128), 0) // (outs // GROUPS)
    return (lane == group + (64 if first else 64 + GROUPS)).astype(jnp.float32)


def exact(left, right, dims):
    return lax.dot_general(
        left, right, (dims, ((), ())), precision=lax.Precision.HIGHEST, preferred_element_type=jnp.float32
    )


def in_parts(sums, rows):
    high = sums.astype(jnp.bfloat16).astype(jnp.float32)
    middle = (sums - high).astype(jnp.bfloat16).astype(jnp.float32)
    low = sums - high - middle
    row = lax.broadcasted_iota(jnp.int32, (rows, 128), 0)
    return jnp.where(row == 0, high, jnp.where(row == 1, middle, jnp.where(row == 2, low, 0.0)))


def sums_of(tile):
    return tile[0:1] + tile[1:2] + tile[2:3]


def weight_grads_kernel(where, cache, features, above, below, grad_normed, normed, vectors, two, away, kept, wide):
    frames, rows, cols, outs = grad_normed.shape
    rows, half = rows - 2, cols // 2
    ins, mids, pieces, part_rows = features.shape[-1], two.shape[1], kept.shape[0], (kept.shape[1] - 16) * 2 // 5
    timed = jnp.concatenate([cache[...], features[...]], 0)
    rows_in = jnp.concatenate([above[:, :half][:, None], timed, below[:, :half][:, None]], 1)
    rstd, f0, s0 = (vectors[k : k + 1] for k in range(3))
    own = normed[:, 1:-1].reshape(-1, outs)
    grad = (grad_normed[:, 1:-1].reshape(-1, outs) - f0 - own * s0) * rstd
    lower = where[0] == 0

    def pool(field, last):
        by_tap = col_sums(wide, field.reshape(frames * rows, cols, outs))
        taps = []
        for b in range(3):
            for e in range(3):
                part = by_tap[e].reshape(frames, rows, half, outs)
                none = jnp.zeros_like(part[:, 0])
                r = [part[:, k] for k in range(rows)]
                stacked = (
                    [r[0], r[1] + r[2], r[3], none],
                    [none, r[0] + r[1], r[2] + r[3], none],
                    [none, r[0], r[1] + r[2], r[3]],
                )[b]
                taps.append(jnp.stack(stacked, 1).astype(jnp.bfloat16).reshape(-1, outs))
        return jnp.concatenate(taps + [last], 1)

    at = lax.broadcasted_iota(jnp.int32, (frames * 4 * half, 32), 0)
    tap = lax.broadcasted_iota(jnp.int32, (frames * 4 * half, 32), 1)
    b, e, row, col = tap // 3, tap % 3, at // half % 4, at % half
    two_rows = (row == 1) & (b < 2) | (row == 2) & (b > 0)
    one_row = (row == 0) & (b == 0) | (row == 2) & (b == 0) | (row == 1) & (b == 2) | (row == 3) & (b == 2)
    in_rows = jnp.where(two_rows, 2.0, jnp.where(one_row, 1.0, 0.0))
    in_cols = jnp.where((e == 0) & (col == half - 1) | (e == 2) & (col == 0), 1.0, 2.0)
    counts = jnp.where(tap < 9, in_rows * in_cols, 0.0).astype(jnp.bfloat16)

    def write(part, at, low, high):
        deep = part_rows if part < 2 else part_rows // 2
        while low.shape[0]:
            x, row = at // deep, part_rows * part + at % deep
            n = min(low.shape[0], deep - at % deep)
            away[x, row : row + n] = jnp.where(lower, high[:n], low[:n]).astype(jnp.bfloat16)
            kept[x, row : row + n] = jnp.where(lower, low[:n], high[:n])
            low, high, at = low[n:], high[n:], at + n

    for part, field, last in ((0, grad, counts), (1, own * rstd, jnp.zeros_like(counts))):
        cells = pool(field, last)
        at = 0
        for a in range(3):
            product = lax.dot_general(
                rows_in[a : a + frames].reshape(-1, ins),
                cells,
                (((0,), (0,)), ((), ())),
                preferred_element_type=jnp.float32,
            )
            for j in range(7):
                block = product[:, 128 * j : 128 * j + 128]
                write(part, at, block[: ins // 2], block[ins // 2 :])
                at += ins // 2
        nothing = jnp.zeros((pieces * part_rows - at, 128), jnp.float32)
        write(part, at, nothing, nothing)

    sums = exact(vectors[3:4], group_lanes(outs, True), ((1,), (0,)))
    sums += exact(vectors[4:5], group_lanes(outs, False), ((1,), (0,)))
    sums = in_parts(sums, 16)
    at = 0
    for a in range(3):
        for j in range(7):
            block = two[a, :, 128 * j : 128 * j + 128]
            write(2, at, block[: mids // 2], block[mids // 2 :])
            at += mids // 2
    nothing = jnp.zeros((pieces * part_rows // 2 - at, 128), jnp.float32)
    write(2, at, nothing, nothing)
    for x in range(pieces):
        away[x, part_rows * 5 // 2 :] = sums.astype(jnp.bfloat16)
        kept[x, part_rows * 5 // 2 :] = sums


def weight_grads(where, cache, features, above, below, grad_normed, normed, vectors, two, pieces, part_rows):
    frames, rows, cols, _ = grad_normed.shape
    shape = (pieces, part_rows * 5 // 2 + 16, 128)
    return pl.pallas_call(
        weight_grads_kernel,
        out_shape=(jax.ShapeDtypeStruct(shape, jnp.bfloat16), jax.ShapeDtypeStruct(shape, jnp.float32)),
        in_specs=whole(1, pltpu.SMEM) + whole(8),
        out_specs=whole(2),
        scratch_shapes=[pltpu.VMEM((frames * (rows - 2), cols + 16, 128), jnp.float32)],
        compiler_params=pltpu.CompilerParams(vmem_limit_bytes=VMEM_LIMIT),
        name="weight_grads",
    )(where, cache, features, above, below, grad_normed, normed, vectors, two)


def add_pair_kernel(kept, came, out, total, sems):
    deep = kept.shape[1] - 16
    sums = in_parts(sums_of(kept[0, deep:] + came[0, deep:].astype(jnp.float32)), 16).astype(jnp.bfloat16)
    moves = []
    for x in range(kept.shape[0]):
        total[x, :deep] = (kept[x, :deep] + came[x, :deep].astype(jnp.float32)).astype(jnp.bfloat16)
        total[x, deep:] = sums
        moves.append(pltpu.make_async_copy(total.at[x], out.at[x], sems.at[x]))
        moves[x].start()
    for move in moves:
        move.wait()


def add_pair(kept, came):
    return pl.pallas_call(
        add_pair_kernel,
        out_shape=jax.ShapeDtypeStruct(kept.shape, jnp.bfloat16),
        in_specs=whole(2),
        out_specs=whole(1, pltpu.HBM)[0],
        scratch_shapes=[pltpu.VMEM(kept.shape, jnp.bfloat16), pltpu.SemaphoreType.DMA((kept.shape[0],))],
        compiler_params=pltpu.CompilerParams(vmem_limit_bytes=VMEM_LIMIT),
        name="add_pair",
    )(kept, came)


def add_row_kernel(came, out):
    total = jnp.sum(came[...].astype(jnp.float32), 0)
    n = out.shape[0] * 8
    out[:, 0] = total[:n].astype(jnp.bfloat16).reshape(-1, 8, 128)
    out[:, 1] = total[n : 2 * n].astype(jnp.bfloat16).reshape(-1, 8, 128)
    tiles = total[2 * n : n * 5 // 2].reshape(-1, 8, 128)
    row = lax.broadcasted_iota(jnp.int32, (1, 8, 128), 1)
    lane = lax.broadcasted_iota(jnp.int32, (1, 8, 128), 2)
    turned = jnp.concatenate([tiles[:, 4:], tiles[:, :4]], 1)
    swap = lambda k: jnp.concatenate([k[..., 64:], k[..., :64]], 2)
    even = jnp.where(row < 4, tiles, swap(turned))
    odd = jnp.where(row < 4, turned, swap(tiles))
    both = jnp.stack([even, odd], 1).reshape(-1, 8, 128)
    sums = in_parts(sums_of(total[n * 5 // 2 :]), 8)
    out[:, 2] = jnp.where(lane < 64, both, sums[None]).astype(jnp.bfloat16)


def add_row(came):
    tiles = (came.shape[1] - 16) // 20
    return pl.pallas_call(
        add_row_kernel,
        out_shape=jax.ShapeDtypeStruct((tiles, 3, 8, 128), jnp.bfloat16),
        in_specs=whole(1),
        out_specs=whole()[0],
        compiler_params=pltpu.CompilerParams(vmem_limit_bytes=VMEM_LIMIT),
        name="add_row",
    )(came)


def combine_kernel(count, tiles_per_block, where, came, vectors, piece, final, lanes):
    outs = vectors.shape[1]
    total = jnp.sum(came[...].astype(jnp.float32), 0)
    sums = sums_of(total[0, 2]) / count
    first = exact(sums, group_lanes(outs, True), ((1,), (1,)))
    second = exact(sums, group_lanes(outs, False), ((1,), (1,)))
    rest = (first - vectors[1:2]) * vectors[0:1]
    final[...] = jnp.concatenate([first, second, rest, jnp.zeros((5, outs), jnp.float32)], 0)
    spread = [second - vectors[2:3]] * 9 + [jnp.zeros((1, 32), jnp.float32)]
    lanes[...] = jnp.broadcast_to(jnp.concatenate(spread, 1), lanes.shape)
    for k in range(piece.shape[0]):
        block = (where[3] * piece.shape[0] + k) // tiles_per_block % 7
        change = lanes[0:1, pl.ds(pl.multiple_of(block * 128, 128), 128)]
        upper = jnp.concatenate([total[k, 2, :4, :64], total[k, 2, 4:, :64]], 1)
        grad = total[k, 0] - change * total[k, 1]
        piece[k] = jnp.concatenate([grad, upper], 0).astype(jnp.bfloat16)


def combine(count, ins, where, came, vectors):
    return pl.pallas_call(
        functools.partial(combine_kernel, count, ins // 16),
        out_shape=(
            jax.ShapeDtypeStruct((came.shape[1], 12, 128), jnp.bfloat16),
            jax.ShapeDtypeStruct(vectors.shape, jnp.float32),
        ),
        in_specs=whole(1, pltpu.SMEM) + whole(2),
        out_specs=whole(2),
        scratch_shapes=[pltpu.VMEM((8, 896), jnp.float32)],
        compiler_params=pltpu.CompilerParams(vmem_limit_bytes=VMEM_LIMIT),
        name="combine",
    )(where, came, vectors)


def grad_pre_kernel(where, grad_normed, normed, vectors, final, out):
    shape = grad_normed.shape
    flat = (-1, shape[-1])
    grad = grad_normed[...].reshape(flat) - final[:1] - normed[...].reshape(flat) * final[1:2]
    out[...] = inside(where, (grad * vectors[:1]).reshape(shape)).astype(jnp.bfloat16)


def grad_before_norm(where, grad_normed, normed, vectors, final):
    return pl.pallas_call(
        grad_pre_kernel,
        out_shape=jax.ShapeDtypeStruct(grad_normed.shape, jnp.bfloat16),
        in_specs=whole(1, pltpu.SMEM) + whole(4),
        out_specs=whole()[0],
        compiler_params=pltpu.CompilerParams(vmem_limit_bytes=VMEM_LIMIT),
        cost_estimate=pl.CostEstimate(flops=2**20, bytes_accessed=2**20, transcendentals=0),
        name="grad_pre",
    )(where, grad_normed, normed, vectors, final)


def unpack_kernel(scale, half, part, final, *rest):
    one, two, flat = rest[-3:]
    pieces, rows = part.shape[0], part.shape[1]
    split = rows * 2 // 3
    step = pl.program_id(0)

    @pl.when(step == 0)
    def _():
        for x in range(pieces):
            flat[split * x : split * (x + 1)] = part[x, :split]
            at = pieces * split + (rows - split) * x
            flat[at : at + rows - split] = part[x, split:]

    for out, begin in ((one, 0), (two, pieces * split)):
        taps, channels, outs = out.shape
        blocks = []
        for j in range(7):
            at = pl.multiple_of(begin + (step * 7 + j) * channels, 16)
            blocks.append(flat[pl.ds(at, channels)])
        lanes = jnp.concatenate(blocks, 1)
        if out is one:
            change = jnp.concatenate([final[2:3], jnp.zeros((1, 128 - outs), jnp.float32)], 1)
            change = jnp.concatenate([change] * taps, 1)
            tap = lax.broadcasted_iota(jnp.int32, (32, change.shape[1]), 0)
            lane = lax.broadcasted_iota(jnp.int32, (32, change.shape[1]), 1)
            change = jnp.where(lane // 128 == tap, change, 0.0)
            high = change.astype(jnp.bfloat16)
            low = (change - high.astype(jnp.float32)).astype(jnp.bfloat16)
            met = jnp.concatenate([blocks[-1].astype(jnp.float32)[:, 96:]] * 2, 1).astype(jnp.bfloat16)
            change = jnp.concatenate([high, low], 0)
            change = jnp.dot(met, change, preferred_element_type=jnp.float32)
        for k in range(taps):
            grad = lanes[:, outs * k : outs * k + outs].astype(jnp.float32)
            if out is one:
                grad = grad - change[:, 128 * k : 128 * k + outs]
            out[k] = grad * scale


def unpack(half, part, final, ins, mids, scale, begun=()):
    return pl.pallas_call(
        functools.partial(unpack_kernel, scale),
        grid_spec=pltpu.PrefetchScalarGridSpec(
            num_scalar_prefetch=1,
            grid=(3,),
            in_specs=whole(2) + whole(len(begun), pl.ANY),
            out_specs=[
                pl.BlockSpec((9, ins // 2, mids), lambda a, half: (a, half[0], 0)),
                pl.BlockSpec((9, mids // 2, mids), lambda a, half: (a, half[0], 0)),
            ],
            scratch_shapes=[pltpu.VMEM((part.shape[0] * part.shape[1], 128), jnp.bfloat16)],
        ),
        out_shape=(
            jax.ShapeDtypeStruct((27, ins, mids), jnp.float32),
            jax.ShapeDtypeStruct((27, mids, mids), jnp.float32),
        ),
        input_output_aliases={3 + k: k for k in range(len(begun))},
        compiler_params=pltpu.CompilerParams(vmem_limit_bytes=VMEM_LIMIT),
        cost_estimate=pl.CostEstimate(flops=2**20, bytes_accessed=2**22, transcendentals=0),
        name="unpack",
    )(half, part, final, *begun)


def feature_grads_kernel(grad_pre, weight, out, wide):
    frames, rows, cols, outs = grad_pre.shape
    own, cells_in, cols_in, ins = out.shape
    by_tap = col_sums(wide, grad_pre[...].astype(jnp.float32).reshape(frames * rows, cols, outs))
    total = jnp.zeros((own * cells_in * cols_in, ins), jnp.float32)
    for b in range(3):
        for e in range(3):
            part = by_tap[e].reshape(frames, rows, cols // 2, outs)
            cells = jnp.stack(
                [part[:, 2 * k + 2 - b] + part[:, 2 * k + 3 - b] for k in range(cells_in)], 1
            ).astype(jnp.bfloat16)
            for a in range(3):
                total += lax.dot_general(
                    cells[2 - a : 2 - a + own].reshape(-1, outs),
                    weight[a, b, e],
                    (((1,), (1,)), ((), ())),
                    preferred_element_type=jnp.float32,
                )
    out[...] = total.reshape(out.shape)


def feature_grads(grad_rowed, weight, shape):
    frames, rows, cols, _ = grad_rowed.shape
    return pl.pallas_call(
        feature_grads_kernel,
        out_shape=jax.ShapeDtypeStruct(shape, jnp.float32),
        in_specs=whole(2),
        out_specs=whole()[0],
        scratch_shapes=[pltpu.VMEM((frames * rows, cols + 16, 128), jnp.float32)],
        compiler_params=pltpu.CompilerParams(vmem_limit_bytes=VMEM_LIMIT),
        cost_estimate=pl.CostEstimate(flops=2**28, bytes_accessed=2**21, transcendentals=0),
        name="feature_grads",
    )(grad_rowed, weight)


SWAP = [(0, 1), (1, 0)]


def body(features, cotangent, weight_one, weight_two, norm_gain, norm_shift):
    frames, ins = features.shape[0], features.shape[-1]
    rows, cols, mids = cotangent.shape[1:]
    xs, rest, height = lax.axis_size("x"), lax.axis_size(REST), lax.axis_size(HEIGHT)
    cells = frames * rows * cols * 2 * xs * rest
    count = cells * (mids // GROUPS)
    at_row = lax.axis_index(HEIGHT)
    owned = lax.axis_index("x") * rest + lax.axis_index(REST)
    where = jnp.stack([lax.axis_index("c"), at_row == 0, at_row == height - 1, owned]).astype(jnp.int32)
    barrier = lax.optimization_barrier

    def exchange(copies, axes):
        return lax.all_to_all(copies, axes, 0, 0)

    def spread(value, copies):
        return jnp.broadcast_to(value[None], (copies,) + value.shape)

    cache = neighbour(features, TM, 1)
    later = neighbour(cotangent, TM, -1)

    features, cotangent = resident(features, cotangent)
    downward, upward = edges(cache, features, cotangent, later)
    downward, upward, weight_one, weight_two = barrier((downward, upward, weight_one, weight_two))
    weight_one, weight_two = resident(weight_one, weight_two)
    above = neighbour(downward, HEIGHT, 1)
    below = neighbour(upward, HEIGHT, -1)
    pre_norm, sums = conv_one(cache, features, above, below, weight_one, cotangent, height)
    came = exchange(sums, HEIGHT)
    grad_hidden, all_taps = hidden_grads(cotangent, later, above, below, weight_two)
    sums, grad_hidden = barrier((came.sum(0), grad_hidden))
    came = exchange(spread(sums, lax.axis_size(TM)), TM)
    hidden, grad_normed, normed, vectors = middle(
        count, where, came, pre_norm, grad_hidden, all_taps, norm_gain, norm_shift
    )
    local_two = second_weight(hidden, cotangent, later, above, below)

    scale = 1.0 / cells**0.5
    part_rows = -(-21 * ins // (2 * 8 * xs * rest)) * 8 * rest
    away, kept = weight_grads(
        where, cache, features, above, below, grad_normed, normed, vectors, local_two, xs, part_rows
    )
    part = add_pair(kept, lax.ppermute(away, "c", SWAP))
    part, hidden = barrier((part, hidden))
    part = add_row(exchange(part, "x"))
    before = neighbour(hidden, TM, 1)
    part, before = barrier((part, before))
    came = exchange(part.reshape(rest, -1, 3, 8, 128), REST)
    decoded = conv(
        jnp.pad(jnp.concatenate([before, hidden], 0), ((0, 0), (0, 0), (1, 1), (0, 0))), weight_two
    ).astype(jnp.bfloat16)
    came, decoded = barrier((came, decoded))
    part, final = combine(count, ins, where, came, vectors)
    grad_pre = grad_before_norm(where, grad_normed, normed, vectors, final)
    part = exchange(spread(part, rest), REST)
    after = neighbour(grad_pre, TM, -1)
    part, after = barrier((part, after))
    part = jnp.concatenate([part[:, :, :8].reshape(-1, 128), part[:, :, 8:].reshape(-1, 128)], 0)
    part = exchange(spread(part, xs), "x")
    grad_features = feature_grads(jnp.concatenate([grad_pre, after], 0), weight_one, features.shape)
    part, grad_features = barrier((part, grad_features))
    other = lax.ppermute(part, "c", SWAP)
    core = where[:1]
    begun = unpack(core, part, final, ins, mids, scale)
    grad_one, grad_two = unpack(1 - core, other, final, ins, mids, scale, begun)
    return decoded, grad_features, grad_one.reshape(weight_one.shape), grad_two.reshape(weight_two.shape)


def solution(mesh):
    split = P(TM, HEIGHT, None, None)
    return jax.shard_map(
        body,
        mesh=fine_mesh(mesh),
        in_specs=(split, split, P(), P(), P(), P()),
        out_specs=(split, split, P(), P()),
        check_vma=False,
    )
```

```python
import functools

import jax
import jax.numpy as jnp
from jax import lax
from jax.experimental import pallas as pl
from jax.experimental.pallas import tpu as pltpu
from jax.sharding import Mesh
from jax.sharding import PartitionSpec as P

GROUPS = 32
EPSILON = 1e-05

TM = ("zh", "y")
HEIGHT = ("zl", "x", "c")
REST = ("zh", "y", "zl")

VMEM_LIMIT = 32 * 2**20


def fine_mesh(mesh):
    tm, height = mesh.shape["tm"], mesh.shape["height"]
    zh = 2 if tm % 2 == 0 else 1
    core = 2
    x = 4 if height % 8 == 0 else height // 2
    return Mesh(mesh.devices.reshape(zh, tm // zh, height // (core * x), x, core), TM + HEIGHT)


def neighbour(value, axis, steps):
    count = lax.axis_size(axis)
    first, last = max(0, -steps), min(count, count - steps)
    return lax.ppermute(value, axis, [(i, i + steps) for i in range(first, last)])


def conv(padded, weight):
    return lax.conv_general_dilated(
        padded[None],
        weight,
        (1, 1, 1),
        "VALID",
        dimension_numbers=("NDHWC", "DHWIO", "NDHWC"),
        preferred_element_type=jnp.float32,
    )[0]


def whole(count=1, space=pltpu.VMEM):
    return [pl.BlockSpec(memory_space=space)] * count


def group_sums(first, second, outs):
    member = lax.broadcasted_iota(jnp.int32, (2, outs, outs), 1) // (outs // GROUPS)
    other = lax.broadcasted_iota(jnp.int32, (2, outs, outs), 2) // (outs // GROUPS)
    same = (member[0] == other[0]).astype(jnp.float32)
    both = jnp.concatenate([first, second, jnp.zeros((6, outs), jnp.float32)], 0)
    return jnp.dot(both, same, precision=lax.Precision.HIGHEST, preferred_element_type=jnp.float32)[:2]


def cell_sums(field):
    return jnp.sum(field.reshape(-1, field.shape[-1]), 0, keepdims=True)


def inside(where, field):
    row = lax.broadcasted_iota(jnp.int32, field.shape, 1)
    last = field.shape[1] - 1
    out = ((row == 0) & (where[1] == 1)) | ((row == last) & (where[2] == 1))
    return jnp.where(out, 0.0, field)


def resident_kernel(*refs):
    count = len(refs) // 2
    sems = refs[-1]
    moves = [pltpu.make_async_copy(refs[k], refs[count + k], sems.at[k]) for k in range(count)]
    for move in moves:
        move.start()
    for move in moves:
        move.wait()


def resident(*arrays):
    count = len(arrays)
    return pl.pallas_call(
        resident_kernel,
        out_shape=[jax.ShapeDtypeStruct(k.shape, k.dtype) for k in arrays],
        in_specs=whole(count, pltpu.HBM),
        out_specs=whole(count),
        scratch_shapes=[pltpu.SemaphoreType.DMA((count,))],
        compiler_params=pltpu.CompilerParams(vmem_limit_bytes=VMEM_LIMIT),
        cost_estimate=pl.CostEstimate(flops=0, bytes_accessed=2**22, transcendentals=0),
        name="resident",
    )(*arrays)


def edges_kernel(cache, features, cot, later, downward, upward):
    cells, rows = features.shape[1], cot.shape[1]
    half = features.shape[2]
    for out, cell, row in ((downward, cells - 1, rows - 2), (upward, 0, 0)):
        out[:, :half] = jnp.concatenate([cache[:, cell], features[:, cell]], 0)
        pair = [jnp.concatenate([cot[:, k], later[:, k]], 0) for k in (row, row + 1)]
        out[:, half:] = jnp.concatenate(pair, 2)


def edges(cache, features, cot, later):
    frames, _, half, ins = features.shape
    shape = jax.ShapeDtypeStruct((2 * frames, half + cot.shape[2], ins), jnp.bfloat16)
    return pl.pallas_call(
        edges_kernel,
        out_shape=(shape, shape),
        in_specs=whole(4),
        out_specs=whole(2),
        compiler_params=pltpu.CompilerParams(vmem_limit_bytes=VMEM_LIMIT),
        name="edges",
    )(cache, features, cot, later)


def conv_one_kernel(cache, features, above, below, weight, cot, pre_norm, sums, wide):
    frames, rows, cols, outs = pre_norm.shape
    cells_in, half, ins = features.shape[1], cols // 2, features.shape[-1]
    timed = jnp.concatenate([cache[...], features[...]], 0)
    rowed = jnp.concatenate([above[:, :half][:, None], timed, below[:, :half][:, None]], 1)
    by_tap = []
    for e in range(3):
        total = jnp.zeros((frames, rows, half, outs), jnp.float32)
        for b in range(3):
            product = sum(
                jnp.dot(
                    rowed[a : a + frames].reshape(-1, ins),
                    weight[a, b, e],
                    preferred_element_type=jnp.float32,
                )
                for a in range(3)
            ).reshape(frames, cells_in + 2, half, outs)
            total += jnp.stack([product[:, (r + b) // 2] for r in range(rows)], 1)
        by_tap.append(total.reshape(frames * rows, half, outs))
    wide[...] = jnp.zeros_like(wide)
    wide[:, 8 : 8 + half, :outs] = by_tap[0]
    even = wide[:, 7 : 7 + half, :outs] + by_tap[1] + by_tap[2]
    wide[:, 8 : 8 + half, :outs] = by_tap[2]
    odd = by_tap[0] + by_tap[1] + wide[:, 9 : 9 + half, :outs]
    wide[:, pl.ds(0, half, stride=2), :outs] = even
    wide[:, pl.ds(1, half, stride=2), :outs] = odd
    pre = wide[:, :cols, :outs].reshape(pre_norm.shape)
    pre_norm[...] = pre
    own = pre[:, 1:-1]
    both = group_sums(cell_sums(own), cell_sums(own * own), outs)
    both = jnp.concatenate([both, cell_sums(cot[...].astype(jnp.float32)), jnp.zeros((1, outs), jnp.float32)], 0)
    sums[...] = jnp.broadcast_to(both[None], sums.shape)


def conv_one(cache, features, above, below, weight, cot, copies):
    frames, cells_in, half, _ = features.shape
    outs = weight.shape[-1]
    rows, cols = 2 * cells_in + 2, 2 * half
    return pl.pallas_call(
        conv_one_kernel,
        out_shape=(
            jax.ShapeDtypeStruct((frames, rows, cols, outs), jnp.float32),
            jax.ShapeDtypeStruct((copies, 4, outs), jnp.float32),
        ),
        in_specs=whole(6),
        out_specs=whole(2),
        scratch_shapes=[pltpu.VMEM((frames * rows, cols + 16, 128), jnp.float32)],
        compiler_params=pltpu.CompilerParams(vmem_limit_bytes=VMEM_LIMIT),
        name="conv_one",
    )(cache, features, above, below, weight, cot)


def fill_cot(wide, cot, later, above, below):
    cols, outs = cot.shape[2:]
    half = cols // 2
    timed = jnp.concatenate([cot[...], later[...]], 0)
    pair = lambda part: jnp.stack([part[:, half:, :outs], part[:, half:, outs:]], 1)
    rowed = jnp.concatenate([pair(above), timed, pair(below)], 1).astype(jnp.float32)
    wide[...] = jnp.zeros_like(wide)
    wide[:, 8 : 8 + cols, :outs] = rowed.reshape(-1, cols, outs)


def col_tap(wide, e, shape):
    part = wide[:, 9 - e : 9 - e + shape[2], : shape[3]].astype(jnp.bfloat16)
    return part.reshape(2 * shape[0], shape[1] + 4, shape[2], shape[3])


def grad_hidden_kernel(cot, later, above, below, weight, grad_hidden, all_taps, wide):
    frames, rows, cols, ins = grad_hidden.shape
    outs = cot.shape[-1]
    fill_cot(wide, cot, later, above, below)
    total = jnp.zeros((frames * rows * cols, ins), jnp.float32)
    for e in range(3):
        part = col_tap(wide, e, cot.shape)
        for a in range(3):
            for b in range(3):
                total += lax.dot_general(
                    part[2 - a : 2 - a + frames, 2 - b : 2 - b + rows].reshape(-1, outs),
                    weight[a, b, e],
                    (((1,), (1,)), ((), ())),
                    preferred_element_type=jnp.float32,
                )
    grad_hidden[...] = total.reshape(grad_hidden.shape)
    all_taps[...] = sum(
        weight[a, b, e].astype(jnp.float32) for a in range(3) for b in range(3) for e in range(3)
    )


def hidden_grads(cot, later, above, below, weight):
    frames, rows, cols, outs = cot.shape
    return pl.pallas_call(
        grad_hidden_kernel,
        out_shape=(
            jax.ShapeDtypeStruct((frames, rows + 2, cols, weight.shape[-2]), jnp.float32),
            jax.ShapeDtypeStruct(weight.shape[-2:], jnp.float32),
        ),
        in_specs=whole(5),
        out_specs=whole(2),
        scratch_shapes=[pltpu.VMEM((2 * frames * (rows + 4), cols + 16, 128), jnp.float32)],
        compiler_params=pltpu.CompilerParams(vmem_limit_bytes=VMEM_LIMIT),
        cost_estimate=pl.CostEstimate(flops=2**30, bytes_accessed=2**21, transcendentals=0),
        name="grad_hidden",
    )(cot, later, above, below, weight)


def middle_kernel(count, where, came, pre_norm, grad_hidden, all_taps, gain, shift, hidden, grad_normed, normed, vectors):
    outs = pre_norm.shape[-1]
    total = jnp.sum(came[...], 0)
    mean = total[:1] / count
    scaled = lax.rsqrt(total[1:2] / count - mean * mean + EPSILON)
    flat = (pre_norm[...].reshape(-1, outs) - mean) * scaled
    shifted = flat * gain[...] + shift[...]
    sigma = 1.0 / (1.0 + jnp.exp(-shifted))
    hidden[...] = inside(where, (shifted * sigma).reshape(pre_norm.shape)).astype(jnp.bfloat16)
    grad = grad_hidden[...].reshape(-1, outs) * sigma * (1.0 + shifted * (1.0 - sigma)) * gain[...]
    grad, flat = grad.reshape(pre_norm.shape), flat.reshape(pre_norm.shape)
    grad_normed[...] = grad
    normed[...] = flat
    own = grad[:, 1:-1]

    cells = count / (outs // GROUPS)
    level = lax.dot_general(
        total[2:3] / cells,
        all_taps[...],
        (((1,), (1,)), ((), ())),
        precision=lax.Precision.HIGHEST,
        preferred_element_type=jnp.float32,
    )
    at = lax.broadcasted_iota(jnp.int32, (16, outs), 0).astype(jnp.float32) * 0.45 - 3.375
    share = jnp.exp(-0.5 * at * at)
    share = share / jnp.sum(share, 0, keepdims=True)
    point = at * gain[...] + shift[...]
    slope = 1.0 / (1.0 + jnp.exp(-point))
    slope = slope * (1.0 + point * (1.0 - slope)) * share
    level = level * gain[...] * (cells / count)
    offsets = group_sums(
        level * jnp.sum(slope, 0, keepdims=True), level * jnp.sum(slope * at, 0, keepdims=True), outs
    )
    rows = [scaled, offsets, cell_sums(own), cell_sums(own * flat[:, 1:-1])]
    vectors[...] = jnp.concatenate(rows + [jnp.zeros((3, outs), jnp.float32)], 0)


def middle(count, where, came, pre_norm, grad_hidden, all_taps, gain, shift):
    shape, outs = pre_norm.shape, pre_norm.shape[-1]
    return pl.pallas_call(
        functools.partial(middle_kernel, count),
        out_shape=(
            jax.ShapeDtypeStruct(shape, jnp.bfloat16),
            jax.ShapeDtypeStruct(shape, jnp.float32),
            jax.ShapeDtypeStruct(shape, jnp.float32),
            jax.ShapeDtypeStruct((8, outs), jnp.float32),
        ),
        in_specs=whole(1, pltpu.SMEM) + whole(6),
        out_specs=whole(4),
        compiler_params=pltpu.CompilerParams(vmem_limit_bytes=VMEM_LIMIT),
        name="middle",
    )(where, came, pre_norm, grad_hidden, all_taps, gain[None], shift[None])


def second_weight_kernel(hidden, cot, later, above, below, out, wide):
    frames, rows, cols, ins = hidden.shape
    outs = cot.shape[-1]
    own = hidden[:, 1:-1].reshape(-1, ins).astype(jnp.float32).T.astype(jnp.bfloat16)
    fill_cot(wide, cot, later, above, below)
    shifted = [col_tap(wide, e, cot.shape) for e in range(3)]
    for a in range(3):
        pieces = [
            shifted[e][2 - a : 2 - a + frames, 3 - b : 3 - b + rows - 2].reshape(-1, outs)
            for b in range(3)
            for e in range(3)
        ]
        pieces.append(jnp.zeros((pieces[0].shape[0], 32), jnp.bfloat16))
        out[a] = jnp.dot(own, jnp.concatenate(pieces, 1), preferred_element_type=jnp.float32)


def second_weight(hidden, cot, later, above, below):
    frames, rows, cols, _ = cot.shape
    return pl.pallas_call(
        second_weight_kernel,
        out_shape=jax.ShapeDtypeStruct((3, hidden.shape[-1], 896), jnp.float32),
        in_specs=whole(5),
        out_specs=whole()[0],
        scratch_shapes=[pltpu.VMEM((2 * frames * (rows + 4), cols + 16, 128), jnp.float32)],
        compiler_params=pltpu.CompilerParams(vmem_limit_bytes=VMEM_LIMIT),
        name="second_weight",
    )(hidden, cot, later, above, below)


def col_sums(wide, cells):
    half = cells.shape[1] // 2
    wide[...] = jnp.zeros_like(wide)
    wide[:, 8 : 8 + cells.shape[1], : cells.shape[2]] = cells

    def every_second(start):
        return wide[:, pl.ds(start, half, stride=2), : cells.shape[2]]

    before, even, odd, after = (every_second(7 + k) for k in range(4))
    return odd + after, even + odd, before + even


def group_lanes(outs, first):
    lane = lax.broadcasted_iota(jnp.int32, (outs, 128), 1)
    group = lax.broadcasted_iota(jnp.int32, (outs, 128), 0) // (outs // GROUPS)
    return (lane == group + (64 if first else 64 + GROUPS)).astype(jnp.float32)


def exact(left, right, dims):
    return lax.dot_general(
        left, right, (dims, ((), ())), precision=lax.Precision.HIGHEST, preferred_element_type=jnp.float32
    )


def in_parts(sums, rows):
    high = sums.astype(jnp.bfloat16).astype(jnp.float32)
    middle = (sums - high).astype(jnp.bfloat16).astype(jnp.float32)
    low = sums - high - middle
    row = lax.broadcasted_iota(jnp.int32, (rows, 128), 0)
    return jnp.where(row == 0, high, jnp.where(row == 1, middle, jnp.where(row == 2, low, 0.0)))


def sums_of(tile):
    return tile[0:1] + tile[1:2] + tile[2:3]


def weight_grads_kernel(where, cache, features, above, below, grad_normed, normed, vectors, two, away, kept, wide):
    frames, rows, cols, outs = grad_normed.shape
    rows, half = rows - 2, cols // 2
    ins, mids, pieces, part_rows = features.shape[-1], two.shape[1], kept.shape[0], (kept.shape[1] - 16) * 2 // 5
    timed = jnp.concatenate([cache[...], features[...]], 0)
    rows_in = jnp.concatenate([above[:, :half][:, None], timed, below[:, :half][:, None]], 1)
    rstd, f0, s0 = (vectors[k : k + 1] for k in range(3))
    own = normed[:, 1:-1].reshape(-1, outs)
    grad = (grad_normed[:, 1:-1].reshape(-1, outs) - f0 - own * s0) * rstd
    lower = where[0] == 0

    def pool(field, last):
        by_tap = col_sums(wide, field.reshape(frames * rows, cols, outs))
        taps = []
        for b in range(3):
            for e in range(3):
                part = by_tap[e].reshape(frames, rows, half, outs)
                none = jnp.zeros_like(part[:, 0])
                r = [part[:, k] for k in range(rows)]
                stacked = (
                    [r[0], r[1] + r[2], r[3], none],
                    [none, r[0] + r[1], r[2] + r[3], none],
                    [none, r[0], r[1] + r[2], r[3]],
                )[b]
                taps.append(jnp.stack(stacked, 1).astype(jnp.bfloat16).reshape(-1, outs))
        return jnp.concatenate(taps + [last], 1)

    at = lax.broadcasted_iota(jnp.int32, (frames * 4 * half, 32), 0)
    tap = lax.broadcasted_iota(jnp.int32, (frames * 4 * half, 32), 1)
    b, e, row, col = tap // 3, tap % 3, at // half % 4, at % half
    two_rows = (row == 1) & (b < 2) | (row == 2) & (b > 0)
    one_row = (row == 0) & (b == 0) | (row == 2) & (b == 0) | (row == 1) & (b == 2) | (row == 3) & (b == 2)
    in_rows = jnp.where(two_rows, 2.0, jnp.where(one_row, 1.0, 0.0))
    in_cols = jnp.where((e == 0) & (col == half - 1) | (e == 2) & (col == 0), 1.0, 2.0)
    counts = jnp.where(tap < 9, in_rows * in_cols, 0.0).astype(jnp.bfloat16)

    def write(part, at, low, high):
        deep = part_rows if part < 2 else part_rows // 2
        while low.shape[0]:
            x, row = at // deep, part_rows * part + at % deep
            n = min(low.shape[0], deep - at % deep)
            away[x, row : row + n] = jnp.where(lower, high[:n], low[:n]).astype(jnp.bfloat16)
            kept[x, row : row + n] = jnp.where(lower, low[:n], high[:n])
            low, high, at = low[n:], high[n:], at + n

    for part, field, last in ((0, grad, counts), (1, own * rstd, jnp.zeros_like(counts))):
        cells = pool(field, last)
        at = 0
        for a in range(3):
            product = lax.dot_general(
                rows_in[a : a + frames].reshape(-1, ins),
                cells,
                (((0,), (0,)), ((), ())),
                preferred_element_type=jnp.float32,
            )
            for j in range(7):
                block = product[:, 128 * j : 128 * j + 128]
                write(part, at, block[: ins // 2], block[ins // 2 :])
                at += ins // 2
        nothing = jnp.zeros((pieces * part_rows - at, 128), jnp.float32)
        write(part, at, nothing, nothing)

    sums = exact(vectors[3:4], group_lanes(outs, True), ((1,), (0,)))
    sums += exact(vectors[4:5], group_lanes(outs, False), ((1,), (0,)))
    sums = in_parts(sums, 16)
    at = 0
    for a in range(3):
        for j in range(7):
            block = two[a, :, 128 * j : 128 * j + 128]
            write(2, at, block[: mids // 2], block[mids // 2 :])
            at += mids // 2
    nothing = jnp.zeros((pieces * part_rows // 2 - at, 128), jnp.float32)
    write(2, at, nothing, nothing)
    for x in range(pieces):
        away[x, part_rows * 5 // 2 :] = sums.astype(jnp.bfloat16)
        kept[x, part_rows * 5 // 2 :] = sums


def weight_grads(where, cache, features, above, below, grad_normed, normed, vectors, two, pieces, part_rows):
    frames, rows, cols, _ = grad_normed.shape
    shape = (pieces, part_rows * 5 // 2 + 16, 128)
    return pl.pallas_call(
        weight_grads_kernel,
        out_shape=(jax.ShapeDtypeStruct(shape, jnp.bfloat16), jax.ShapeDtypeStruct(shape, jnp.float32)),
        in_specs=whole(1, pltpu.SMEM) + whole(8),
        out_specs=whole(2),
        scratch_shapes=[pltpu.VMEM((frames * (rows - 2), cols + 16, 128), jnp.float32)],
        compiler_params=pltpu.CompilerParams(vmem_limit_bytes=VMEM_LIMIT),
        name="weight_grads",
    )(where, cache, features, above, below, grad_normed, normed, vectors, two)


def add_pair_kernel(kept, came, out, total, sems):
    deep = kept.shape[1] - 16
    sums = in_parts(sums_of(kept[0, deep:] + came[0, deep:].astype(jnp.float32)), 16).astype(jnp.bfloat16)
    moves = []
    for x in range(kept.shape[0]):
        total[x, :deep] = (kept[x, :deep] + came[x, :deep].astype(jnp.float32)).astype(jnp.bfloat16)
        total[x, deep:] = sums
        moves.append(pltpu.make_async_copy(total.at[x], out.at[x], sems.at[x]))
        moves[x].start()
    for move in moves:
        move.wait()


def add_pair(kept, came):
    return pl.pallas_call(
        add_pair_kernel,
        out_shape=jax.ShapeDtypeStruct(kept.shape, jnp.bfloat16),
        in_specs=whole(2),
        out_specs=whole(1, pltpu.HBM)[0],
        scratch_shapes=[pltpu.VMEM(kept.shape, jnp.bfloat16), pltpu.SemaphoreType.DMA((kept.shape[0],))],
        compiler_params=pltpu.CompilerParams(vmem_limit_bytes=VMEM_LIMIT),
        name="add_pair",
    )(kept, came)


def add_row_kernel(came, out):
    total = jnp.sum(came[...].astype(jnp.float32), 0)
    n = out.shape[0] * 8
    out[:, 0] = total[:n].astype(jnp.bfloat16).reshape(-1, 8, 128)
    out[:, 1] = total[n : 2 * n].astype(jnp.bfloat16).reshape(-1, 8, 128)
    tiles = total[2 * n : n * 5 // 2].reshape(-1, 8, 128)
    row = lax.broadcasted_iota(jnp.int32, (1, 8, 128), 1)
    lane = lax.broadcasted_iota(jnp.int32, (1, 8, 128), 2)
    turned = jnp.concatenate([tiles[:, 4:], tiles[:, :4]], 1)
    swap = lambda k: jnp.concatenate([k[..., 64:], k[..., :64]], 2)
    even = jnp.where(row < 4, tiles, swap(turned))
    odd = jnp.where(row < 4, turned, swap(tiles))
    both = jnp.stack([even, odd], 1).reshape(-1, 8, 128)
    sums = in_parts(sums_of(total[n * 5 // 2 :]), 8)
    out[:, 2] = jnp.where(lane < 64, both, sums[None]).astype(jnp.bfloat16)


def add_row(came):
    tiles = (came.shape[1] - 16) // 20
    return pl.pallas_call(
        add_row_kernel,
        out_shape=jax.ShapeDtypeStruct((tiles, 3, 8, 128), jnp.bfloat16),
        in_specs=whole(1),
        out_specs=whole()[0],
        compiler_params=pltpu.CompilerParams(vmem_limit_bytes=VMEM_LIMIT),
        name="add_row",
    )(came)


def combine_kernel(count, tiles_per_block, where, came, vectors, piece, final, lanes):
    outs = vectors.shape[1]
    total = jnp.sum(came[...].astype(jnp.float32), 0)
    sums = sums_of(total[0, 2]) / count
    first = exact(sums, group_lanes(outs, True), ((1,), (1,)))
    second = exact(sums, group_lanes(outs, False), ((1,), (1,)))
    rest = (first - vectors[1:2]) * vectors[0:1]
    final[...] = jnp.concatenate([first, second, rest, jnp.zeros((5, outs), jnp.float32)], 0)
    spread = [second - vectors[2:3]] * 9 + [jnp.zeros((1, 32), jnp.float32)]
    lanes[...] = jnp.broadcast_to(jnp.concatenate(spread, 1), lanes.shape)
    for k in range(piece.shape[0]):
        block = (where[3] * piece.shape[0] + k) // tiles_per_block % 7
        change = lanes[0:1, pl.ds(pl.multiple_of(block * 128, 128), 128)]
        upper = jnp.concatenate([total[k, 2, :4, :64], total[k, 2, 4:, :64]], 1)
        grad = total[k, 0] - change * total[k, 1]
        piece[k] = jnp.concatenate([grad, upper], 0).astype(jnp.bfloat16)


def combine(count, ins, where, came, vectors):
    return pl.pallas_call(
        functools.partial(combine_kernel, count, ins // 16),
        out_shape=(
            jax.ShapeDtypeStruct((came.shape[1], 12, 128), jnp.bfloat16),
            jax.ShapeDtypeStruct(vectors.shape, jnp.float32),
        ),
        in_specs=whole(1, pltpu.SMEM) + whole(2),
        out_specs=whole(2),
        scratch_shapes=[pltpu.VMEM((8, 896), jnp.float32)],
        compiler_params=pltpu.CompilerParams(vmem_limit_bytes=VMEM_LIMIT),
        name="combine",
    )(where, came, vectors)


def grad_pre_kernel(where, grad_normed, normed, vectors, final, out):
    shape = grad_normed.shape
    flat = (-1, shape[-1])
    grad = grad_normed[...].reshape(flat) - final[:1] - normed[...].reshape(flat) * final[1:2]
    out[...] = inside(where, (grad * vectors[:1]).reshape(shape)).astype(jnp.bfloat16)


def grad_before_norm(where, grad_normed, normed, vectors, final):
    return pl.pallas_call(
        grad_pre_kernel,
        out_shape=jax.ShapeDtypeStruct(grad_normed.shape, jnp.bfloat16),
        in_specs=whole(1, pltpu.SMEM) + whole(4),
        out_specs=whole()[0],
        compiler_params=pltpu.CompilerParams(vmem_limit_bytes=VMEM_LIMIT),
        cost_estimate=pl.CostEstimate(flops=2**20, bytes_accessed=2**20, transcendentals=0),
        name="grad_pre",
    )(where, grad_normed, normed, vectors, final)


def unpack_kernel(scale, half, part, final, *rest):
    one, two, flat = rest[-3:]
    pieces, rows = part.shape[0], part.shape[1]
    split = rows * 2 // 3
    step = pl.program_id(0)

    @pl.when(step == 0)
    def _():
        for x in range(pieces):
            flat[split * x : split * (x + 1)] = part[x, :split]
            at = pieces * split + (rows - split) * x
            flat[at : at + rows - split] = part[x, split:]

    for out, begin in ((one, 0), (two, pieces * split)):
        taps, channels, outs = out.shape
        blocks = []
        for j in range(7):
            at = pl.multiple_of(begin + (step * 7 + j) * channels, 16)
            blocks.append(flat[pl.ds(at, channels)].astype(jnp.float32))
        lanes = jnp.concatenate(blocks, 1) * scale
        if out is one:
            change = jnp.concatenate([final[2:3]] * taps + [jnp.zeros((1, 32), jnp.float32)], 1)
            tap = lax.broadcasted_iota(jnp.int32, (32, change.shape[1]), 0)
            lane = lax.broadcasted_iota(jnp.int32, (32, change.shape[1]), 1)
            change = jnp.where(lane // outs == tap, change, 0.0)
            high = change.astype(jnp.bfloat16)
            low = (change - high.astype(jnp.float32)).astype(jnp.bfloat16)
            met = jnp.concatenate([blocks[-1][:, 96:]] * 2, 1).astype(jnp.bfloat16)
            change = jnp.concatenate([high, low], 0)
            lanes -= jnp.dot(met, change, preferred_element_type=jnp.float32) * scale
        for k in range(taps):
            out[k] = lanes[:, outs * k : outs * k + outs]


def unpack(half, part, final, ins, mids, scale, begun=()):
    return pl.pallas_call(
        functools.partial(unpack_kernel, scale),
        grid_spec=pltpu.PrefetchScalarGridSpec(
            num_scalar_prefetch=1,
            grid=(3,),
            in_specs=whole(2) + whole(len(begun), pl.ANY),
            out_specs=[
                pl.BlockSpec((9, ins // 2, mids), lambda a, half: (a, half[0], 0)),
                pl.BlockSpec((9, mids // 2, mids), lambda a, half: (a, half[0], 0)),
            ],
            scratch_shapes=[pltpu.VMEM((part.shape[0] * part.shape[1], 128), jnp.bfloat16)],
        ),
        out_shape=(
            jax.ShapeDtypeStruct((27, ins, mids), jnp.float32),
            jax.ShapeDtypeStruct((27, mids, mids), jnp.float32),
        ),
        input_output_aliases={3 + k: k for k in range(len(begun))},
        compiler_params=pltpu.CompilerParams(vmem_limit_bytes=VMEM_LIMIT),
        cost_estimate=pl.CostEstimate(flops=2**20, bytes_accessed=2**22, transcendentals=0),
        name="unpack",
    )(half, part, final, *begun)


def feature_grads_kernel(grad_pre, weight, out, wide):
    frames, rows, cols, outs = grad_pre.shape
    own, cells_in, cols_in, ins = out.shape
    by_tap = col_sums(wide, grad_pre[...].astype(jnp.float32).reshape(frames * rows, cols, outs))
    total = jnp.zeros((own * cells_in * cols_in, ins), jnp.float32)
    for b in range(3):
        for e in range(3):
            part = by_tap[e].reshape(frames, rows, cols // 2, outs)
            cells = jnp.stack(
                [part[:, 2 * k + 2 - b] + part[:, 2 * k + 3 - b] for k in range(cells_in)], 1
            ).astype(jnp.bfloat16)
            for a in range(3):
                total += lax.dot_general(
                    cells[2 - a : 2 - a + own].reshape(-1, outs),
                    weight[a, b, e],
                    (((1,), (1,)), ((), ())),
                    preferred_element_type=jnp.float32,
                )
    out[...] = total.reshape(out.shape)


def feature_grads(grad_rowed, weight, shape):
    frames, rows, cols, _ = grad_rowed.shape
    return pl.pallas_call(
        feature_grads_kernel,
        out_shape=jax.ShapeDtypeStruct(shape, jnp.float32),
        in_specs=whole(2),
        out_specs=whole()[0],
        scratch_shapes=[pltpu.VMEM((frames * rows, cols + 16, 128), jnp.float32)],
        compiler_params=pltpu.CompilerParams(vmem_limit_bytes=VMEM_LIMIT),
        cost_estimate=pl.CostEstimate(flops=2**28, bytes_accessed=2**21, transcendentals=0),
        name="feature_grads",
    )(grad_rowed, weight)


SWAP = [(0, 1), (1, 0)]


def body(features, cotangent, weight_one, weight_two, norm_gain, norm_shift):
    frames, ins = features.shape[0], features.shape[-1]
    rows, cols, mids = cotangent.shape[1:]
    xs, rest, height = lax.axis_size("x"), lax.axis_size(REST), lax.axis_size(HEIGHT)
    cells = frames * rows * cols * 2 * xs * rest
    count = cells * (mids // GROUPS)
    at_row = lax.axis_index(HEIGHT)
    owned = lax.axis_index("x") * rest + lax.axis_index(REST)
    where = jnp.stack([lax.axis_index("c"), at_row == 0, at_row == height - 1, owned]).astype(jnp.int32)
    barrier = lax.optimization_barrier

    def exchange(copies, axes):
        return lax.all_to_all(copies, axes, 0, 0)

    def spread(value, copies):
        return jnp.broadcast_to(value[None], (copies,) + value.shape)

    cache = neighbour(features, TM, 1)
    later = neighbour(cotangent, TM, -1)

    features, cotangent = resident(features, cotangent)
    downward, upward = edges(cache, features, cotangent, later)
    downward, upward, weight_one, weight_two = barrier((downward, upward, weight_one, weight_two))
    weight_one, weight_two = resident(weight_one, weight_two)
    above = neighbour(downward, HEIGHT, 1)
    below = neighbour(upward, HEIGHT, -1)
    pre_norm, sums = conv_one(cache, features, above, below, weight_one, cotangent, height)
    came = exchange(sums, HEIGHT)
    grad_hidden, all_taps = hidden_grads(cotangent, later, above, below, weight_two)
    sums, grad_hidden = barrier((came.sum(0), grad_hidden))
    came = exchange(spread(sums, lax.axis_size(TM)), TM)
    hidden, grad_normed, normed, vectors = middle(
        count, where, came, pre_norm, grad_hidden, all_taps, norm_gain, norm_shift
    )
    local_two = second_weight(hidden, cotangent, later, above, below)

    scale = 1.0 / cells**0.5
    part_rows = -(-21 * ins // (2 * 8 * xs * rest)) * 8 * rest
    away, kept = weight_grads(
        where, cache, features, above, below, grad_normed, normed, vectors, local_two, xs, part_rows
    )
    part = add_pair(kept, lax.ppermute(away, "c", SWAP))
    part, hidden = barrier((add_row(exchange(part, "x")), hidden))
    before = neighbour(hidden, TM, 1)
    came = exchange(part.reshape(rest, -1, 3, 8, 128), REST)
    came, before = barrier((came, before))
    part, final = combine(count, ins, where, came, vectors)
    grad_pre = grad_before_norm(where, grad_normed, normed, vectors, final)
    part = exchange(spread(part, rest), REST)
    after = neighbour(grad_pre, TM, -1)
    decoded = conv(
        jnp.pad(jnp.concatenate([before, hidden], 0), ((0, 0), (0, 0), (1, 1), (0, 0))), weight_two
    ).astype(jnp.bfloat16)
    part, after, decoded = barrier((part, after, decoded))
    part = jnp.concatenate([part[:, :, :8].reshape(-1, 128), part[:, :, 8:].reshape(-1, 128)], 0)
    part = exchange(spread(part, xs), "x")
    grad_features = feature_grads(jnp.concatenate([grad_pre, after], 0), weight_one, features.shape)
    part, grad_features = barrier((part, grad_features))
    other = lax.ppermute(part, "c", SWAP)
    core = where[:1]
    begun = unpack(core, part, final, ins, mids, scale)
    grad_one, grad_two = unpack(1 - core, other, final, ins, mids, scale, begun)
    return decoded, grad_features, grad_one.reshape(weight_one.shape), grad_two.reshape(weight_two.shape)


def solution(mesh):
    split = P(TM, HEIGHT, None, None)
    return jax.shard_map(
        body,
        mesh=fine_mesh(mesh),
        in_specs=(split, split, P(), P(), P(), P()),
        out_specs=(split, split, P(), P()),
        check_vma=False,
    )
```
